512 devices in a mesh: face: 4 (over z_hi), tile: 128 (over x, z_lo, y, core).
Axes of the slice: x: 4, y: 8, z: 8 (z_hi: 4, z_lo: 2; z = z_hi * 2 + z_lo), core: 2. Of those that a mesh axis runs over, the one named last changes fastest.
Arguments:
- sample: bfloat16 [12, 1024, 32, 192], P('face', 'tile'), may hold values from -6 to 6
- noise_field: bfloat16 [12, 1024, 32, 192], P('face', 'tile'), may hold values from -6 to 6
- coarse_state: bfloat16 [12, 128, 4, 192], P('face', 'tile'), may hold values from -6 to 6
- first_kernel: bfloat16 [3, 3, 384, 192], replicated, may hold values from -0.109375 to 0.109375
- first_bias: float32 [192], replicated, may hold values from -3 to 3
- second_kernel: bfloat16 [3, 3, 192, 192], replicated, may hold values from -0.15625 to 0.15625
- second_bias: float32 [192], replicated, may hold values from -3 to 3
- ns_neighbour: int32 [12, 2], replicated, may hold values from 0 to 2
- we_neighbour: int32 [12, 2], replicated, may hold values from 0 to 11
- edge_code: int32 [12, 4], replicated, may hold values from 0 to 1
Outputs:
- next_sample: bfloat16 [12, 1024, 32, 192], P('face', 'tile')
The draws below stay inside these ranges and needn't reach their ends.
Inputs may be any that keep to these rules, and one draw needn't show every extreme that they name: ns_neighbour counts within the face's own group: it names face 3 (f // 3) + value.
All inputs are finite; a program needn't handle non-finite values.
Results may differ from the reference program's by a relative error of at most 0.0022.
Values may be sent and summed in bfloat16 or wider, within the bound.
A program may use at most 64 MiB of HBM per device.

```python
import jax
import jax.numpy as jnp
from jax import lax

C = 192
FACES = 12
UP = 8
FW = 32
H = 1024
HC = 128
WC = 4


def with_ends(array, own_key, smallest, largest):
    dims = array.shape
    place = [jax.random.randint(jax.random.fold_in(own_key, axis), (), 0, dims[axis]) for axis in range(len(dims))]
    array = array.at[tuple(place)].set(smallest)
    longest = dims.index(max(dims))
    place[longest] = (place[longest] + 1) % dims[longest]
    return array.at[tuple(place)].set(largest)


def shard_levels(rng, extent, split, low, largest):
    loudness = 1.0
    for dim, parts in split:
        steps = jax.random.uniform(jax.random.fold_in(jax.random.fold_in(rng, 6), dim), (parts,), jnp.float32, low / len(split), largest / len(split))
        loudness = loudness * jnp.repeat(jnp.exp(steps), extent[dim] // parts).reshape((-1,) + (1,) * (len(extent) - 1 - dim))
    return loudness


def normal_values(rng, shape, spread, reach, shards=(), kind=jnp.bfloat16):
    level = shard_levels(rng, shape, shards, -0.22, 0.18) if shards else 1.0
    array = jax.random.normal(rng, shape, jnp.float32) * spread * level
    return jnp.minimum(jnp.maximum(array, -reach), reach).astype(kind)


def setup_inputs(seed: int = 0) -> dict:
    arg_keys = jax.random.split(jax.random.key(seed), 11)
    return {
        "sample": normal_values(arg_keys[0], (FACES, H, FW, C), 1.0, 6.0, ((0, 4), (1, 128))),
        "noise_field": normal_values(arg_keys[1], (FACES, H, FW, C), 1.0, 6.0, ((0, 4), (1, 128))),
        "coarse_state": normal_values(arg_keys[2], (FACES, HC, WC, C), 1.0, 6.0, ((0, 4), (1, 128))),
        "first_kernel": normal_values(arg_keys[3], (3, 3, 2 * C, C), (18 * C) ** -0.5, 0.109375),
        "first_bias": normal_values(arg_keys[4], (C,), 0.5, 3.0, (), jnp.float32),
        "second_kernel": normal_values(arg_keys[5], (3, 3, C, C), (9 * C) ** -0.5, 0.15625),
        "second_bias": normal_values(arg_keys[6], (C,), 0.5, 3.0, (), jnp.float32),
        "ns_neighbour": with_ends(jax.random.randint(arg_keys[7], (FACES, 2), 0, 3), jax.random.fold_in(arg_keys[7], 1), 0, 2).astype(jnp.int32),
        "we_neighbour": with_ends(jax.random.randint(arg_keys[8], (FACES, 2), 0, FACES), jax.random.fold_in(arg_keys[8], 1), 0, FACES - 1).astype(jnp.int32),
        "edge_code": with_ends(jax.random.randint(arg_keys[9], (FACES, 4), 0, 2), jax.random.fold_in(arg_keys[9], 1), 0, 1).astype(jnp.int32),
    }


noise_gain = 0.6
input_gain = 0.7071067811865476
skip_gain = 0.5
output_gain = 0.7071067811865476
step_ratio = -0.4


def face_pad(one_field, ns_neighbour, we_neighbour, edge_code):
    face_total = one_field.shape[0]
    row_count = one_field.shape[1]
    group_base = (jnp.arange(face_total, dtype=jnp.int32) // 3) * 3
    north_src = group_base + ns_neighbour[:, 0]
    south_src = group_base + ns_neighbour[:, 1]
    west_src = we_neighbour[:, 0]
    east_src = we_neighbour[:, 1]
    top_rows = jnp.where((edge_code[:, 0] == 1)[:, None, None], one_field[north_src, 0], one_field[north_src, row_count - 1])
    bottom_rows = jnp.where((edge_code[:, 1] == 1)[:, None, None], one_field[south_src, row_count - 1], one_field[south_src, 0])
    west_cols = jnp.where((edge_code[:, 2] == 1)[:, None, None], one_field[west_src, :, 0], one_field[west_src, :, -1])
    east_cols = jnp.where((edge_code[:, 3] == 1)[:, None, None], one_field[east_src, :, -1], one_field[east_src, :, 0])
    corner = jnp.zeros((face_total, 1, one_field.shape[3]), one_field.dtype)
    top_full = jnp.concatenate([corner, top_rows, corner], axis=1)
    bottom_full = jnp.concatenate([corner, bottom_rows, corner], axis=1)
    middle = jnp.concatenate([west_cols[:, :, None], one_field, east_cols[:, :, None]], axis=2)
    return jnp.concatenate([top_full[:, None], middle, bottom_full[:, None]], axis=1)


def convolve(padded, kernel):
    row_count = padded.shape[1] - 2
    col_count = padded.shape[2] - 2
    width_in = padded.shape[3]
    width_out = kernel.shape[3]

    def one_face(face_block):
        accumulated = jnp.zeros((row_count * col_count, width_out), jnp.float32)
        for shift_row in range(3):
            for shift_col in range(3):
                window = face_block[shift_row:shift_row + row_count, shift_col:shift_col + col_count]
                accumulated = accumulated + jnp.dot(window.reshape(row_count * col_count, width_in), kernel[shift_row, shift_col], preferred_element_type=jnp.float32)
        return accumulated.reshape(row_count, col_count, width_out)

    return lax.map(one_face, padded)


def reference(sample, noise_field, coarse_state, first_kernel, first_bias, second_kernel, second_bias, ns_neighbour, we_neighbour, edge_code):
    perturbed = sample.astype(jnp.float32) + noise_gain * noise_field.astype(jnp.float32)
    net_input = (perturbed * input_gain).astype(jnp.bfloat16)
    upsampled = jnp.repeat(jnp.repeat(coarse_state, UP, axis=1), UP, axis=2)
    mixed_input = jnp.concatenate([net_input, upsampled], axis=-1)
    activation = convolve(face_pad(mixed_input, ns_neighbour, we_neighbour, edge_code), first_kernel) + first_bias
    hidden = jax.nn.silu(activation).astype(jnp.bfloat16)
    feature = convolve(face_pad(hidden, ns_neighbour, we_neighbour, edge_code), second_kernel) + second_bias
    denoised = skip_gain * perturbed + output_gain * feature
    next_sample = perturbed + step_ratio * (perturbed - denoised)
    return next_sample.astype(jnp.bfloat16)
```

```python
import functools

import jax
import jax.numpy as jnp
from jax import lax
from jax.experimental import pallas as pl
from jax.experimental.pallas import tpu as pltpu
from jax.sharding import PartitionSpec as P

MESH = pl.DeviceIdType.MESH
f32 = jnp.float32
bf16 = jnp.bfloat16

noise_gain = 0.6
input_gain = 0.7071067811865476
skip_gain = 0.5
output_gain = 0.7071067811865476
step_ratio = -0.4

UP = 8
FACES = 3
ROWS = 8
COLS = 32
COARSE = COLS // UP
PIX = ROWS * COLS
BLOCKS = 6


def dot(a, b):
    return jnp.dot(a, b, preferred_element_type=f32)


def column_of(shape):
    return lax.rem(lax.broadcasted_iota(jnp.int32, shape, 0), COLS)


def from_west(z):
    return jnp.where(column_of(z.shape) == 0, 0.0, pltpu.roll(z, 1, 0))


def from_east(z):
    return jnp.where(column_of(z.shape) == COLS - 1, 0.0, pltpu.roll(z, z.shape[0] - 1, 0))


def along_rows(v0, v1, v2):
    return pltpu.roll(v0, 1, 0) + v1 + pltpu.roll(v2, v2.shape[0] - 1, 0)


def spread(rows, count=16):
    width = rows[0][1].shape[1]
    place = lax.broadcasted_iota(jnp.int32, (count, width), 0)
    out = jnp.zeros((count, width), f32)
    for at, row in rows:
        out = jnp.where(place == at, jnp.broadcast_to(row, (count, width)), out)
    return out


def kernel(
    groups,
    tiles,
    sample_hbm,
    noise_hbm,
    coarse_hbm,
    w1_hbm,
    w2_hbm,
    b1,
    b2,
    ns,
    we,
    code,
    out,
    sample,
    noise,
    coarse,
    w1,
    w2,
    pf,
    acc,
    xp,
    hp,
    up,
    cclass,
    cols1,
    cols2,
    corner1,
    corner2,
    rows1,
    rows2,
    pick,
    zcol,
    zrow,
    load_sem,
    send_sem,
    recv_sem,
):
    g = lax.axis_index("face")
    t = lax.axis_index("tile")
    above = lax.rem(t + tiles - 1, tiles)
    below = lax.rem(t + 1, tiles)
    first = t == 0
    last = t == tiles - 1
    C = pf.shape[2]

    loads = [
        pltpu.make_async_copy(src, dst, load_sem.at[i])
        for i, (src, dst) in enumerate(
            [(sample_hbm, sample), (noise_hbm, noise), (coarse_hbm, coarse), (w1_hbm, w1), (w2_hbm, w2)]
        )
    ]
    for copy in loads:
        copy.start()

    barrier = pltpu.get_barrier_semaphore()
    for d in range(groups):
        for k, there in enumerate((t, above, below)):
            if d or k:
                pl.semaphore_signal(
                    barrier, inc=1, device_id=(lax.rem(g + d, groups), there), device_id_type=MESH
                )

    def copies(stage, cols, corner, rows):
        made = []

        def add(src, dst, there):
            n = len(made)
            made.append(
                pltpu.make_async_remote_copy(
                    src_ref=src,
                    dst_ref=dst,
                    send_sem=send_sem.at[stage, n],
                    recv_sem=recv_sem.at[stage, n],
                    device_id=there,
                    device_id_type=MESH,
                )
            )

        for d in (2, 1, 3):
            far = lax.rem(g + d, groups)
            table = pl.ds(0, 4) if stage == 0 else pl.ds(1, 3)
            add(cols.at[g, table], cols.at[g, table], (far, t))
            add(corner.at[0], cols.at[g, 5], (far, above))
            add(corner.at[1], cols.at[g, 4], (far, below))
        add(rows.at[2], rows.at[1], (g, above))
        add(rows.at[3], rows.at[0], (g, below))
        add(corner.at[0], cols.at[g, 5], (g, above))
        add(corner.at[1], cols.at[g, 4], (g, below))
        return made

    lane = lax.broadcasted_iota(jnp.int32, (16, groups * BLOCKS * 16), 1)
    place = lax.broadcasted_iota(jnp.int32, (16, groups * BLOCKS * 16), 0)
    for side in range(2):
        for f in range(FACES):
            face = g * FACES + f
            src = we[face, side]
            edge = code[face, 2 + side]
            src_side = edge if side else 1 - edge
            src_g = (
                (src >= 3).astype(jnp.int32) + (src >= 6).astype(jnp.int32) + (src >= 9).astype(jnp.int32)
            )
            src_f = src - 3 * src_g
            base = src_g * (BLOCKS * 16)
            near = base + 4 * 16 + src_f * 2 + src_side
            for part in range(2):
                over = jnp.where(first, -1, near + 8 * part)
                under = jnp.where(last, -1, near + 16 + 8 * part)
                if part == 0:
                    inner = base + (1 + src_f) * 16 + src_side * 8 + place - 1
                else:
                    inner = jnp.broadcast_to(base + src_f * 4 + src_side * 3, place.shape)
                target = jnp.where(place == 0, over, jnp.where(place == ROWS + 1, under, inner))
                target = jnp.where(place > ROWS + 1, -1, target)
                at = part * 96 + side * 48 + f * 16
                pick[at : at + 16, :] = jnp.where(lane == target, 1.0, 0.0).astype(bf16)

    zero_row = jnp.zeros((COLS, C), bf16)
    for f in range(FACES):
        for ref in (xp, hp):
            ref[f, 0:COLS] = zero_row
            ref[f, COLS + PIX : 2 * COLS + PIX] = zero_row
    for d in range(groups):
        cols2[d, 0] = jnp.zeros((16, C), bf16)

    def fill_tables(values, gain, cols, corner, extra):
        tops, ends = [], []
        for f in range(FACES):
            lines = [[values[f, i * COLS + j : i * COLS + j + 1, :] for i in range(ROWS)] for j in (0, COLS - 1)]
            west, east = [spread(list(enumerate(line)), ROWS) * gain for line in lines]
            cols[g, 1 + f] = jnp.concatenate([west, east], axis=0).astype(bf16)
            tops += [(2 * f, west[0:1]), (2 * f + 1, east[0:1])]
            ends += [(2 * f, west[ROWS - 1 : ROWS]), (2 * f + 1, east[ROWS - 1 : ROWS])]
        corner[0] = spread(tops + extra).astype(bf16)
        corner[1] = spread(ends + extra).astype(bf16)

    for copy in loads[:3]:
        copy.wait()
    for f in range(FACES):
        p = sample[f].astype(f32) + noise_gain * noise[f].astype(f32)
        p = p.reshape(PIX, C)
        pf[f] = p
        net = (p * input_gain).astype(bf16)
        xp[f, COLS : COLS + PIX] = net
        rows1[2, f, 0] = net[0:COLS]
        rows1[3, f, 0] = net[PIX - COLS : PIX]
    raw, edges = [], []
    for f in range(FACES):
        c = coarse[f, 0].astype(f32)
        each = [c[j : j + 1] for j in range(COARSE)]
        raw += [(4 * f + j, each[j]) for j in range(COARSE)]
        edges += [(8 + 2 * f, each[0]), (9 + 2 * f, each[COARSE - 1])]
        wide = jnp.concatenate([jnp.broadcast_to(e, (UP, C)) for e in each], axis=0).astype(bf16)
        up[f * COLS : (f + 1) * COLS] = wide
        rows1[2, f, 1] = wide
        rows1[3, f, 1] = wide
    cols1[g, 0] = spread(raw).astype(bf16)
    fill_tables(pf, input_gain, cols1, corner1, edges)

    pl.semaphore_wait(barrier, 3 * groups - 1)
    sent1 = copies(0, cols1, corner1, rows1)
    for copy in sent1:
        copy.start()

    def conv_own(src, w, f, b):
        z = dot(src[f, 0:PIX], w[0, b, 0:C])
        z = z + dot(src[f, COLS : COLS + PIX], w[1, b, 0:C])
        return z + dot(src[f, 2 * COLS : 2 * COLS + PIX], w[2, b, 0:C])

    loads[3].wait()
    parts = []
    for b in range(3):
        c0, c1, c2 = [dot(up[...], w1[a, b, C : 2 * C]) for a in range(3)]
        parts.append((c1 + c2, c0 + c1 + c2, c0 + c1))
    for k in range(3):
        cclass[k] = from_west(parts[0][k]) + parts[1][k] + from_east(parts[2][k]) + b1[...]

    def own1(f, _):
        z = from_west(conv_own(xp, w1, f, 0)) + conv_own(xp, w1, f, 1) + from_east(conv_own(xp, w1, f, 2))
        at = pl.ds(pl.multiple_of(f * COLS, COLS), COLS)
        acc[f, 0:COLS] = z[0:COLS] + cclass[0, at]
        for i in range(1, ROWS - 1):
            acc[f, i * COLS : (i + 1) * COLS] = z[i * COLS : (i + 1) * COLS] + cclass[1, at]
        acc[f, PIX - COLS : PIX] = z[PIX - COLS : PIX] + cclass[2, at]
        return 0

    lax.fori_loop(0, FACES, own1, 0)

    def edge_rows(rows):
        tops, ends = [], []
        for f in range(FACES):
            face = g * FACES + f
            top_f = jnp.where(first, ns[face, 0], f)
            top_k = jnp.where(first, 2 * code[face, 0], 0)
            end_f = jnp.where(last, ns[face, 1], f)
            end_k = jnp.where(last, 1 + 2 * code[face, 1], 1)
            tops.append(rows[top_k, top_f])
            ends.append(rows[end_k, end_f])
        return tops, ends

    def add_borders(tops, ends, picked, w, wide):
        for k, (row, a) in enumerate(((tops, 0), (ends, 2))):
            z = []
            for b in range(3):
                y = dot(row[0], w[a, b, 0:C])
                if wide:
                    y = y + dot(row[1], w[a, b, C : 2 * C])
                z.append(y)
            zrow[k] = from_west(z[0]) + z[1] + from_east(z[2])
        for k, b in ((0, 0), (1, 2)):
            v = []
            for a in range(3):
                y = dot(picked[0][48 * k : 48 * k + 48], w[a, b, 0:C])
                if wide:
                    y = y + dot(picked[1][48 * k : 48 * k + 48], w[a, b, C : 2 * C])
                v.append(y)
            zcol[k] = along_rows(*v)

    column = column_of((COLS, C))

    def with_borders(f, i):
        z = acc[f, i * COLS : (i + 1) * COLS]
        if i == 0:
            z = z + zrow[0, pl.ds(pl.multiple_of(f * COLS, COLS), COLS)]
        if i == ROWS - 1:
            z = z + zrow[1, pl.ds(pl.multiple_of(f * COLS, COLS), COLS)]
        west = zcol[0, pl.ds(f * 16 + i + 1, 1), :]
        east = zcol[1, pl.ds(f * 16 + i + 1, 1), :]
        z = z + jnp.where(column == 0, jnp.broadcast_to(west, z.shape), 0.0)
        return z + jnp.where(column == COLS - 1, jnp.broadcast_to(east, z.shape), 0.0)

    for copy in sent1:
        copy.wait_recv()
    picked = dot(pick[...], cols1[...].reshape(groups * BLOCKS * 16, C)).astype(bf16)
    tops, ends = edge_rows(rows1)
    pair = lambda rows: [jnp.concatenate([r[k] for r in rows], axis=0) for k in range(2)]
    add_borders(pair(tops), pair(ends), (picked[0:96], picked[96:192]), w1, True)

    def activate(f, _):
        for i in range(ROWS):
            u = with_borders(f, i)
            h = u / (1.0 + jnp.exp(-u))
            acc[f, i * COLS : (i + 1) * COLS] = h
            hp[f, (i + 1) * COLS : (i + 2) * COLS] = h.astype(bf16)
        return 0

    lax.fori_loop(0, FACES, activate, 0)
    fill_tables(acc, 1.0, cols2, corner2, [])
    for f in range(FACES):
        rows2[2, f] = hp[f, COLS : 2 * COLS]
        rows2[3, f] = hp[f, PIX : PIX + COLS]
    sent2 = copies(1, cols2, corner2, rows2)
    for copy in sent2:
        copy.start()

    loads[4].wait()

    def own2(f, _):
        z = from_west(conv_own(hp, w2, f, 0)) + conv_own(hp, w2, f, 1) + from_east(conv_own(hp, w2, f, 2))
        acc[f] = z + b2[...]
        return 0

    lax.fori_loop(0, FACES, own2, 0)

    for copy in sent2:
        copy.wait_recv()
    picked = dot(pick[0:96, :], cols2[...].reshape(groups * BLOCKS * 16, C)).astype(bf16)
    tops, ends = edge_rows(rows2)
    add_borders(
        [jnp.concatenate(tops, axis=0)], [jnp.concatenate(ends, axis=0)], (picked,), w2, False
    )

    def finish(f, _):
        for i in range(ROWS):
            feature = with_borders(f, i)
            p = pf[f, i * COLS : (i + 1) * COLS]
            denoised = skip_gain * p + output_gain * feature
            out[f, i] = (p + step_ratio * (p - denoised)).astype(bf16)
        return 0

    lax.fori_loop(0, FACES, finish, 0)
    for copy in sent1 + sent2:
        copy.wait_send()


def on_device(groups, tiles, sample, noise, coarse, w1, b1, w2, b2, ns, we, code):
    C = sample.shape[-1]
    hbm = pl.BlockSpec(memory_space=pl.ANY)
    vmem = pl.BlockSpec(memory_space=pltpu.VMEM)
    smem = pl.BlockSpec(memory_space=pltpu.SMEM)
    return pl.pallas_call(
        functools.partial(kernel, groups, tiles),
        out_shape=jax.ShapeDtypeStruct(sample.shape, bf16),
        in_specs=[hbm] * 5 + [vmem] * 2 + [smem] * 3,
        out_specs=vmem,
        scratch_shapes=[
            pltpu.VMEM(sample.shape, bf16),
            pltpu.VMEM(noise.shape, bf16),
            pltpu.VMEM(coarse.shape, bf16),
            pltpu.VMEM(w1.shape, bf16),
            pltpu.VMEM(w2.shape, bf16),
            pltpu.VMEM((FACES, PIX, C), f32),
            pltpu.VMEM((FACES, PIX, C), f32),
            pltpu.VMEM((FACES, PIX + 2 * COLS, C), bf16),
            pltpu.VMEM((FACES, PIX + 2 * COLS, C), bf16),
            pltpu.VMEM((FACES * COLS, C), bf16),
            pltpu.VMEM((3, FACES * COLS, C), f32),
            pltpu.VMEM((groups, BLOCKS, 16, C), bf16),
            pltpu.VMEM((groups, BLOCKS, 16, C), bf16),
            pltpu.VMEM((2, 16, C), bf16),
            pltpu.VMEM((2, 16, C), bf16),
            pltpu.VMEM((4, FACES, 2, COLS, C), bf16),
            pltpu.VMEM((4, FACES, COLS, C), bf16),
            pltpu.VMEM((192, groups * BLOCKS * 16), bf16),
            pltpu.VMEM((2, 48, C), f32),
            pltpu.VMEM((2, FACES * COLS, C), f32),
            pltpu.SemaphoreType.DMA((5,)),
            pltpu.SemaphoreType.DMA((2, 13)),
            pltpu.SemaphoreType.DMA((2, 13)),
        ],
        compiler_params=pltpu.CompilerParams(
            collective_id=0, has_side_effects=True, vmem_limit_bytes=32 * 2**20
        ),
    )(sample, noise, coarse, w1, w2, b1.reshape(1, C), b2.reshape(1, C), ns, we, code)


def solution(mesh):
    return jax.shard_map(
        functools.partial(on_device, mesh.shape["face"], mesh.shape["tile"]),
        mesh=mesh,
        in_specs=(P("face", "tile", None, None),) * 3 + (P(),) * 7,
        out_specs=P("face", "tile", None, None),
        check_vma=False,
    )
```

```python
import functools

import jax
import jax.numpy as jnp
from jax import lax
from jax.experimental import pallas as pl
from jax.experimental.pallas import tpu as pltpu
from jax.sharding import PartitionSpec as P

MESH = pl.DeviceIdType.MESH
f32 = jnp.float32
bf16 = jnp.bfloat16
i32 = jnp.int32

noise_gain = 0.6
input_gain = 0.7071067811865476
skip_gain = 0.5
output_gain = 0.7071067811865476
step_ratio = -0.4

UP = 8
FACES = 3
ROWS = 8
COLS = 32
COARSE = COLS // UP
PIX = ROWS * COLS
SIDES = 2 * FACES
WIDE = 256

BLOCKS = 12
OUTER, INNER, OVER, UNDER, EMPTY = 1, 4, 7, 9, 11
STACK = 16
FIRST = 4


def dot(a, b):
    return jnp.dot(a, b, preferred_element_type=f32)


def dot_t(a, b):
    return lax.dot_general(a, b, (((1,), (1,)), ((), ())), preferred_element_type=f32)


def column_of(shape):
    return lax.rem(lax.broadcasted_iota(i32, shape, 0), COLS)


def from_west(z):
    return jnp.where(column_of(z.shape) == 0, 0.0, pltpu.roll(z, 1, 0))


def from_east(z):
    return jnp.where(column_of(z.shape) == COLS - 1, 0.0, pltpu.roll(z, z.shape[0] - 1, 0))


def along_rows(v0, v1, v2):
    return pltpu.roll(v0, 1, 0) + v1 + pltpu.roll(v2, v2.shape[0] - 1, 0)


def silu(u):
    return u / (1.0 + jnp.exp(-u))


def spread(rows, count):
    width = rows[0][1].shape[1]
    place = lax.broadcasted_iota(i32, (count, width), 0)
    out = jnp.zeros((count, width), f32)
    for at, row in rows:
        out = jnp.where(place == at, jnp.broadcast_to(row, (count, width)), out)
    return out


def kernel(
    groups,
    tiles,
    sample_hbm,
    noise_hbm,
    coarse_hbm,
    ns_hbm,
    we_hbm,
    code_hbm,
    w1_hbm,
    b1_hbm,
    w2_hbm,
    b2_hbm,
    out,
    sample,
    noise,
    coarse,
    ns,
    we,
    code,
    w1,
    b1,
    w2,
    b2,
    pf,
    acc,
    xp,
    hp,
    up,
    cclass,
    cols,
    corner,
    rows1,
    rows2,
    pick,
    zcol,
    zrow,
    load_sem,
    send_sem,
    recv_sem,
):
    g = lax.axis_index("face")
    t = lax.axis_index("tile")
    above = lax.rem(t + tiles - 1, tiles)
    below = lax.rem(t + 1, tiles)
    first = t == 0
    last = t == tiles - 1
    C = acc.shape[2]
    lines = groups * BLOCKS * 16

    loads = [
        pltpu.make_async_copy(src, dst, load_sem.at[i])
        for i, (src, dst) in enumerate(
            [
                (sample_hbm, sample),
                (noise_hbm, noise),
                (coarse_hbm, coarse),
                (ns_hbm, ns),
                (we_hbm, we),
                (code_hbm, code),
                (w1_hbm, w1),
                (b1_hbm, b1),
                (w2_hbm, w2),
                (b2_hbm, b2),
            ]
        )
    ]
    for copy in loads[:6]:
        copy.start()

    barrier = pltpu.get_barrier_semaphore()
    for d in (2, 1, 3, 0):
        for k, there in enumerate((t, above, below)):
            if d or k:
                pl.semaphore_signal(
                    barrier, inc=1, device_id=(lax.rem(g + d, groups), there), device_id_type=MESH
                )

    for f in range(FACES):
        zero_row = jnp.zeros((COLS, WIDE), bf16)
        xp[f, 0:COLS] = zero_row
        xp[f, COLS + PIX : 2 * COLS + PIX] = zero_row
        xp[f, COLS : COLS + PIX, 128:WIDE] = jnp.zeros((PIX, WIDE - 128), bf16)
        pf[f, :, 128:WIDE] = jnp.zeros((PIX, WIDE - 128), f32)
    for d in range(groups):
        cols[d, EMPTY] = jnp.zeros((16, WIDE), bf16)

    for copy in loads[:3]:
        copy.wait()
    for f in range(FACES):
        p = sample[f].astype(f32) + noise_gain * noise[f].astype(f32)
        p = p.reshape(PIX, C)
        pf[f, :, 0:C] = p
        xp[f, COLS : COLS + PIX, 0:C] = (p * input_gain).astype(bf16)
        for r in range(2):
            rows1[2, f, r] = xp[f, (1 + r) * COLS : (2 + r) * COLS]
            rows1[3, f, r] = xp[f, PIX - COLS + r * COLS : PIX + r * COLS]
    raw, tops, ends = [], [], []
    for f in range(FACES):
        c = coarse[f, 0].astype(f32)
        c = jnp.concatenate([jnp.zeros((COARSE, WIDE - C), f32), c], axis=1)
        each = [c[j : j + 1] for j in range(COARSE)]
        raw += [(4 * f + j, each[j]) for j in range(COARSE)]
        edges = [(24 + 2 * f, each[0]), (25 + 2 * f, each[COARSE - 1])]
        wide = jnp.concatenate([jnp.broadcast_to(e, (UP, WIDE)) for e in each], axis=0).astype(bf16)
        up[f * COLS : (f + 1) * COLS] = wide
        rows1[2, f, 2] = wide
        rows1[3, f, 2] = wide
        tops += edges
        ends += edges
        for k, block, j in ((0, OUTER, 0), (3, OUTER, COLS - 1), (1, INNER, 1), (2, INNER, COLS - 2)):
            line = [pf[f, i * COLS + j : i * COLS + j + 1, :] * input_gain for i in range(ROWS)]
            half = spread(list(enumerate(line)), ROWS)
            if k in (0, 1):
                lower = half
            else:
                cols[g, block + f] = jnp.concatenate([lower, half], axis=0).astype(bf16)
            tops += [(8 * f + 2 * k + r, line[r]) for r in range(2)]
            ends += [(8 * f + 2 * k + r, line[ROWS - 2 + r]) for r in range(2)]
    cols[g, 0] = spread(raw, 16).astype(bf16)
    corner[0] = spread(tops, 32).astype(bf16).reshape(2, 16, WIDE)
    corner[1] = spread(ends, 32).astype(bf16).reshape(2, 16, WIDE)

    sent = []

    def add(src, dst, there):
        n = len(sent)
        sent.append(
            pltpu.make_async_remote_copy(
                src_ref=src,
                dst_ref=dst,
                send_sem=send_sem.at[n],
                recv_sem=recv_sem.at[n],
                device_id=there,
                device_id_type=MESH,
            )
        )

    table = cols.at[g, pl.ds(0, OVER)]
    over = cols.at[g, pl.ds(OVER, 2)]
    under = cols.at[g, pl.ds(UNDER, 2)]
    for d in (2, 1, 3):
        far = lax.rem(g + d, groups)
        add(corner.at[0], under, (far, above))
        add(corner.at[1], over, (far, below))
        add(table, table, (far, t))
    add(corner.at[0], under, (g, above))
    add(corner.at[1], over, (g, below))
    add(rows1.at[2], rows1.at[1], (g, above))
    add(rows1.at[3], rows1.at[0], (g, below))

    pl.semaphore_wait(barrier, 3 * groups - 1)
    for copy in sent:
        copy.start()
    for copy in loads[6:]:
        copy.start()
    for copy in loads[3:6]:
        copy.wait()

    lane = lax.broadcasted_iota(i32, (STACK, lines), 1)
    place = lax.broadcasted_iota(i32, (STACK, lines), 0)

    def split(face):
        group = sum((face >= FACES * k).astype(i32) for k in range(1, groups))
        return group, face - FACES * group

    def across(face, side):
        edge = code[2 + side, face]
        return we[side, face], 3 * jnp.where(side == 1, edge, 1 - edge)

    def write_pick(at, face, column, beyond):
        group, f = split(face)
        base = group * (BLOCKS * 16)
        inner = ((column == 1) | (column == 2)).astype(i32)
        high = (column >= 2).astype(i32)

        def line(ff, row):
            if row < 0:
                return base + OVER * 16 + ff * 8 + column * 2 + 2 + row
            if row >= ROWS:
                return base + UNDER * 16 + ff * 8 + column * 2 + row - ROWS
            return base + (OUTER + inner * (INNER - OUTER) + ff) * 16 + high * 8 + row

        def condition(ff, row):
            if row < 0:
                return base + OVER * 16 + 24 + ff * 2 + high
            if row >= ROWS:
                return base + UNDER * 16 + 24 + ff * 2 + high
            return base + ff * COARSE + high * (COARSE - 1)

        n, s = ns[0, face], ns[1, face]
        flip_n, flip_s = code[0, face] == 1, code[1, face] == 1
        for part, where in enumerate((line, condition)):
            north = jnp.where(beyond, -1, jnp.where(flip_n, where(n, 0), where(n, -1)))
            south = jnp.where(beyond, -1, jnp.where(flip_s, where(s, ROWS - 1), where(s, ROWS)))
            target = jnp.broadcast_to(where(f, 0), place.shape)
            if part == 0:
                target = target + place - FIRST
            for q, value in (
                (0, where(f, -2)),
                (1, where(f, -1)),
                (2, jnp.where(first, -1, where(f, 0))),
                (3, jnp.where(first, north, where(f, -1))),
                (12, jnp.where(last, south, where(f, ROWS))),
                (13, jnp.where(last, -1, where(f, ROWS - 1))),
                (14, where(f, ROWS)),
                (15, where(f, ROWS + 1)),
            ):
                target = jnp.where(place == q, value, target)
            at = pl.multiple_of(at, STACK)
            pick[part, pl.ds(at, STACK), :] = jnp.where(lane == target, 1.0, 0.0).astype(bf16)

    def pick_side(n, _):
        side = (n >= FACES).astype(i32)
        face = g * FACES + n - FACES * side
        near, column = across(face, side)
        west_face, west_column = across(near, 0)
        east_face, east_column = across(near, 1)
        at_west = column == 0
        at_east = column == 3
        write_pick(n * STACK, near, column, True)
        write_pick(
            (SIDES + n) * STACK,
            jnp.where(at_west, west_face, near),
            jnp.where(at_west, west_column, 2),
            at_west,
        )
        write_pick((2 * SIDES + n) * STACK, near, column, False)
        write_pick(
            (3 * SIDES + n) * STACK,
            jnp.where(at_east, east_face, near),
            jnp.where(at_east, east_column, 1),
            at_east,
        )
        return 0

    lax.fori_loop(0, SIDES, pick_side, 0)

    def tap1(x, a, b):
        return dot_t(x, w1[a, b, :, 0:WIDE])

    def tap1_coarse(x, a, b):
        return dot_t(x, w1[a, b, :, w1.shape[3] - WIDE :])

    def tap2(x, a, b):
        return dot(x, w2[a, b])

    def conv_own(src, tap, f, b):
        z = tap(src[f, 0:PIX], 0, b)
        z = z + tap(src[f, COLS : COLS + PIX], 1, b)
        return z + tap(src[f, 2 * COLS : 2 * COLS + PIX], 2, b)

    for copy in loads[6:]:
        copy.wait()
    parts = []
    for b in range(3):
        c0, c1, c2 = [tap1_coarse(up[...], a, b) for a in range(3)]
        parts.append((c1 + c2, c0 + c1 + c2, c0 + c1))
    for k in range(3):
        cclass[k] = from_west(parts[0][k]) + parts[1][k] + from_east(parts[2][k]) + b1[...]

    def own1(f, _):
        z = from_west(conv_own(xp, tap1, f, 0)) + conv_own(xp, tap1, f, 1) + from_east(conv_own(xp, tap1, f, 2))
        at = pl.ds(pl.multiple_of(f * COLS, COLS), COLS)
        for i in range(ROWS):
            k = 0 if i == 0 else 2 if i == ROWS - 1 else 1
            acc[f, i * COLS : (i + 1) * COLS] = z[i * COLS : (i + 1) * COLS] + cclass[k, at]
        return 0

    lax.fori_loop(0, FACES, own1, 0)

    for copy in sent:
        copy.wait_recv()
    table = cols[...].reshape(lines, WIDE)
    picked = [dot(pick[part], table).astype(bf16) for part in range(2)]

    tops, ends, after, before = [], [], [], []
    for f in range(FACES):
        face = g * FACES + f
        n, s = jnp.where(first, ns[0, face], f), jnp.where(last, ns[1, face], f)
        flip_n, flip_s = code[0, face], code[1, face]
        k = jnp.where(first, 2 * flip_n, 0)
        r = jnp.where(k == 0, 1, 0)
        tops.append((rows1[k, n, r], rows1[k, n, 2]))
        k = jnp.where(last, 1 + 2 * flip_s, 1)
        r = jnp.where(k == 1, 0, 1)
        ends.append((rows1[k, s, r], rows1[k, s, 2]))
        s = jnp.where(first, ns[1, face], f)
        k = jnp.where(first, 2 - 2 * flip_s, 2)
        r = jnp.where(k == 0, 1, 0)
        after.append((rows1[k, s, r], rows1[k, s, 2]))
        n = jnp.where(last, ns[0, face], f)
        k = jnp.where(last, 3 - 2 * flip_n, 3)
        r = jnp.where(k == 1, 0, 1)
        before.append((rows1[k, n, r], rows1[k, n, 2]))

    def landed(k, r):
        return [(rows1[k, f, r], rows1[k, f, 2]) for f in range(FACES)]

    ROW = FACES * COLS
    stacks = (
        landed(0, 0) + tops + before,
        landed(0, 1) + landed(1, 0),
        after + landed(1, 1) + ends,
    )
    half = FACES * STACK
    sides = SIDES * STACK
    z_over, z_under, z_top, z_end = [], [], [], []
    v_side, v_near = [[], []], []
    for b in range(3):
        over, under, near = 0.0, 0.0, []
        for a in range(3):
            y = 0.0
            for part, tap in enumerate((tap1, tap1_coarse)):
                chosen = picked[part]
                if b == 0:
                    extra = [chosen[0:half], chosen[sides : 2 * sides]]
                elif b == 1:
                    extra = [chosen[2 * sides : 3 * sides]]
                else:
                    extra = [chosen[half : 2 * half], chosen[3 * sides : 4 * sides]]
                y = y + tap(jnp.concatenate([r[part] for r in stacks[a]] + extra, axis=0), a, b)
            if a == 0:
                over = over + y[0:ROW]
                z_top.append(y[ROW : 2 * ROW])
                under = under + y[2 * ROW : 3 * ROW]
            elif a == 1:
                over = over + y[0:ROW]
                under = under + y[ROW : 2 * ROW]
            else:
                over = over + y[0:ROW]
                under = under + y[ROW : 2 * ROW]
                z_end.append(y[2 * ROW : 3 * ROW])
            rest = y[len(stacks[a]) * COLS :]
            if b != 1:
                v_side[b // 2].append(rest[0:half])
                rest = rest[half:]
            near.append(rest)
        z_over.append(over)
        z_under.append(under)
        v_near.append(near)

    for k, z in enumerate((z_over, z_under, z_top, z_end)):
        z = from_west(z[0]) + z[1] + from_east(z[2])
        zrow[k] = z if k >= 2 else z + b1[...]
    for k in range(2):
        zcol[k] = along_rows(*v_side[k])
    near = along_rows(*[v_near[0][a] + v_near[1][a] + v_near[2][a] for a in range(3)]) + b1[...]
    near = silu(near)
    place = lax.rem(lax.broadcasted_iota(i32, near.shape, 0), STACK)
    low = jnp.where(first, 0.0, pltpu.roll(near, 2, 0))
    high = jnp.where(last, 0.0, pltpu.roll(near, near.shape[0] - 2, 0))
    near = jnp.where(place == FIRST - 1, low, jnp.where(place == FIRST + ROWS, high, near))
    near = near.astype(bf16)

    column = column_of((COLS, C))

    def with_sides(z, f, q):
        west = zcol[0, pl.ds(f * STACK + q, 1), :]
        east = zcol[1, pl.ds(f * STACK + q, 1), :]
        z = z + jnp.where(column == 0, jnp.broadcast_to(west, z.shape), 0.0)
        return z + jnp.where(column == COLS - 1, jnp.broadcast_to(east, z.shape), 0.0)

    def activate(f, _):
        at = pl.ds(pl.multiple_of(f * COLS, COLS), COLS)
        rows2[0, f] = silu(with_sides(zrow[0, at], f, 1)).astype(bf16)
        rows2[1, f] = silu(with_sides(zrow[1, at], f, STACK - 2)).astype(bf16)
        for i in range(ROWS):
            z = acc[f, i * COLS : (i + 1) * COLS]
            if i == 0:
                z = z + zrow[2, at]
            if i == ROWS - 1:
                z = z + zrow[3, at]
            h = silu(with_sides(z, f, FIRST + i)).astype(bf16)
            hp[f, (i + 1) * COLS : (i + 2) * COLS] = h
            if i == 0:
                rows2[2, f] = h
            if i == ROWS - 1:
                rows2[3, f] = h
        return 0

    lax.fori_loop(0, FACES, activate, 0)
    for f in range(FACES):
        face = g * FACES + f
        n, s = jnp.where(first, ns[0, face], f), jnp.where(last, ns[1, face], f)
        hp[f, 0:COLS] = rows2[jnp.where(first, 2 * code[0, face], 0), n]
        hp[f, PIX + COLS : PIX + 2 * COLS] = rows2[jnp.where(last, 1 + 2 * code[1, face], 1), s]
    for k in range(2):
        zcol[k] = along_rows(*[tap2(near[half * k : half * k + half], a, 2 * k) for a in range(3)])

    def finish(f, _):
        z = from_west(conv_own(hp, tap2, f, 0)) + conv_own(hp, tap2, f, 1) + from_east(conv_own(hp, tap2, f, 2))
        for i in range(ROWS):
            feature = with_sides(z[i * COLS : (i + 1) * COLS], f, FIRST + i) + b2[...]
            p = pf[f, i * COLS : (i + 1) * COLS, 0:C]
            denoised = skip_gain * p + output_gain * feature
            out[f, i] = (p + step_ratio * (p - denoised)).astype(bf16)
        return 0

    lax.fori_loop(0, FACES, finish, 0)
    for copy in sent:
        copy.wait_send()


def on_device(groups, tiles, sample, noise, coarse, w1, b1, w2, b2, ns, we, code):
    C = sample.shape[-1]
    w1 = jnp.swapaxes(w1, 2, 3)
    operands = (sample, noise, coarse, ns.T, we.T, code.T, w1, b1.reshape(1, C), w2, b2.reshape(1, C))
    return pl.pallas_call(
        functools.partial(kernel, groups, tiles),
        out_shape=jax.ShapeDtypeStruct(sample.shape, bf16),
        in_specs=[pl.BlockSpec(memory_space=pltpu.HBM)] * len(operands),
        out_specs=pl.BlockSpec(memory_space=pltpu.VMEM),
        scratch_shapes=[
            (pltpu.SMEM if x.dtype == i32 else pltpu.VMEM)(x.shape, x.dtype) for x in operands
        ]
        + [
            pltpu.VMEM((FACES, PIX, WIDE), f32),
            pltpu.VMEM((FACES, PIX, C), f32),
            pltpu.VMEM((FACES, PIX + 2 * COLS, WIDE), bf16),
            pltpu.VMEM((FACES, PIX + 2 * COLS, C), bf16),
            pltpu.VMEM((FACES * COLS, WIDE), bf16),
            pltpu.VMEM((3, FACES * COLS, C), f32),
            pltpu.VMEM((groups, BLOCKS, 16, WIDE), bf16),
            pltpu.VMEM((2, 2, 16, WIDE), bf16),
            pltpu.VMEM((4, FACES, 3, COLS, WIDE), bf16),
            pltpu.VMEM((4, FACES, COLS, C), bf16),
            pltpu.VMEM((2, 4 * SIDES * STACK, groups * BLOCKS * 16), bf16),
            pltpu.VMEM((2, FACES * STACK, C), f32),
            pltpu.VMEM((4, FACES * COLS, C), f32),
            pltpu.SemaphoreType.DMA((len(operands),)),
            pltpu.SemaphoreType.DMA((13,)),
            pltpu.SemaphoreType.DMA((13,)),
        ],
        compiler_params=pltpu.CompilerParams(
            collective_id=0, has_side_effects=True, vmem_limit_bytes=32 * 2**20
        ),
    )(*operands)


def solution(mesh):
    return jax.shard_map(
        functools.partial(on_device, mesh.shape["face"], mesh.shape["tile"]),
        mesh=mesh,
        in_specs=(P("face", "tile", None, None),) * 3 + (P(),) * 7,
        out_specs=P("face", "tile", None, None),
        check_vma=False,
    )
```

```python
import functools

import jax
import jax.numpy as jnp
from jax import lax
from jax.experimental import pallas as pl
from jax.experimental.pallas import tpu as pltpu
from jax.sharding import PartitionSpec as P

MESH = pl.DeviceIdType.MESH
f32 = jnp.float32
bf16 = jnp.bfloat16
i32 = jnp.int32

noise_gain = 0.6
input_gain = 0.7071067811865476
skip_gain = 0.5
output_gain = 0.7071067811865476
step_ratio = -0.4

UP = 8
FACES = 3
ROWS = 8
COLS = 32
COARSE = COLS // UP
PIX = ROWS * COLS
SIDES = 2 * FACES
WIDE = 256

BLOCKS = 12
OUTER, INNER, OVER, UNDER, EMPTY = 1, 4, 7, 9, 11
STACK = 16
FIRST = 4


def dot(a, b):
    return jnp.dot(a, b, preferred_element_type=f32)


def dot_t(a, b):
    return lax.dot_general(a, b, (((1,), (1,)), ((), ())), preferred_element_type=f32)


def column_of(shape):
    return lax.rem(lax.broadcasted_iota(i32, shape, 0), COLS)


def from_west(z):
    return jnp.where(column_of(z.shape) == 0, 0.0, pltpu.roll(z, 1, 0))


def from_east(z):
    return jnp.where(column_of(z.shape) == COLS - 1, 0.0, pltpu.roll(z, z.shape[0] - 1, 0))


def along_rows(v0, v1, v2):
    return pltpu.roll(v0, 1, 0) + v1 + pltpu.roll(v2, v2.shape[0] - 1, 0)


def silu(u):
    return u / (1.0 + jnp.exp(-u))


def spread(rows, count):
    width = rows[0][1].shape[1]
    place = lax.broadcasted_iota(i32, (count, width), 0)
    out = jnp.zeros((count, width), f32)
    for at, row in rows:
        out = jnp.where(place == at, jnp.broadcast_to(row, (count, width)), out)
    return out


def kernel(
    groups,
    tiles,
    sample_hbm,
    noise_hbm,
    coarse_hbm,
    ns_hbm,
    we_hbm,
    code_hbm,
    w1_hbm,
    b1_hbm,
    w2_hbm,
    b2_hbm,
    out,
    sample,
    noise,
    coarse,
    ns,
    we,
    code,
    w1,
    b1,
    w2,
    b2,
    pf,
    acc,
    xp,
    hp,
    up,
    cclass,
    cols,
    corner,
    rows1,
    rows2,
    pick,
    zcol,
    zrow,
    load_sem,
    send_sem,
    recv_sem,
):
    g = lax.axis_index("face")
    t = lax.axis_index("tile")
    above = lax.rem(t + tiles - 1, tiles)
    below = lax.rem(t + 1, tiles)
    first = t == 0
    last = t == tiles - 1
    C = acc.shape[2]
    lines = groups * BLOCKS * 16

    loads = [
        pltpu.make_async_copy(src, dst, load_sem.at[i])
        for i, (src, dst) in enumerate(
            [
                (sample_hbm, sample),
                (noise_hbm, noise),
                (coarse_hbm, coarse),
                (ns_hbm, ns),
                (we_hbm, we),
                (code_hbm, code),
                (w1_hbm, w1),
                (b1_hbm, b1),
                (w2_hbm, w2),
                (b2_hbm, b2),
            ]
        )
    ]
    for copy in loads[:6]:
        copy.start()

    barrier = pltpu.get_barrier_semaphore()
    for d in (2, 1, 3, 0):
        for k, there in enumerate((t, above, below)):
            if d or k:
                pl.semaphore_signal(
                    barrier, inc=1, device_id=(lax.rem(g + d, groups), there), device_id_type=MESH
                )

    for f in range(FACES):
        zero_row = jnp.zeros((COLS, WIDE), bf16)
        xp[f, 0:COLS] = zero_row
        xp[f, COLS + PIX : 2 * COLS + PIX] = zero_row
        xp[f, COLS : COLS + PIX, 128:WIDE] = jnp.zeros((PIX, WIDE - 128), bf16)
        pf[f, :, 128:WIDE] = jnp.zeros((PIX, WIDE - 128), f32)
    for d in range(groups):
        cols[d, EMPTY] = jnp.zeros((16, WIDE), bf16)

    for copy in loads[:3]:
        copy.wait()
    for f in range(FACES):
        p = sample[f].astype(f32) + noise_gain * noise[f].astype(f32)
        p = p.reshape(PIX, C)
        pf[f, :, 0:C] = p
        xp[f, COLS : COLS + PIX, 0:C] = (p * input_gain).astype(bf16)
        for r in range(2):
            rows1[2, f, r] = xp[f, (1 + r) * COLS : (2 + r) * COLS]
            rows1[3, f, r] = xp[f, PIX - COLS + r * COLS : PIX + r * COLS]
    raw, tops, ends = [], [], []
    for f in range(FACES):
        c = coarse[f, 0].astype(f32)
        c = jnp.concatenate([jnp.zeros((COARSE, WIDE - C), f32), c], axis=1)
        each = [c[j : j + 1] for j in range(COARSE)]
        raw += [(4 * f + j, each[j]) for j in range(COARSE)]
        edges = [(24 + 2 * f, each[0]), (25 + 2 * f, each[COARSE - 1])]
        wide = jnp.concatenate([jnp.broadcast_to(e, (UP, WIDE)) for e in each], axis=0).astype(bf16)
        up[f * COLS : (f + 1) * COLS] = wide
        rows1[2, f, 2] = wide
        rows1[3, f, 2] = wide
        tops += edges
        ends += edges
        for k, block, j in ((0, OUTER, 0), (3, OUTER, COLS - 1), (1, INNER, 1), (2, INNER, COLS - 2)):
            line = [pf[f, i * COLS + j : i * COLS + j + 1, :] * input_gain for i in range(ROWS)]
            half = spread(list(enumerate(line)), ROWS)
            if k in (0, 1):
                lower = half
            else:
                cols[g, block + f] = jnp.concatenate([lower, half], axis=0).astype(bf16)
            tops += [(8 * f + 2 * k + r, line[r]) for r in range(2)]
            ends += [(8 * f + 2 * k + r, line[ROWS - 2 + r]) for r in range(2)]
    cols[g, 0] = spread(raw, 16).astype(bf16)
    corner[0] = spread(tops, 32).astype(bf16).reshape(2, 16, WIDE)
    corner[1] = spread(ends, 32).astype(bf16).reshape(2, 16, WIDE)

    sent = []

    def add(src, dst, there):
        n = len(sent)
        sent.append(
            pltpu.make_async_remote_copy(
                src_ref=src,
                dst_ref=dst,
                send_sem=send_sem.at[n],
                recv_sem=recv_sem.at[n],
                device_id=there,
                device_id_type=MESH,
            )
        )

    table = cols.at[g, pl.ds(0, OVER)]
    over = cols.at[g, pl.ds(OVER, 2)]
    under = cols.at[g, pl.ds(UNDER, 2)]
    for d in (2, 1, 3):
        far = lax.rem(g + d, groups)
        add(corner.at[0], under, (far, above))
        add(corner.at[1], over, (far, below))
        add(table, table, (far, t))
    add(corner.at[0], under, (g, above))
    add(corner.at[1], over, (g, below))
    add(rows1.at[2], rows1.at[1], (g, above))
    add(rows1.at[3], rows1.at[0], (g, below))

    pl.semaphore_wait(barrier, 3 * groups - 1)
    for copy in sent:
        copy.start()
    for copy in loads[6:]:
        copy.start()
    for copy in loads[3:6]:
        copy.wait()

    lane = lax.broadcasted_iota(i32, (STACK, lines), 1)
    place = lax.broadcasted_iota(i32, (STACK, lines), 0)

    def split(face):
        group = sum((face >= FACES * k).astype(i32) for k in range(1, groups))
        return group, face - FACES * group

    def across(face, side):
        edge = code[2 + side, face]
        return we[side, face], 3 * jnp.where(side == 1, edge, 1 - edge)

    def write_pick(at, face, column, beyond):
        group, f = split(face)
        base = group * (BLOCKS * 16)
        inner = ((column == 1) | (column == 2)).astype(i32)
        high = (column >= 2).astype(i32)

        def line(ff, row):
            if row < 0:
                return base + OVER * 16 + ff * 8 + column * 2 + 2 + row
            if row >= ROWS:
                return base + UNDER * 16 + ff * 8 + column * 2 + row - ROWS
            return base + (OUTER + inner * (INNER - OUTER) + ff) * 16 + high * 8 + row

        def condition(ff, row):
            if row < 0:
                return base + OVER * 16 + 24 + ff * 2 + high
            if row >= ROWS:
                return base + UNDER * 16 + 24 + ff * 2 + high
            return base + ff * COARSE + high * (COARSE - 1)

        n, s = ns[0, face], ns[1, face]
        flip_n, flip_s = code[0, face] == 1, code[1, face] == 1
        for part, where in enumerate((line, condition)):
            north = jnp.where(beyond, -1, jnp.where(flip_n, where(n, 0), where(n, -1)))
            south = jnp.where(beyond, -1, jnp.where(flip_s, where(s, ROWS - 1), where(s, ROWS)))
            target = jnp.broadcast_to(where(f, 0), place.shape)
            if part == 0:
                target = target + place - FIRST
            for q, value in (
                (0, where(f, -2)),
                (1, where(f, -1)),
                (2, jnp.where(first, -1, where(f, 0))),
                (3, jnp.where(first, north, where(f, -1))),
                (12, jnp.where(last, south, where(f, ROWS))),
                (13, jnp.where(last, -1, where(f, ROWS - 1))),
                (14, where(f, ROWS)),
                (15, where(f, ROWS + 1)),
            ):
                target = jnp.where(place == q, value, target)
            at = pl.multiple_of(at, STACK)
            pick[part, pl.ds(at, STACK), :] = jnp.where(lane == target, 1.0, 0.0).astype(bf16)

    def pick_side(n, _):
        side = (n >= FACES).astype(i32)
        face = g * FACES + n - FACES * side
        near, column = across(face, side)
        west_face, west_column = across(near, 0)
        east_face, east_column = across(near, 1)
        at_west = column == 0
        at_east = column == 3
        write_pick(n * STACK, near, column, True)
        write_pick(
            (SIDES + n) * STACK,
            jnp.where(at_west, west_face, near),
            jnp.where(at_west, west_column, 2),
            at_west,
        )
        write_pick((2 * SIDES + n) * STACK, near, column, False)
        write_pick(
            (3 * SIDES + n) * STACK,
            jnp.where(at_east, east_face, near),
            jnp.where(at_east, east_column, 1),
            at_east,
        )
        return 0

    lax.fori_loop(0, SIDES, pick_side, 0)

    def tap1(x, a, b):
        return dot_t(x, w1[a, b, :, 0:WIDE])

    def tap1_coarse(x, a, b):
        return dot_t(x, w1[a, b, :, w1.shape[3] - WIDE :])

    def tap2(x, a, b):
        return dot(x, w2[a, b])

    def conv_own(src, tap, f, b):
        z = tap(src[f, 0:PIX], 0, b)
        z = z + tap(src[f, COLS : COLS + PIX], 1, b)
        return z + tap(src[f, 2 * COLS : 2 * COLS + PIX], 2, b)

    for copy in loads[6:]:
        copy.wait()
    parts = []
    for b in range(3):
        c0, c1, c2 = [tap1_coarse(up[...], a, b) for a in range(3)]
        parts.append((c1 + c2, c0 + c1 + c2, c0 + c1))
    for k in range(3):
        cclass[k] = from_west(parts[0][k]) + parts[1][k] + from_east(parts[2][k]) + b1[...]

    def own1(f, _):
        z = from_west(conv_own(xp, tap1, f, 0)) + conv_own(xp, tap1, f, 1) + from_east(conv_own(xp, tap1, f, 2))
        at = pl.ds(pl.multiple_of(f * COLS, COLS), COLS)
        for i in range(ROWS):
            k = 0 if i == 0 else 2 if i == ROWS - 1 else 1
            acc[f, i * COLS : (i + 1) * COLS] = z[i * COLS : (i + 1) * COLS] + cclass[k, at]
        return 0

    lax.fori_loop(0, FACES, own1, 0)

    for copy in sent:
        copy.wait_recv()
    table = cols[...].reshape(lines, WIDE)
    picked = [dot(pick[part], table).astype(bf16) for part in range(2)]

    tops, ends, after, before = [], [], [], []
    for f in range(FACES):
        face = g * FACES + f
        n, s = jnp.where(first, ns[0, face], f), jnp.where(last, ns[1, face], f)
        flip_n, flip_s = code[0, face], code[1, face]
        k = jnp.where(first, 2 * flip_n, 0)
        r = jnp.where(k == 0, 1, 0)
        tops.append((rows1[k, n, r], rows1[k, n, 2]))
        k = jnp.where(last, 1 + 2 * flip_s, 1)
        r = jnp.where(k == 1, 0, 1)
        ends.append((rows1[k, s, r], rows1[k, s, 2]))
        s = jnp.where(first, ns[1, face], f)
        k = jnp.where(first, 2 - 2 * flip_s, 2)
        r = jnp.where(k == 0, 1, 0)
        after.append((rows1[k, s, r], rows1[k, s, 2]))
        n = jnp.where(last, ns[0, face], f)
        k = jnp.where(last, 3 - 2 * flip_n, 3)
        r = jnp.where(k == 1, 0, 1)
        before.append((rows1[k, n, r], rows1[k, n, 2]))

    def landed(k, r):
        return [(rows1[k, f, r], rows1[k, f, 2]) for f in range(FACES)]

    ROW = FACES * COLS
    stacks = (
        landed(0, 0) + tops + before,
        landed(0, 1) + landed(1, 0),
        after + landed(1, 1) + ends,
    )
    half = FACES * STACK
    sides = SIDES * STACK
    z_over, z_under, z_top, z_end = [], [], [], []
    v_side, v_near = [[], []], []
    for b in range(3):
        over, under, near = 0.0, 0.0, []
        for a in range(3):
            y = 0.0
            for part, tap in enumerate((tap1, tap1_coarse)):
                chosen = picked[part]
                if b == 0:
                    extra = [chosen[0:half], chosen[sides : 2 * sides]]
                elif b == 1:
                    extra = [chosen[2 * sides : 3 * sides]]
                else:
                    extra = [chosen[half : 2 * half], chosen[3 * sides : 4 * sides]]
                y = y + tap(jnp.concatenate([r[part] for r in stacks[a]] + extra, axis=0), a, b)
            if a == 0:
                over = over + y[0:ROW]
                z_top.append(y[ROW : 2 * ROW])
                under = under + y[2 * ROW : 3 * ROW]
            elif a == 1:
                over = over + y[0:ROW]
                under = under + y[ROW : 2 * ROW]
            else:
                over = over + y[0:ROW]
                under = under + y[ROW : 2 * ROW]
                z_end.append(y[2 * ROW : 3 * ROW])
            rest = y[len(stacks[a]) * COLS :]
            if b != 1:
                v_side[b // 2].append(rest[0:half])
                rest = rest[half:]
            near.append(rest)
        z_over.append(over)
        z_under.append(under)
        v_near.append(near)

    for k, z in enumerate((z_over, z_under, z_top, z_end)):
        z = from_west(z[0]) + z[1] + from_east(z[2])
        zrow[k] = z if k >= 2 else z + b1[...]
    for k in range(2):
        zcol[k] = along_rows(*v_side[k])
    near = along_rows(*[v_near[0][a] + v_near[1][a] + v_near[2][a] for a in range(3)]) + b1[...]
    near = silu(near)
    place = lax.rem(lax.broadcasted_iota(i32, near.shape, 0), STACK)
    low = jnp.where(first, 0.0, pltpu.roll(near, 2, 0))
    high = jnp.where(last, 0.0, pltpu.roll(near, near.shape[0] - 2, 0))
    near = jnp.where(place == FIRST - 1, low, jnp.where(place == FIRST + ROWS, high, near))
    near = near.astype(bf16)

    column = column_of((COLS, C))

    def with_sides(z, f, q):
        west = zcol[0, pl.ds(f * STACK + q, 1), :]
        east = zcol[1, pl.ds(f * STACK + q, 1), :]
        z = z + jnp.where(column == 0, jnp.broadcast_to(west, z.shape), 0.0)
        return z + jnp.where(column == COLS - 1, jnp.broadcast_to(east, z.shape), 0.0)

    def activate(f, _):
        at = pl.ds(pl.multiple_of(f * COLS, COLS), COLS)
        rows2[0, f] = silu(with_sides(zrow[0, at], f, 1)).astype(bf16)
        rows2[1, f] = silu(with_sides(zrow[1, at], f, STACK - 2)).astype(bf16)
        for i in range(ROWS):
            z = acc[f, i * COLS : (i + 1) * COLS]
            if i == 0:
                z = z + zrow[2, at]
            if i == ROWS - 1:
                z = z + zrow[3, at]
            h = silu(with_sides(z, f, FIRST + i)).astype(bf16)
            hp[f, (i + 1) * COLS : (i + 2) * COLS] = h
            if i == 0:
                rows2[2, f] = h
            if i == ROWS - 1:
                rows2[3, f] = h
        return 0

    lax.fori_loop(0, FACES, activate, 0)
    for f in range(FACES):
        face = g * FACES + f
        n, s = jnp.where(first, ns[0, face], f), jnp.where(last, ns[1, face], f)
        hp[f, 0:COLS] = rows2[jnp.where(first, 2 * code[0, face], 0), n]
        hp[f, PIX + COLS : PIX + 2 * COLS] = rows2[jnp.where(last, 1 + 2 * code[1, face], 1), s]
    for k in range(2):
        zcol[k] = along_rows(*[tap2(near[half * k : half * k + half], a, 2 * k) for a in range(3)])

    def finish(f, _):
        z = from_west(conv_own(hp, tap2, f, 0)) + conv_own(hp, tap2, f, 1) + from_east(conv_own(hp, tap2, f, 2))
        for i in range(ROWS):
            feature = with_sides(z[i * COLS : (i + 1) * COLS], f, FIRST + i) + b2[...]
            p = pf[f, i * COLS : (i + 1) * COLS, 0:C]
            denoised = skip_gain * p + output_gain * feature
            out[f, i] = (p + step_ratio * (p - denoised)).astype(bf16)
        return 0

    lax.fori_loop(0, FACES, finish, 0)
    for copy in sent:
        copy.wait_send()


def on_device(groups, tiles, sample, noise, coarse, w1, b1, w2, b2, ns, we, code):
    C = sample.shape[-1]
    w1 = jnp.swapaxes(w1, 2, 3)
    operands = (sample, noise, coarse, ns.T, we.T, code.T, w1, b1.reshape(1, C), w2, b2.reshape(1, C))
    return pl.pallas_call(
        functools.partial(kernel, groups, tiles),
        out_shape=jax.ShapeDtypeStruct(sample.shape, bf16),
        in_specs=[pl.BlockSpec(memory_space=pltpu.HBM)] * len(operands),
        out_specs=pl.BlockSpec(memory_space=pltpu.VMEM),
        scratch_shapes=[
            (pltpu.SMEM if x.dtype == i32 else pltpu.VMEM)(x.shape, x.dtype) for x in operands
        ]
        + [
            pltpu.VMEM((FACES, PIX, WIDE), f32),
            pltpu.VMEM((FACES, PIX, C), f32),
            pltpu.VMEM((FACES, PIX + 2 * COLS, WIDE), bf16),
            pltpu.VMEM((FACES, PIX + 2 * COLS, C), bf16),
            pltpu.VMEM((FACES * COLS, WIDE), bf16),
            pltpu.VMEM((3, FACES * COLS, C), f32),
            pltpu.VMEM((groups, BLOCKS, 16, WIDE), bf16),
            pltpu.VMEM((2, 2, 16, WIDE), bf16),
            pltpu.VMEM((4, FACES, 3, COLS, WIDE), bf16),
            pltpu.VMEM((4, FACES, COLS, C), bf16),
            pltpu.VMEM((2, 4 * SIDES * STACK, groups * BLOCKS * 16), bf16),
            pltpu.VMEM((2, FACES * STACK, C), f32),
            pltpu.VMEM((4, FACES * COLS, C), f32),
            pltpu.SemaphoreType.DMA((len(operands),)),
            pltpu.SemaphoreType.DMA((13,)),
            pltpu.SemaphoreType.DMA((13,)),
        ],
        compiler_params=pltpu.CompilerParams(
            collective_id=0, has_side_effects=True, vmem_limit_bytes=32 * 2**20
        ),
    )(*[pltpu.with_memory_space_constraint(x, pltpu.HBM) for x in operands])


def solution(mesh):
    return jax.shard_map(
        functools.partial(on_device, mesh.shape["face"], mesh.shape["tile"]),
        mesh=mesh,
        in_specs=(P("face", "tile", None, None),) * 3 + (P(),) * 7,
        out_specs=P("face", "tile", None, None),
        check_vma=False,
    )
```

```python
import functools

import jax
import jax.numpy as jnp
from jax import lax
from jax.experimental import pallas as pl
from jax.experimental.pallas import tpu as pltpu
from jax.sharding import PartitionSpec as P

MESH = pl.DeviceIdType.MESH
f32 = jnp.float32
bf16 = jnp.bfloat16
i32 = jnp.int32

noise_gain = 0.6
input_gain = 0.7071067811865476
skip_gain = 0.5
output_gain = 0.7071067811865476
step_ratio = -0.4

UP = 8
FACES = 3
ROWS = 8
COLS = 32
COARSE = COLS // UP
PIX = ROWS * COLS
SIDES = 2 * FACES
WIDE = 256

BLOCKS = 12
OUTER, INNER, OVER, UNDER, EMPTY = 1, 4, 7, 9, 11
STACK = 16
FIRST = 4


def dot(a, b):
    return jnp.dot(a, b, preferred_element_type=f32)


def dot_t(a, b):
    return lax.dot_general(a, b, (((1,), (1,)), ((), ())), preferred_element_type=f32)


def column_of(shape):
    return lax.rem(lax.broadcasted_iota(i32, shape, 0), COLS)


def from_west(z):
    return jnp.where(column_of(z.shape) == 0, 0.0, pltpu.roll(z, 1, 0))


def from_east(z):
    return jnp.where(column_of(z.shape) == COLS - 1, 0.0, pltpu.roll(z, z.shape[0] - 1, 0))


def along_rows(v0, v1, v2):
    return pltpu.roll(v0, 1, 0) + v1 + pltpu.roll(v2, v2.shape[0] - 1, 0)


def silu(u):
    return u / (1.0 + jnp.exp(-u))


def spread(rows, count):
    width = rows[0][1].shape[1]
    place = lax.broadcasted_iota(i32, (count, width), 0)
    out = jnp.zeros((count, width), f32)
    for at, row in rows:
        out = jnp.where(place == at, jnp.broadcast_to(row, (count, width)), out)
    return out


def kernel(
    groups,
    tiles,
    sample_hbm,
    noise_hbm,
    coarse_hbm,
    ns_hbm,
    we_hbm,
    code_hbm,
    w1_hbm,
    b1_hbm,
    w2_hbm,
    b2_hbm,
    out,
    sample,
    noise,
    coarse,
    ns,
    we,
    code,
    w1,
    b1,
    w2,
    b2,
    pf,
    acc,
    acc2,
    own_line,
    z_line,
    xp,
    hp,
    up,
    cclass,
    cols,
    corner,
    rows1,
    rows2,
    pick,
    zcol,
    zrow,
    load_sem,
    send_sem,
    recv_sem,
):
    g = lax.axis_index("face")
    t = lax.axis_index("tile")
    above = lax.rem(t + tiles - 1, tiles)
    below = lax.rem(t + 1, tiles)
    first = t == 0
    last = t == tiles - 1
    C = acc.shape[2]
    lines = groups * BLOCKS * 16

    loads = [
        pltpu.make_async_copy(src, dst, load_sem.at[i])
        for i, (src, dst) in enumerate(
            [
                (sample_hbm, sample),
                (noise_hbm, noise),
                (coarse_hbm, coarse),
                (ns_hbm, ns),
                (we_hbm, we),
                (code_hbm, code),
                (w1_hbm, w1),
                (b1_hbm, b1),
                (w2_hbm, w2),
                (b2_hbm, b2),
            ]
        )
    ]
    for copy in loads[:6]:
        copy.start()

    barrier = pltpu.get_barrier_semaphore()
    for d in (2, 1, 3, 0):
        for k, there in enumerate((t, above, below)):
            if d or k:
                pl.semaphore_signal(
                    barrier, inc=1, device_id=(lax.rem(g + d, groups), there), device_id_type=MESH
                )

    for f in range(FACES):
        zero_row = jnp.zeros((COLS, WIDE), bf16)
        xp[f, 0:COLS] = zero_row
        xp[f, COLS + PIX : 2 * COLS + PIX] = zero_row
        xp[f, COLS : COLS + PIX, 128:WIDE] = jnp.zeros((PIX, WIDE - 128), bf16)
        pf[f, :, 128:WIDE] = jnp.zeros((PIX, WIDE - 128), f32)
        hp[f, 0 : 2 * COLS] = jnp.zeros((2 * COLS, C), bf16)
        hp[f, PIX : PIX + 2 * COLS] = jnp.zeros((2 * COLS, C), bf16)
    for d in range(groups):
        cols[d, EMPTY] = jnp.zeros((16, WIDE), bf16)

    for copy in loads[:3]:
        copy.wait()
    for f in range(FACES):
        p = sample[f].astype(f32) + noise_gain * noise[f].astype(f32)
        p = p.reshape(PIX, C)
        pf[f, :, 0:C] = p
        xp[f, COLS : COLS + PIX, 0:C] = (p * input_gain).astype(bf16)
        for r in range(2):
            rows1[2, f, r] = xp[f, (1 + r) * COLS : (2 + r) * COLS]
            rows1[3, f, r] = xp[f, PIX - COLS + r * COLS : PIX + r * COLS]
    raw, tops, ends = [], [], []
    for f in range(FACES):
        c = coarse[f, 0].astype(f32)
        c = jnp.concatenate([jnp.zeros((COARSE, WIDE - C), f32), c], axis=1)
        each = [c[j : j + 1] for j in range(COARSE)]
        raw += [(4 * f + j, each[j]) for j in range(COARSE)]
        edges = [(24 + 2 * f, each[0]), (25 + 2 * f, each[COARSE - 1])]
        wide = jnp.concatenate([jnp.broadcast_to(e, (UP, WIDE)) for e in each], axis=0).astype(bf16)
        up[f * COLS : (f + 1) * COLS] = wide
        rows1[2, f, 2] = wide
        rows1[3, f, 2] = wide
        tops += edges
        ends += edges
        for k, block, j in ((0, OUTER, 0), (3, OUTER, COLS - 1), (1, INNER, 1), (2, INNER, COLS - 2)):
            line = [pf[f, i * COLS + j : i * COLS + j + 1, :] * input_gain for i in range(ROWS)]
            half = spread(list(enumerate(line)), ROWS)
            if k in (0, 1):
                lower = half
            else:
                cols[g, block + f] = jnp.concatenate([lower, half], axis=0).astype(bf16)
            tops += [(8 * f + 2 * k + r, line[r]) for r in range(2)]
            ends += [(8 * f + 2 * k + r, line[ROWS - 2 + r]) for r in range(2)]
    cols[g, 0] = spread(raw, 16).astype(bf16)
    corner[0] = spread(tops, 32).astype(bf16).reshape(2, 16, WIDE)
    corner[1] = spread(ends, 32).astype(bf16).reshape(2, 16, WIDE)

    sent = []

    def add(src, dst, there):
        n = len(sent)
        sent.append(
            pltpu.make_async_remote_copy(
                src_ref=src,
                dst_ref=dst,
                send_sem=send_sem.at[n],
                recv_sem=recv_sem.at[n],
                device_id=there,
                device_id_type=MESH,
            )
        )

    table = cols.at[g, pl.ds(0, OVER)]
    over = cols.at[g, pl.ds(OVER, 2)]
    under = cols.at[g, pl.ds(UNDER, 2)]
    for d in (2, 1, 3):
        far = lax.rem(g + d, groups)
        add(corner.at[0], under, (far, above))
        add(corner.at[1], over, (far, below))
        add(table, table, (far, t))
    add(corner.at[0], under, (g, above))
    add(corner.at[1], over, (g, below))
    add(rows1.at[2], rows1.at[1], (g, above))
    add(rows1.at[3], rows1.at[0], (g, below))

    pl.semaphore_wait(barrier, 3 * groups - 1)
    for copy in sent:
        copy.start()
    for copy in loads[6:]:
        copy.start()
    for copy in loads[3:6]:
        copy.wait()

    lane = lax.broadcasted_iota(i32, (STACK, lines), 1)
    place = lax.broadcasted_iota(i32, (STACK, lines), 0)

    def split(face):
        group = sum((face >= FACES * k).astype(i32) for k in range(1, groups))
        return group, face - FACES * group

    def across(face, side):
        edge = code[2 + side, face]
        return we[side, face], 3 * jnp.where(side == 1, edge, 1 - edge)

    def write_pick(at, face, column, beyond):
        group, f = split(face)
        base = group * (BLOCKS * 16)
        inner = ((column == 1) | (column == 2)).astype(i32)
        high = (column >= 2).astype(i32)

        def line(ff, row):
            if row < 0:
                return base + OVER * 16 + ff * 8 + column * 2 + 2 + row
            if row >= ROWS:
                return base + UNDER * 16 + ff * 8 + column * 2 + row - ROWS
            return base + (OUTER + inner * (INNER - OUTER) + ff) * 16 + high * 8 + row

        def condition(ff, row):
            if row < 0:
                return base + OVER * 16 + 24 + ff * 2 + high
            if row >= ROWS:
                return base + UNDER * 16 + 24 + ff * 2 + high
            return base + ff * COARSE + high * (COARSE - 1)

        n, s = ns[0, face], ns[1, face]
        flip_n, flip_s = code[0, face] == 1, code[1, face] == 1
        for part, where in enumerate((line, condition)):
            north = jnp.where(beyond, -1, jnp.where(flip_n, where(n, 0), where(n, -1)))
            south = jnp.where(beyond, -1, jnp.where(flip_s, where(s, ROWS - 1), where(s, ROWS)))
            target = jnp.broadcast_to(where(f, 0), place.shape)
            if part == 0:
                target = target + place - FIRST
            for q, value in (
                (0, where(f, -2)),
                (1, where(f, -1)),
                (2, jnp.where(first, -1, where(f, 0))),
                (3, jnp.where(first, north, where(f, -1))),
                (12, jnp.where(last, south, where(f, ROWS))),
                (13, jnp.where(last, -1, where(f, ROWS - 1))),
                (14, where(f, ROWS)),
                (15, where(f, ROWS + 1)),
            ):
                target = jnp.where(place == q, value, target)
            at = pl.multiple_of(at, STACK)
            pick[part, pl.ds(at, STACK), :] = jnp.where(lane == target, 1.0, 0.0).astype(bf16)

    def pick_side(n, _):
        side = (n >= FACES).astype(i32)
        face = g * FACES + n - FACES * side
        near, column = across(face, side)
        west_face, west_column = across(near, 0)
        east_face, east_column = across(near, 1)
        at_west = column == 0
        at_east = column == 3
        write_pick(n * STACK, near, column, True)
        write_pick(
            (SIDES + n) * STACK,
            jnp.where(at_west, west_face, near),
            jnp.where(at_west, west_column, 2),
            at_west,
        )
        write_pick((2 * SIDES + n) * STACK, near, column, False)
        write_pick(
            (3 * SIDES + n) * STACK,
            jnp.where(at_east, east_face, near),
            jnp.where(at_east, east_column, 1),
            at_east,
        )
        return 0

    lax.fori_loop(0, SIDES, pick_side, 0)

    def tap1(x, a, b):
        return dot_t(x, w1[a, b, :, 0:WIDE])

    def tap1_coarse(x, a, b):
        return dot_t(x, w1[a, b, :, w1.shape[3] - WIDE :])

    def tap2(x, a, b):
        return dot(x, w2[a, b])

    def conv_own(src, tap, f, b):
        z = tap(src[f, 0:PIX], 0, b)
        z = z + tap(src[f, COLS : COLS + PIX], 1, b)
        return z + tap(src[f, 2 * COLS : 2 * COLS + PIX], 2, b)

    for copy in loads[6:]:
        copy.wait()
    parts = []
    for b in range(3):
        c0, c1, c2 = [tap1_coarse(up[...], a, b) for a in range(3)]
        parts.append((c1 + c2, c0 + c1 + c2, c0 + c1))
    for k in range(3):
        cclass[k] = from_west(parts[0][k]) + parts[1][k] + from_east(parts[2][k]) + b1[...]

    def own1(f, _):
        z = from_west(conv_own(xp, tap1, f, 0)) + conv_own(xp, tap1, f, 1) + from_east(conv_own(xp, tap1, f, 2))
        at = pl.ds(pl.multiple_of(f * COLS, COLS), COLS)
        for i in range(ROWS):
            k = 0 if i == 0 else 2 if i == ROWS - 1 else 1
            acc[f, i * COLS : (i + 1) * COLS] = z[i * COLS : (i + 1) * COLS] + cclass[k, at]
        return 0

    lax.fori_loop(0, FACES, own1, 0)

    column = column_of((COLS, C))
    border = (column == 0) | (column == COLS - 1)

    def inside(f, _):
        for i in range(1, ROWS - 1):
            h = silu(acc[f, i * COLS : (i + 1) * COLS])
            hp[f, (i + 1) * COLS : (i + 2) * COLS] = jnp.where(border, 0.0, h).astype(bf16)
        return 0

    lax.fori_loop(0, FACES, inside, 0)

    def own2(f, _):
        z = from_west(conv_own(hp, tap2, f, 0)) + conv_own(hp, tap2, f, 1) + from_east(conv_own(hp, tap2, f, 2))
        acc2[f] = z + b2[...]
        return 0

    lax.fori_loop(0, FACES, own2, 0)
    for k, j in ((0, 0), (1, COLS - 1)):
        for f in range(FACES):
            line = [(FIRST + i, acc[f, i * COLS + j : i * COLS + j + 1, :]) for i in range(1, ROWS - 1)]
            own_line[k, f * STACK : (f + 1) * STACK] = spread(line, STACK)

    for copy in sent:
        copy.wait_recv()
    table = cols[...].reshape(lines, WIDE)
    picked = [dot(pick[part], table).astype(bf16) for part in range(2)]

    tops, ends, after, before = [], [], [], []
    for f in range(FACES):
        face = g * FACES + f
        n, s = jnp.where(first, ns[0, face], f), jnp.where(last, ns[1, face], f)
        flip_n, flip_s = code[0, face], code[1, face]
        k = jnp.where(first, 2 * flip_n, 0)
        r = jnp.where(k == 0, 1, 0)
        tops.append((rows1[k, n, r], rows1[k, n, 2]))
        k = jnp.where(last, 1 + 2 * flip_s, 1)
        r = jnp.where(k == 1, 0, 1)
        ends.append((rows1[k, s, r], rows1[k, s, 2]))
        s = jnp.where(first, ns[1, face], f)
        k = jnp.where(first, 2 - 2 * flip_s, 2)
        r = jnp.where(k == 0, 1, 0)
        after.append((rows1[k, s, r], rows1[k, s, 2]))
        n = jnp.where(last, ns[0, face], f)
        k = jnp.where(last, 3 - 2 * flip_n, 3)
        r = jnp.where(k == 1, 0, 1)
        before.append((rows1[k, n, r], rows1[k, n, 2]))

    def landed(k, r):
        return [(rows1[k, f, r], rows1[k, f, 2]) for f in range(FACES)]

    ROW = FACES * COLS
    stacks = (
        landed(0, 0) + tops + before,
        landed(0, 1) + landed(1, 0),
        after + landed(1, 1) + ends,
    )
    half = FACES * STACK
    sides = SIDES * STACK
    z_over, z_under, z_top, z_end = [], [], [], []
    v_side, v_near = [[], []], []
    for b in range(3):
        over, under, near = 0.0, 0.0, []
        for a in range(3):
            y = 0.0
            for part, tap in enumerate((tap1, tap1_coarse)):
                chosen = picked[part]
                if b == 0:
                    extra = [chosen[0:half], chosen[sides : 2 * sides]]
                elif b == 1:
                    extra = [chosen[2 * sides : 3 * sides]]
                else:
                    extra = [chosen[half : 2 * half], chosen[3 * sides : 4 * sides]]
                y = y + tap(jnp.concatenate([r[part] for r in stacks[a]] + extra, axis=0), a, b)
            if a == 0:
                over = over + y[0:ROW]
                z_top.append(y[ROW : 2 * ROW])
                under = under + y[2 * ROW : 3 * ROW]
            elif a == 1:
                over = over + y[0:ROW]
                under = under + y[ROW : 2 * ROW]
            else:
                over = over + y[0:ROW]
                under = under + y[ROW : 2 * ROW]
                z_end.append(y[2 * ROW : 3 * ROW])
            rest = y[len(stacks[a]) * COLS :]
            if b != 1:
                v_side[b // 2].append(rest[0:half])
                rest = rest[half:]
            near.append(rest)
        z_over.append(over)
        z_under.append(under)
        v_near.append(near)

    for k, z in enumerate((z_over, z_under, z_top, z_end)):
        z = from_west(z[0]) + z[1] + from_east(z[2])
        zrow[k] = z if k >= 2 else z + b1[...]
    for k in range(2):
        zcol[k] = along_rows(*v_side[k])
    near = along_rows(*[v_near[0][a] + v_near[1][a] + v_near[2][a] for a in range(3)]) + b1[...]
    near = silu(near)
    place = lax.rem(lax.broadcasted_iota(i32, near.shape, 0), STACK)
    low = jnp.where(first, 0.0, pltpu.roll(near, 2, 0))
    high = jnp.where(last, 0.0, pltpu.roll(near, near.shape[0] - 2, 0))
    near = jnp.where(place == FIRST - 1, low, jnp.where(place == FIRST + ROWS, high, near))
    near = near.astype(bf16)

    def with_sides(z, f, q):
        west = zcol[0, pl.ds(f * STACK + q, 1), :]
        east = zcol[1, pl.ds(f * STACK + q, 1), :]
        z = z + jnp.where(column == 0, jnp.broadcast_to(west, z.shape), 0.0)
        return z + jnp.where(column == COLS - 1, jnp.broadcast_to(east, z.shape), 0.0)

    def activate(f, _):
        at = pl.ds(pl.multiple_of(f * COLS, COLS), COLS)
        rows2[0, f] = silu(with_sides(zrow[0, at], f, 1)).astype(bf16)
        rows2[1, f] = silu(with_sides(zrow[1, at], f, STACK - 2)).astype(bf16)
        rows2[2, f] = silu(with_sides(acc[f, 0:COLS] + zrow[2, at], f, FIRST)).astype(bf16)
        z = acc[f, PIX - COLS : PIX] + zrow[3, at]
        rows2[3, f] = silu(with_sides(z, f, FIRST + ROWS - 1)).astype(bf16)
        return 0

    lax.fori_loop(0, FACES, activate, 0)
    place = lax.rem(lax.broadcasted_iota(i32, (half, C), 0), STACK)
    between = (place > FIRST) & (place < FIRST + ROWS - 1)
    west, east = [
        jnp.where(between, silu(own_line[k] + zcol[k]), 0.0).astype(bf16) for k in range(2)
    ]
    tops, ends = [], []
    for f in range(FACES):
        face = g * FACES + f
        n, s = jnp.where(first, ns[0, face], f), jnp.where(last, ns[1, face], f)
        tops.append(rows2[jnp.where(first, 2 * code[0, face], 0), n])
        ends.append(rows2[jnp.where(last, 1 + 2 * code[1, face], 1), s])
    top, end = [[rows2[k, f] for f in range(FACES)] for k in (2, 3)]
    stacks = (tops + top, top + end, end + ends)
    lines = ([near[0:half], west], [west, east], [near[half : 2 * half], east])
    z_rows, v = [[], [], [], []], []
    for b in range(3):
        y = [tap2(jnp.concatenate(stacks[a] + lines[b], axis=0), a, b) for a in range(3)]
        z_rows[0].append(y[0][0:ROW] + y[1][0:ROW])
        z_rows[1].append(y[0][ROW : 2 * ROW])
        z_rows[2].append(y[2][0:ROW])
        z_rows[3].append(y[1][ROW : 2 * ROW] + y[2][ROW : 2 * ROW])
        v.append([[x[2 * ROW + k * half : 2 * ROW + (k + 1) * half] for x in y] for k in range(2)])
    for k, z in enumerate(z_rows):
        zrow[k] = from_west(z[0]) + z[1] + from_east(z[2])
    z_line[0] = along_rows(*[v[0][0][a] + v[1][0][a] for a in range(3)])
    z_line[1] = along_rows(*v[0][1])
    z_line[2] = along_rows(*v[2][1])
    z_line[3] = along_rows(*[v[2][0][a] + v[1][1][a] for a in range(3)])

    few = lax.broadcasted_iota(i32, (8, C), 0)

    def finish(f, _):
        at = pl.ds(pl.multiple_of(f * COLS, COLS), COLS)
        for i in range(ROWS):
            z = acc2[f, i * COLS : (i + 1) * COLS]
            for k, row in enumerate((0, 1, ROWS - 2, ROWS - 1)):
                if i == row:
                    z = z + zrow[k, at]
            line = [
                jnp.broadcast_to(z_line[k, pl.ds(f * STACK + FIRST + i, 1), :], (8, C)) for k in range(4)
            ]
            west = jnp.where(few == 0, line[0], jnp.where(few == 1, line[1], 0.0))
            east = jnp.where(few == 6, line[2], jnp.where(few == 7, line[3], 0.0))
            feature = jnp.concatenate([z[0:8] + west, z[8 : COLS - 8], z[COLS - 8 :] + east], axis=0)
            p = pf[f, i * COLS : (i + 1) * COLS, 0:C]
            denoised = skip_gain * p + output_gain * feature
            out[f, i] = (p + step_ratio * (p - denoised)).astype(bf16)
        return 0

    lax.fori_loop(0, FACES, finish, 0)
    for copy in sent:
        copy.wait_send()


def on_device(groups, tiles, sample, noise, coarse, w1, b1, w2, b2, ns, we, code):
    C = sample.shape[-1]
    w1 = jnp.swapaxes(w1, 2, 3)
    operands = (sample, noise, coarse, ns.T, we.T, code.T, w1, b1.reshape(1, C), w2, b2.reshape(1, C))
    return pl.pallas_call(
        functools.partial(kernel, groups, tiles),
        out_shape=jax.ShapeDtypeStruct(sample.shape, bf16),
        in_specs=[pl.BlockSpec(memory_space=pltpu.HBM)] * len(operands),
        out_specs=pl.BlockSpec(memory_space=pltpu.VMEM),
        scratch_shapes=[
            (pltpu.SMEM if x.dtype == i32 else pltpu.VMEM)(x.shape, x.dtype) for x in operands
        ]
        + [
            pltpu.VMEM((FACES, PIX, WIDE), f32),
            pltpu.VMEM((FACES, PIX, C), f32),
            pltpu.VMEM((FACES, PIX, C), f32),
            pltpu.VMEM((2, FACES * STACK, C), f32),
            pltpu.VMEM((4, FACES * STACK, C), f32),
            pltpu.VMEM((FACES, PIX + 2 * COLS, WIDE), bf16),
            pltpu.VMEM((FACES, PIX + 2 * COLS, C), bf16),
            pltpu.VMEM((FACES * COLS, WIDE), bf16),
            pltpu.VMEM((3, FACES * COLS, C), f32),
            pltpu.VMEM((groups, BLOCKS, 16, WIDE), bf16),
            pltpu.VMEM((2, 2, 16, WIDE), bf16),
            pltpu.VMEM((4, FACES, 3, COLS, WIDE), bf16),
            pltpu.VMEM((4, FACES, COLS, C), bf16),
            pltpu.VMEM((2, 4 * SIDES * STACK, groups * BLOCKS * 16), bf16),
            pltpu.VMEM((2, FACES * STACK, C), f32),
            pltpu.VMEM((4, FACES * COLS, C), f32),
            pltpu.SemaphoreType.DMA((len(operands),)),
            pltpu.SemaphoreType.DMA((13,)),
            pltpu.SemaphoreType.DMA((13,)),
        ],
        compiler_params=pltpu.CompilerParams(
            collective_id=0, has_side_effects=True, vmem_limit_bytes=32 * 2**20
        ),
    )(*[pltpu.with_memory_space_constraint(x, pltpu.HBM) for x in operands])


def solution(mesh):
    return jax.shard_map(
        functools.partial(on_device, mesh.shape["face"], mesh.shape["tile"]),
        mesh=mesh,
        in_specs=(P("face", "tile", None, None),) * 3 + (P(),) * 7,
        out_specs=P("face", "tile", None, None),
        check_vma=False,
    )
```

```python
import functools

import jax
import jax.numpy as jnp
from jax import lax
from jax.experimental import pallas as pl
from jax.experimental.pallas import tpu as pltpu
from jax.sharding import PartitionSpec as P

MESH = pl.DeviceIdType.MESH
f32 = jnp.float32
bf16 = jnp.bfloat16
i32 = jnp.int32

noise_gain = 0.6
input_gain = 0.7071067811865476
skip_gain = 0.5
output_gain = 0.7071067811865476
step_ratio = -0.4

UP = 8
FACES = 3
ROWS = 8
COLS = 32
COARSE = COLS // UP
PIX = ROWS * COLS
SIDES = 2 * FACES
WIDE = 256

BLOCKS = 6
FACE, OVER, UNDER = 1, 4, 5
LINE = 384
CORNER = 4 * FACES
STACK = 16
FIRST = 4


def dot(a, b):
    return jnp.dot(a, b, preferred_element_type=f32)


def dot_t(a, b):
    return lax.dot_general(a, b, (((1,), (1,)), ((), ())), preferred_element_type=f32)


def column_of(shape):
    return lax.rem(lax.broadcasted_iota(i32, shape, 0), COLS)


def from_west(z):
    return jnp.where(column_of(z.shape) == 0, 0.0, pltpu.roll(z, 1, 0))


def from_east(z):
    return jnp.where(column_of(z.shape) == COLS - 1, 0.0, pltpu.roll(z, z.shape[0] - 1, 0))


def along_rows(v0, v1, v2):
    return pltpu.roll(v0, 1, 0) + v1 + pltpu.roll(v2, v2.shape[0] - 1, 0)


def silu(u):
    return u / (1.0 + jnp.exp(-u))


def spread(rows, count):
    width = rows[0][1].shape[1]
    place = lax.broadcasted_iota(i32, (count, width), 0)
    out = jnp.zeros((count, width), f32)
    for at, row in rows:
        out = jnp.where(place == at, jnp.broadcast_to(row, (count, width)), out)
    return out


def pack(outer, inner):
    rest = outer[:, 128:WIDE] + pltpu.roll(inner[:, 128:WIDE], 64, 1)
    return jnp.concatenate([outer[:, 0:128], rest, inner[:, 0:128]], axis=1).astype(bf16)


def unpack_outer(y):
    lane = lax.broadcasted_iota(i32, y.shape, 1)
    return jnp.where(lane < LINE // 2, y, 0.0)


def unpack_inner(y):
    return unpack_outer(jnp.concatenate([y[:, 128:], pltpu.roll(y[:, 0:128], 64, 1)], axis=1))


def kernel(
    groups,
    tiles,
    sample_hbm,
    noise_hbm,
    coarse_hbm,
    ns_hbm,
    we_hbm,
    code_hbm,
    w1_hbm,
    b1_hbm,
    w2_hbm,
    b2_hbm,
    out,
    sample,
    noise,
    coarse,
    ns,
    we,
    code,
    w1,
    b1,
    w2,
    b2,
    pf,
    acc,
    acc2,
    own_line,
    z_line,
    xp,
    hp,
    up,
    cclass,
    cols,
    corner,
    rows1,
    rows2,
    pick,
    zcol,
    zrow,
    load_sem,
    send_sem,
    recv_sem,
):
    g = lax.axis_index("face")
    t = lax.axis_index("tile")
    above = lax.rem(t + tiles - 1, tiles)
    below = lax.rem(t + 1, tiles)
    first = t == 0
    last = t == tiles - 1
    C = acc.shape[2]
    lines = groups * BLOCKS * 16

    barrier = pltpu.get_barrier_semaphore()
    for d in (2, 1, 3, 0):
        for k, there in enumerate((t, above, below)):
            if d or k:
                pl.semaphore_signal(
                    barrier, inc=1, device_id=(lax.rem(g + d, groups), there), device_id_type=MESH
                )

    loads = [
        pltpu.make_async_copy(src, dst, load_sem.at[i])
        for i, (src, dst) in enumerate(
            [
                (sample_hbm, sample),
                (noise_hbm, noise),
                (coarse_hbm, coarse),
                (ns_hbm, ns),
                (we_hbm, we),
                (code_hbm, code),
                (w1_hbm, w1),
                (b1_hbm, b1),
                (w2_hbm, w2),
                (b2_hbm, b2),
            ]
        )
    ]
    for copy in loads[:6]:
        copy.start()

    for f in range(FACES):
        zero_row = jnp.zeros((COLS, WIDE), bf16)
        xp[f, 0:COLS] = zero_row
        xp[f, COLS + PIX : 2 * COLS + PIX] = zero_row
        xp[f, COLS : COLS + PIX, 128:WIDE] = jnp.zeros((PIX, WIDE - 128), bf16)
        pf[f, :, 128:WIDE] = jnp.zeros((PIX, WIDE - 128), f32)
        hp[f, 0 : 2 * COLS] = jnp.zeros((2 * COLS, C), bf16)
        hp[f, PIX : PIX + 2 * COLS] = jnp.zeros((2 * COLS, C), bf16)

    for copy in loads[:3]:
        copy.wait()
    for f in range(FACES):
        p = sample[f].astype(f32) + noise_gain * noise[f].astype(f32)
        p = p.reshape(PIX, C)
        pf[f, :, 0:C] = p
        xp[f, COLS : COLS + PIX, 0:C] = (p * input_gain).astype(bf16)
        for r in range(2):
            rows1[2, f, r] = xp[f, (1 + r) * COLS : (2 + r) * COLS]
            rows1[3, f, r] = xp[f, PIX - COLS + r * COLS : PIX + r * COLS]
    raw, tops, ends = [([], []) for _ in range(3)]
    blank = jnp.zeros((COARSE, WIDE - C), f32)
    for f in range(FACES):
        c = coarse[f, 0].astype(f32)
        line = jnp.concatenate([c, blank], axis=1)
        c = jnp.concatenate([blank, c], axis=1)
        each = [c[j : j + 1] for j in range(COARSE)]
        wide = jnp.concatenate([jnp.broadcast_to(e, (UP, WIDE)) for e in each], axis=0).astype(bf16)
        up[f * COLS : (f + 1) * COLS] = wide
        rows1[2, f, 2] = wide
        rows1[3, f, 2] = wide
        for inner, j in ((0, 0), (1, COARSE - 1)):
            raw[inner].append((f, line[j : j + 1]))
            tops[inner].append((CORNER + f, line[j : j + 1]))
            ends[inner].append((CORNER + f, line[j : j + 1]))
        halves = ([], [])
        for inner, high, j in ((0, 0, 0), (0, 1, COLS - 1), (1, 0, 1), (1, 1, COLS - 2)):
            line_j = [pf[f, i * COLS + j : i * COLS + j + 1, :] * input_gain for i in range(ROWS)]
            halves[inner].append(spread(list(enumerate(line_j)), ROWS))
            tops[inner].extend((4 * f + 2 * high + r, line_j[r]) for r in range(2))
            ends[inner].extend((4 * f + 2 * high + r, line_j[ROWS - 2 + r]) for r in range(2))
        cols[g, FACE + f] = pack(*[jnp.concatenate(h, axis=0) for h in halves])
    cols[g, 0] = pack(*[spread(x, 16) for x in raw])
    corner[0] = pack(*[spread(x, 16) for x in tops])
    corner[1] = pack(*[spread(x, 16) for x in ends])

    sent = []

    def add(src, dst, there):
        n = len(sent)
        sent.append(
            pltpu.make_async_remote_copy(
                src_ref=src,
                dst_ref=dst,
                send_sem=send_sem.at[n],
                recv_sem=recv_sem.at[n],
                device_id=there,
                device_id_type=MESH,
            )
        )

    table = cols.at[g, pl.ds(0, OVER)]
    over = cols.at[g, OVER]
    under = cols.at[g, UNDER]
    for d in (2, 1, 3):
        far = lax.rem(g + d, groups)
        add(corner.at[0], under, (far, above))
        add(corner.at[1], over, (far, below))
        add(table, table, (far, t))
    add(corner.at[0], under, (g, above))
    add(corner.at[1], over, (g, below))
    add(rows1.at[2], rows1.at[1], (g, above))
    add(rows1.at[3], rows1.at[0], (g, below))

    pl.semaphore_wait(barrier, 3 * groups - 1)
    for copy in sent:
        copy.start()
    for copy in loads[6:]:
        copy.start()
    for copy in loads[3:6]:
        copy.wait()

    lane = lax.broadcasted_iota(i32, (STACK, lines), 1)
    place = lax.broadcasted_iota(i32, (STACK, lines), 0)

    def split(face):
        group = sum((face >= FACES * k).astype(i32) for k in range(1, groups))
        return group, face - FACES * group

    def across(face, side):
        edge = code[2 + side, face]
        return we[side, face], 3 * jnp.where(side == 1, edge, 1 - edge)

    def write_pick(at, face, column, beyond):
        group, f = split(face)
        base = group * (BLOCKS * 16)
        inner = (column == 1) | (column == 2)
        high = (column >= 2).astype(i32)

        def line(ff, row):
            if row < 0:
                return base + OVER * 16 + ff * 4 + high * 2 + 2 + row
            if row >= ROWS:
                return base + UNDER * 16 + ff * 4 + high * 2 + row - ROWS
            return base + (FACE + ff) * 16 + high * 8 + row

        def condition(ff, row):
            if row < 0:
                return base + OVER * 16 + CORNER + ff
            if row >= ROWS:
                return base + UNDER * 16 + CORNER + ff
            return base + ff

        n, s = ns[0, face], ns[1, face]
        flip_n, flip_s = code[0, face] == 1, code[1, face] == 1
        for part, where in enumerate((line, condition)):
            north = jnp.where(beyond, -1, jnp.where(flip_n, where(n, 0), where(n, -1)))
            south = jnp.where(beyond, -1, jnp.where(flip_s, where(s, ROWS - 1), where(s, ROWS)))
            target = jnp.broadcast_to(where(f, 0), place.shape)
            if part == 0:
                target = target + place - FIRST
            for q, value in (
                (0, where(f, -2)),
                (1, where(f, -1)),
                (2, jnp.where(first, -1, where(f, 0))),
                (3, jnp.where(first, north, where(f, -1))),
                (12, jnp.where(last, south, where(f, ROWS))),
                (13, jnp.where(last, -1, where(f, ROWS - 1))),
                (14, where(f, ROWS)),
                (15, where(f, ROWS + 1)),
            ):
                target = jnp.where(place == q, value, target)
            at = pl.multiple_of(at, STACK)
            second = high == 1 if part else inner
            for k, chosen in ((0, jnp.where(second, -1, target)), (1, jnp.where(second, target, -1))):
                pick[part, k, pl.ds(at, STACK), :] = jnp.where(lane == chosen, 1.0, 0.0).astype(bf16)

    def pick_side(n, _):
        side = (n >= FACES).astype(i32)
        face = g * FACES + n - FACES * side
        near, column = across(face, side)
        west_face, west_column = across(near, 0)
        east_face, east_column = across(near, 1)
        at_west = column == 0
        at_east = column == 3
        write_pick(n * STACK, near, column, True)
        write_pick(
            (2 * SIDES + n) * STACK,
            jnp.where(at_west, west_face, near),
            jnp.where(at_west, west_column, 2),
            at_west,
        )
        write_pick((SIDES + n) * STACK, near, column, False)
        write_pick(
            (3 * SIDES + n) * STACK,
            jnp.where(at_east, east_face, near),
            jnp.where(at_east, east_column, 1),
            at_east,
        )
        return 0

    lax.fori_loop(0, SIDES, pick_side, 0)

    def tap1(x, a, b):
        return dot_t(x, w1[a, b, :, 0:WIDE])

    def tap1_coarse(x, a, b):
        return dot_t(x, w1[a, b, :, w1.shape[3] - WIDE :])

    def tap2(x, a, b):
        return dot(x, w2[a, b])

    def conv_own(src, tap, f, b):
        z = tap(src[f, 0:PIX], 0, b)
        z = z + tap(src[f, COLS : COLS + PIX], 1, b)
        return z + tap(src[f, 2 * COLS : 2 * COLS + PIX], 2, b)

    for copy in loads[6:]:
        copy.wait()
    parts = []
    for b in range(3):
        c0, c1, c2 = [tap1_coarse(up[...], a, b) for a in range(3)]
        parts.append((c1 + c2, c0 + c1 + c2, c0 + c1))
    for k in range(3):
        cclass[k] = from_west(parts[0][k]) + parts[1][k] + from_east(parts[2][k]) + b1[...]

    def own1(f, _):
        z = from_west(conv_own(xp, tap1, f, 0)) + conv_own(xp, tap1, f, 1) + from_east(conv_own(xp, tap1, f, 2))
        at = pl.ds(pl.multiple_of(f * COLS, COLS), COLS)
        for i in range(ROWS):
            k = 0 if i == 0 else 2 if i == ROWS - 1 else 1
            acc[f, i * COLS : (i + 1) * COLS] = z[i * COLS : (i + 1) * COLS] + cclass[k, at]
        return 0

    lax.fori_loop(0, FACES, own1, 0)

    column = column_of((COLS, C))
    border = (column == 0) | (column == COLS - 1)

    def inside(f, _):
        for i in range(1, ROWS - 1):
            h = silu(acc[f, i * COLS : (i + 1) * COLS])
            hp[f, (i + 1) * COLS : (i + 2) * COLS] = jnp.where(border, 0.0, h).astype(bf16)
        return 0

    lax.fori_loop(0, FACES, inside, 0)

    def own2(f, _):
        z = from_west(conv_own(hp, tap2, f, 0)) + conv_own(hp, tap2, f, 1) + from_east(conv_own(hp, tap2, f, 2))
        acc2[f] = z + b2[...]
        return 0

    lax.fori_loop(0, FACES, own2, 0)
    for k, j in ((0, 0), (1, COLS - 1)):
        for f in range(FACES):
            line = [(FIRST + i, acc[f, i * COLS + j : i * COLS + j + 1, :]) for i in range(1, ROWS - 1)]
            own_line[k, f * STACK : (f + 1) * STACK] = spread(line, STACK)

    for copy in sent[-2:]:
        copy.wait_recv()

    tops, ends, after, before = [], [], [], []
    for f in range(FACES):
        face = g * FACES + f
        n, s = jnp.where(first, ns[0, face], f), jnp.where(last, ns[1, face], f)
        flip_n, flip_s = code[0, face], code[1, face]
        k = jnp.where(first, 2 * flip_n, 0)
        r = jnp.where(k == 0, 1, 0)
        tops.append((rows1[k, n, r], rows1[k, n, 2]))
        k = jnp.where(last, 1 + 2 * flip_s, 1)
        r = jnp.where(k == 1, 0, 1)
        ends.append((rows1[k, s, r], rows1[k, s, 2]))
        s = jnp.where(first, ns[1, face], f)
        k = jnp.where(first, 2 - 2 * flip_s, 2)
        r = jnp.where(k == 0, 1, 0)
        after.append((rows1[k, s, r], rows1[k, s, 2]))
        n = jnp.where(last, ns[0, face], f)
        k = jnp.where(last, 3 - 2 * flip_n, 3)
        r = jnp.where(k == 1, 0, 1)
        before.append((rows1[k, n, r], rows1[k, n, 2]))

    def landed(k, r):
        return [(rows1[k, f, r], rows1[k, f, 2]) for f in range(FACES)]

    ROW = FACES * COLS
    stacks = (
        landed(0, 0) + tops + before,
        landed(0, 1) + landed(1, 0),
        after + landed(1, 1) + ends,
    )
    taps = (tap1, tap1_coarse)
    z_rows = [[], [], [], []]
    for b in range(3):
        y = [
            sum(tap(jnp.concatenate([r[k] for r in stacks[a]], axis=0), a, b) for k, tap in enumerate(taps))
            for a in range(3)
        ]
        z_rows[0].append(y[0][0:ROW] + y[1][0:ROW] + y[2][0:ROW])
        z_rows[1].append(y[0][2 * ROW :] + y[1][ROW:] + y[2][ROW : 2 * ROW])
        z_rows[2].append(y[0][ROW : 2 * ROW])
        z_rows[3].append(y[2][2 * ROW :])
    for k, z in enumerate(z_rows):
        z = from_west(z[0]) + z[1] + from_east(z[2])
        zrow[k] = z if k >= 2 else z + b1[...]

    for copy in sent[:-2]:
        copy.wait_recv()
    table = cols[...].reshape(lines, LINE)
    half = FACES * STACK
    sides = SIDES * STACK
    y = unpack_outer(dot(pick[0, 0], table[:, 0:WIDE]))
    z = unpack_inner(dot(pick[0, 1, 2 * sides :], table[:, LINE - WIDE :]))
    picked = [jnp.concatenate([y[0 : 2 * sides], y[2 * sides :] + z], axis=0).astype(bf16)]
    y = unpack_outer(dot(pick[1, 0], table[:, 0:WIDE]))
    z = unpack_inner(dot(pick[1, 1], table[:, LINE - WIDE :]))
    picked.append(pltpu.roll(y + z, 64, 1).astype(bf16))

    v_side, v_near = [], []
    for b in range(3):
        lines_b = []
        for chosen in picked:
            if b == 0:
                beside = [chosen[0:half], chosen[2 * sides : 3 * sides]]
            elif b == 1:
                beside = [chosen[sides : 2 * sides]]
            else:
                beside = [chosen[half : 2 * half], chosen[3 * sides :]]
            lines_b.append(jnp.concatenate(beside, axis=0))
        y = [sum(tap(x, a, b) for tap, x in zip(taps, lines_b)) for a in range(3)]
        if b != 1:
            v_side.append([x[0:half] for x in y])
            y = [x[half:] for x in y]
        v_near.append(y)
    for k in range(2):
        zcol[k] = along_rows(*v_side[k])
    near = along_rows(*[v_near[0][a] + v_near[1][a] + v_near[2][a] for a in range(3)]) + b1[...]
    near = silu(near)
    place = lax.rem(lax.broadcasted_iota(i32, near.shape, 0), STACK)
    low = jnp.where(first, 0.0, pltpu.roll(near, 2, 0))
    high = jnp.where(last, 0.0, pltpu.roll(near, near.shape[0] - 2, 0))
    near = jnp.where(place == FIRST - 1, low, jnp.where(place == FIRST + ROWS, high, near))
    near = near.astype(bf16)

    def with_sides(z, f, q):
        west = zcol[0, pl.ds(f * STACK + q, 1), :]
        east = zcol[1, pl.ds(f * STACK + q, 1), :]
        z = z + jnp.where(column == 0, jnp.broadcast_to(west, z.shape), 0.0)
        return z + jnp.where(column == COLS - 1, jnp.broadcast_to(east, z.shape), 0.0)

    def activate(f, _):
        at = pl.ds(pl.multiple_of(f * COLS, COLS), COLS)
        rows2[0, f] = silu(with_sides(zrow[0, at], f, 1)).astype(bf16)
        rows2[1, f] = silu(with_sides(zrow[1, at], f, STACK - 2)).astype(bf16)
        rows2[2, f] = silu(with_sides(acc[f, 0:COLS] + zrow[2, at], f, FIRST)).astype(bf16)
        z = acc[f, PIX - COLS : PIX] + zrow[3, at]
        rows2[3, f] = silu(with_sides(z, f, FIRST + ROWS - 1)).astype(bf16)
        return 0

    lax.fori_loop(0, FACES, activate, 0)
    place = lax.rem(lax.broadcasted_iota(i32, (half, C), 0), STACK)
    between = (place > FIRST) & (place < FIRST + ROWS - 1)
    west, east = [
        jnp.where(between, silu(own_line[k] + zcol[k]), 0.0).astype(bf16) for k in range(2)
    ]
    tops, ends = [], []
    for f in range(FACES):
        face = g * FACES + f
        n, s = jnp.where(first, ns[0, face], f), jnp.where(last, ns[1, face], f)
        tops.append(rows2[jnp.where(first, 2 * code[0, face], 0), n])
        ends.append(rows2[jnp.where(last, 1 + 2 * code[1, face], 1), s])
    top, end = [[rows2[k, f] for f in range(FACES)] for k in (2, 3)]
    stacks = (tops + top, top + end, end + ends)
    lines = ([near[0:half], west], [west, east], [near[half : 2 * half], east])
    z_rows, v = [[], [], [], []], []
    for b in range(3):
        y = [tap2(jnp.concatenate(stacks[a] + lines[b], axis=0), a, b) for a in range(3)]
        z_rows[0].append(y[0][0:ROW] + y[1][0:ROW])
        z_rows[1].append(y[0][ROW : 2 * ROW])
        z_rows[2].append(y[2][0:ROW])
        z_rows[3].append(y[1][ROW : 2 * ROW] + y[2][ROW : 2 * ROW])
        v.append([[x[2 * ROW + k * half : 2 * ROW + (k + 1) * half] for x in y] for k in range(2)])
    for k, z in enumerate(z_rows):
        zrow[k] = from_west(z[0]) + z[1] + from_east(z[2])
    z_line[0] = along_rows(*[v[0][0][a] + v[1][0][a] for a in range(3)])
    z_line[1] = along_rows(*v[0][1])
    z_line[2] = along_rows(*v[2][1])
    z_line[3] = along_rows(*[v[2][0][a] + v[1][1][a] for a in range(3)])

    few = lax.broadcasted_iota(i32, (8, C), 0)

    def finish(f, _):
        at = pl.ds(pl.multiple_of(f * COLS, COLS), COLS)
        for i in range(ROWS):
            z = acc2[f, i * COLS : (i + 1) * COLS]
            for k, row in enumerate((0, 1, ROWS - 2, ROWS - 1)):
                if i == row:
                    z = z + zrow[k, at]
            line = [
                jnp.broadcast_to(z_line[k, pl.ds(f * STACK + FIRST + i, 1), :], (8, C)) for k in range(4)
            ]
            west = jnp.where(few == 0, line[0], jnp.where(few == 1, line[1], 0.0))
            east = jnp.where(few == 6, line[2], jnp.where(few == 7, line[3], 0.0))
            feature = jnp.concatenate([z[0:8] + west, z[8 : COLS - 8], z[COLS - 8 :] + east], axis=0)
            p = pf[f, i * COLS : (i + 1) * COLS, 0:C]
            denoised = skip_gain * p + output_gain * feature
            out[f, i] = (p + step_ratio * (p - denoised)).astype(bf16)
        return 0

    lax.fori_loop(0, FACES, finish, 0)
    for copy in sent:
        copy.wait_send()


def on_device(groups, tiles, sample, noise, coarse, w1, b1, w2, b2, ns, we, code):
    C = sample.shape[-1]
    w1 = jnp.swapaxes(w1, 2, 3)
    operands = (sample, noise, coarse, ns.T, we.T, code.T, w1, b1.reshape(1, C), w2, b2.reshape(1, C))
    return pl.pallas_call(
        functools.partial(kernel, groups, tiles),
        out_shape=jax.ShapeDtypeStruct(sample.shape, bf16),
        in_specs=[pl.BlockSpec(memory_space=pltpu.HBM)] * len(operands),
        out_specs=pl.BlockSpec(memory_space=pltpu.VMEM),
        scratch_shapes=[
            (pltpu.SMEM if x.dtype == i32 else pltpu.VMEM)(x.shape, x.dtype) for x in operands
        ]
        + [
            pltpu.VMEM((FACES, PIX, WIDE), f32),
            pltpu.VMEM((FACES, PIX, C), f32),
            pltpu.VMEM((FACES, PIX, C), f32),
            pltpu.VMEM((2, FACES * STACK, C), f32),
            pltpu.VMEM((4, FACES * STACK, C), f32),
            pltpu.VMEM((FACES, PIX + 2 * COLS, WIDE), bf16),
            pltpu.VMEM((FACES, PIX + 2 * COLS, C), bf16),
            pltpu.VMEM((FACES * COLS, WIDE), bf16),
            pltpu.VMEM((3, FACES * COLS, C), f32),
            pltpu.VMEM((groups, BLOCKS, 16, LINE), bf16),
            pltpu.VMEM((2, 16, LINE), bf16),
            pltpu.VMEM((4, FACES, 3, COLS, WIDE), bf16),
            pltpu.VMEM((4, FACES, COLS, C), bf16),
            pltpu.VMEM((2, 2, 4 * SIDES * STACK, groups * BLOCKS * 16), bf16),
            pltpu.VMEM((2, FACES * STACK, C), f32),
            pltpu.VMEM((4, FACES * COLS, C), f32),
            pltpu.SemaphoreType.DMA((len(operands),)),
            pltpu.SemaphoreType.DMA((13,)),
            pltpu.SemaphoreType.DMA((13,)),
        ],
        compiler_params=pltpu.CompilerParams(
            collective_id=0, has_side_effects=True, vmem_limit_bytes=32 * 2**20
        ),
    )(*[pltpu.with_memory_space_constraint(x, pltpu.HBM) for x in operands])


def solution(mesh):
    return jax.shard_map(
        functools.partial(on_device, mesh.shape["face"], mesh.shape["tile"]),
        mesh=mesh,
        in_specs=(P("face", "tile", None, None),) * 3 + (P(),) * 7,
        out_specs=P("face", "tile", None, None),
        check_vma=False,
    )
```

```python
import functools

import jax
import jax.numpy as jnp
from jax import lax
from jax.experimental import pallas as pl
from jax.experimental.pallas import tpu as pltpu
from jax.sharding import PartitionSpec as P

MESH = pl.DeviceIdType.MESH
f32 = jnp.float32
bf16 = jnp.bfloat16
i32 = jnp.int32

noise_gain = 0.6
input_gain = 0.7071067811865476
skip_gain = 0.5
output_gain = 0.7071067811865476
step_ratio = -0.4
feature_gain = -step_ratio * output_gain

UP = 8
FACES = 3
ROWS = 8
COLS = 32
COARSE = COLS // UP
PIX = ROWS * COLS
SIDES = 2 * FACES
WIDE = 256

BLOCKS = 6
FACE, OVER, UNDER = 1, 4, 5
LINE = 384
CORNER = 4 * FACES
STACK = 16
FIRST = 4


def dot(a, b):
    return jnp.dot(a, b, preferred_element_type=f32)


def dot_t(a, b):
    return lax.dot_general(a, b, (((1,), (1,)), ((), ())), preferred_element_type=f32)


def column_of(shape):
    return lax.rem(lax.broadcasted_iota(i32, shape, 0), COLS)


def from_west(z):
    return jnp.where(column_of(z.shape) == 0, 0.0, pltpu.roll(z, 1, 0))


def from_east(z):
    return jnp.where(column_of(z.shape) == COLS - 1, 0.0, pltpu.roll(z, z.shape[0] - 1, 0))


def along_rows(v0, v1, v2):
    return pltpu.roll(v0, 1, 0) + v1 + pltpu.roll(v2, v2.shape[0] - 1, 0)


def silu(u):
    return u / (1.0 + jnp.exp(-u))


def spread(rows, count):
    width = rows[0][1].shape[1]
    place = lax.broadcasted_iota(i32, (count, width), 0)
    out = jnp.zeros((count, width), f32)
    for at, row in rows:
        out = jnp.where(place == at, jnp.broadcast_to(row, (count, width)), out)
    return out


def pack(outer, inner):
    rest = outer[:, 128:WIDE] + pltpu.roll(inner[:, 128:WIDE], 64, 1)
    return jnp.concatenate([outer[:, 0:128], rest, inner[:, 0:128]], axis=1).astype(bf16)


def unpack_outer(y):
    lane = lax.broadcasted_iota(i32, y.shape, 1)
    return jnp.where(lane < LINE // 2, y, 0.0)


def unpack_inner(y):
    return unpack_outer(jnp.concatenate([y[:, 128:], pltpu.roll(y[:, 0:128], 64, 1)], axis=1))


def kernel(
    groups,
    tiles,
    sample_hbm,
    noise_hbm,
    coarse_hbm,
    ns_hbm,
    we_hbm,
    code_hbm,
    w1_hbm,
    b1_hbm,
    w2_hbm,
    b2_hbm,
    out,
    sample,
    noise,
    coarse,
    ns,
    we,
    code,
    w1,
    b1,
    w2,
    b2,
    pf,
    acc,
    acc2,
    own_line,
    z_line,
    xp,
    hp,
    up,
    cclass,
    cols,
    corner,
    rows1,
    rows2,
    pick,
    zcol,
    zrow,
    load_sem,
    send_sem,
    recv_sem,
):
    g = lax.axis_index("face")
    t = lax.axis_index("tile")
    above = lax.rem(t + tiles - 1, tiles)
    below = lax.rem(t + 1, tiles)
    first = t == 0
    last = t == tiles - 1
    C = acc.shape[2]
    lines = groups * BLOCKS * 16

    barrier = pltpu.get_barrier_semaphore()
    for d in (2, 1, 3, 0):
        for k, there in enumerate((t, above, below)):
            if d or k:
                pl.semaphore_signal(
                    barrier, inc=1, device_id=(lax.rem(g + d, groups), there), device_id_type=MESH
                )

    loads = [
        pltpu.make_async_copy(src, dst, load_sem.at[i])
        for i, (src, dst) in enumerate(
            [
                (sample_hbm, sample),
                (noise_hbm, noise),
                (coarse_hbm, coarse),
                (ns_hbm, ns),
                (we_hbm, we),
                (code_hbm, code),
                (w1_hbm, w1),
                (b1_hbm, b1),
                (w2_hbm, w2),
                (b2_hbm, b2),
            ]
        )
    ]
    for copy in loads[:6]:
        copy.start()

    for f in range(FACES):
        zero_row = jnp.zeros((COLS, WIDE), bf16)
        xp[f, 0:COLS] = zero_row
        xp[f, COLS + PIX : 2 * COLS + PIX] = zero_row
        xp[f, COLS : COLS + PIX, 128:WIDE] = jnp.zeros((PIX, WIDE - 128), bf16)
        pf[f, :, 128:WIDE] = jnp.zeros((PIX, WIDE - 128), f32)
        hp[f, 0 : 2 * COLS] = jnp.zeros((2 * COLS, C), bf16)
        hp[f, PIX : PIX + 2 * COLS] = jnp.zeros((2 * COLS, C), bf16)

    for copy in loads[:3]:
        copy.wait()
    for f in range(FACES):
        p = sample[f].astype(f32) + noise_gain * noise[f].astype(f32)
        p = p.reshape(PIX, C)
        pf[f, :, 0:C] = p
        xp[f, COLS : COLS + PIX, 0:C] = (p * input_gain).astype(bf16)
        for r in range(2):
            rows1[2, f, r] = xp[f, (1 + r) * COLS : (2 + r) * COLS]
            rows1[3, f, r] = xp[f, PIX - COLS + r * COLS : PIX + r * COLS]
    raw, tops, ends = [([], []) for _ in range(3)]
    blank = jnp.zeros((COARSE, WIDE - C), f32)
    for f in range(FACES):
        c = coarse[f, 0].astype(f32)
        line = jnp.concatenate([c, blank], axis=1)
        c = jnp.concatenate([blank, c], axis=1)
        each = [c[j : j + 1] for j in range(COARSE)]
        wide = jnp.concatenate([jnp.broadcast_to(e, (UP, WIDE)) for e in each], axis=0).astype(bf16)
        up[f * COLS : (f + 1) * COLS] = wide
        rows1[2, f, 2] = wide
        rows1[3, f, 2] = wide
        for inner, j in ((0, 0), (1, COARSE - 1)):
            raw[inner].append((f, line[j : j + 1]))
            tops[inner].append((CORNER + f, line[j : j + 1]))
            ends[inner].append((CORNER + f, line[j : j + 1]))
        halves = ([], [])
        for inner, high, j in ((0, 0, 0), (0, 1, COLS - 1), (1, 0, 1), (1, 1, COLS - 2)):
            line_j = [pf[f, i * COLS + j : i * COLS + j + 1, :] * input_gain for i in range(ROWS)]
            halves[inner].append(spread(list(enumerate(line_j)), ROWS))
            tops[inner].extend((4 * f + 2 * high + r, line_j[r]) for r in range(2))
            ends[inner].extend((4 * f + 2 * high + r, line_j[ROWS - 2 + r]) for r in range(2))
        cols[g, FACE + f] = pack(*[jnp.concatenate(h, axis=0) for h in halves])
    cols[g, 0] = pack(*[spread(x, 16) for x in raw])
    corner[0] = pack(*[spread(x, 16) for x in tops])
    corner[1] = pack(*[spread(x, 16) for x in ends])

    sent = []

    def add(src, dst, there):
        n = len(sent)
        sent.append(
            pltpu.make_async_remote_copy(
                src_ref=src,
                dst_ref=dst,
                send_sem=send_sem.at[n],
                recv_sem=recv_sem.at[n],
                device_id=there,
                device_id_type=MESH,
            )
        )

    table = cols.at[g, pl.ds(0, OVER)]
    over = cols.at[g, OVER]
    under = cols.at[g, UNDER]
    for d in (2, 1, 3):
        far = lax.rem(g + d, groups)
        add(corner.at[0], under, (far, above))
        add(corner.at[1], over, (far, below))
        add(table, table, (far, t))
    add(corner.at[0], under, (g, above))
    add(corner.at[1], over, (g, below))
    add(rows1.at[2], rows1.at[1], (g, above))
    add(rows1.at[3], rows1.at[0], (g, below))

    pl.semaphore_wait(barrier, 3 * groups - 1)
    for copy in sent:
        copy.start()
    for copy in loads[6:]:
        copy.start()
    for copy in loads[3:6]:
        copy.wait()

    lane = lax.broadcasted_iota(i32, (STACK, lines), 1)
    place = lax.broadcasted_iota(i32, (STACK, lines), 0)

    def split(face):
        group = sum((face >= FACES * k).astype(i32) for k in range(1, groups))
        return group, face - FACES * group

    def across(face, side):
        edge = code[2 + side, face]
        return we[side, face], 3 * jnp.where(side == 1, edge, 1 - edge)

    def write_pick(at, face, column, beyond):
        group, f = split(face)
        base = group * (BLOCKS * 16)
        inner = (column == 1) | (column == 2)
        high = (column >= 2).astype(i32)

        def line(ff, row):
            if row < 0:
                return base + OVER * 16 + ff * 4 + high * 2 + 2 + row
            if row >= ROWS:
                return base + UNDER * 16 + ff * 4 + high * 2 + row - ROWS
            return base + (FACE + ff) * 16 + high * 8 + row

        def condition(ff, row):
            if row < 0:
                return base + OVER * 16 + CORNER + ff
            if row >= ROWS:
                return base + UNDER * 16 + CORNER + ff
            return base + ff

        n, s = ns[0, face], ns[1, face]
        flip_n, flip_s = code[0, face] == 1, code[1, face] == 1
        for part, where in enumerate((line, condition)):
            north = jnp.where(beyond, -1, jnp.where(flip_n, where(n, 0), where(n, -1)))
            south = jnp.where(beyond, -1, jnp.where(flip_s, where(s, ROWS - 1), where(s, ROWS)))
            target = jnp.broadcast_to(where(f, 0), place.shape)
            if part == 0:
                target = target + place - FIRST
            for q, value in (
                (0, where(f, -2)),
                (1, where(f, -1)),
                (2, jnp.where(first, -1, where(f, 0))),
                (3, jnp.where(first, north, where(f, -1))),
                (12, jnp.where(last, south, where(f, ROWS))),
                (13, jnp.where(last, -1, where(f, ROWS - 1))),
                (14, where(f, ROWS)),
                (15, where(f, ROWS + 1)),
            ):
                target = jnp.where(place == q, value, target)
            at = pl.multiple_of(at, STACK)
            second = high == 1 if part else inner
            for k, chosen in ((0, jnp.where(second, -1, target)), (1, jnp.where(second, target, -1))):
                pick[part, k, pl.ds(at, STACK), :] = jnp.where(lane == chosen, 1.0, 0.0).astype(bf16)

    def pick_side(n, _):
        side = (n >= FACES).astype(i32)
        face = g * FACES + n - FACES * side
        near, column = across(face, side)
        west_face, west_column = across(near, 0)
        east_face, east_column = across(near, 1)
        at_west = column == 0
        at_east = column == 3
        write_pick(n * STACK, near, column, True)
        write_pick(
            (2 * SIDES + n) * STACK,
            jnp.where(at_west, west_face, near),
            jnp.where(at_west, west_column, 2),
            at_west,
        )
        write_pick((SIDES + n) * STACK, near, column, False)
        write_pick(
            (3 * SIDES + n) * STACK,
            jnp.where(at_east, east_face, near),
            jnp.where(at_east, east_column, 1),
            at_east,
        )
        return 0

    lax.fori_loop(0, SIDES, pick_side, 0)

    def tap1(x, a, b):
        return dot_t(x, w1[a, b, :, 0:WIDE])

    def tap1_coarse(x, a, b):
        return dot_t(x, w1[a, b, :, w1.shape[3] - WIDE :])

    def tap2(x, a, b):
        return dot(x, w2[a, b])

    def conv_own(src, tap, f, b):
        z = tap(src[f, 0:PIX], 0, b)
        z = z + tap(src[f, COLS : COLS + PIX], 1, b)
        return z + tap(src[f, 2 * COLS : 2 * COLS + PIX], 2, b)

    for copy in loads[6:]:
        copy.wait()
    parts = []
    for b in range(3):
        c0, c1, c2 = [tap1_coarse(up[...], a, b) for a in range(3)]
        parts.append((c1 + c2, c0 + c1 + c2, c0 + c1))
    for k in range(3):
        cclass[k] = from_west(parts[0][k]) + parts[1][k] + from_east(parts[2][k]) + b1[...]

    def own1(f, _):
        z = from_west(conv_own(xp, tap1, f, 0)) + conv_own(xp, tap1, f, 1) + from_east(conv_own(xp, tap1, f, 2))
        at = pl.ds(pl.multiple_of(f * COLS, COLS), COLS)
        for i in range(ROWS):
            k = 0 if i == 0 else 2 if i == ROWS - 1 else 1
            acc[f, i * COLS : (i + 1) * COLS] = z[i * COLS : (i + 1) * COLS] + cclass[k, at]
        return 0

    lax.fori_loop(0, FACES, own1, 0)

    column = column_of((COLS, C))
    border = (column == 0) | (column == COLS - 1)

    def inside(f, _):
        for i in range(1, ROWS - 1):
            h = silu(acc[f, i * COLS : (i + 1) * COLS])
            hp[f, (i + 1) * COLS : (i + 2) * COLS] = jnp.where(border, 0.0, h).astype(bf16)
        return 0

    lax.fori_loop(0, FACES, inside, 0)

    def own2(f, _):
        z = from_west(conv_own(hp, tap2, f, 0)) + conv_own(hp, tap2, f, 1) + from_east(conv_own(hp, tap2, f, 2))
        p = pf[f, :, 0:C]
        denoised = skip_gain * p + output_gain * (z + b2[...])
        z = p + step_ratio * (p - denoised)
        acc2[f] = z
        for i in range(2, ROWS - 2):
            out[f, i] = z[i * COLS : (i + 1) * COLS].astype(bf16)
        return 0

    lax.fori_loop(0, FACES, own2, 0)
    for k, j in ((0, 0), (1, COLS - 1)):
        for f in range(FACES):
            line = [(FIRST + i, acc[f, i * COLS + j : i * COLS + j + 1, :]) for i in range(1, ROWS - 1)]
            own_line[k, f * STACK : (f + 1) * STACK] = spread(line, STACK)

    for copy in sent[-2:]:
        copy.wait_recv()

    tops, ends, after, before = [], [], [], []
    for f in range(FACES):
        face = g * FACES + f
        n, s = jnp.where(first, ns[0, face], f), jnp.where(last, ns[1, face], f)
        flip_n, flip_s = code[0, face], code[1, face]
        k = jnp.where(first, 2 * flip_n, 0)
        r = jnp.where(k == 0, 1, 0)
        tops.append((rows1[k, n, r], rows1[k, n, 2]))
        k = jnp.where(last, 1 + 2 * flip_s, 1)
        r = jnp.where(k == 1, 0, 1)
        ends.append((rows1[k, s, r], rows1[k, s, 2]))
        s = jnp.where(first, ns[1, face], f)
        k = jnp.where(first, 2 - 2 * flip_s, 2)
        r = jnp.where(k == 0, 1, 0)
        after.append((rows1[k, s, r], rows1[k, s, 2]))
        n = jnp.where(last, ns[0, face], f)
        k = jnp.where(last, 3 - 2 * flip_n, 3)
        r = jnp.where(k == 1, 0, 1)
        before.append((rows1[k, n, r], rows1[k, n, 2]))

    def landed(k, r):
        return [(rows1[k, f, r], rows1[k, f, 2]) for f in range(FACES)]

    ROW = FACES * COLS
    stacks = (
        landed(0, 0) + tops + before,
        landed(0, 1) + landed(1, 0),
        after + landed(1, 1) + ends,
    )
    taps = (tap1, tap1_coarse)
    z_rows = [[], [], [], []]
    for b in range(3):
        y = [
            sum(tap(jnp.concatenate([r[k] for r in stacks[a]], axis=0), a, b) for k, tap in enumerate(taps))
            for a in range(3)
        ]
        z_rows[0].append(y[0][0:ROW] + y[1][0:ROW] + y[2][0:ROW])
        z_rows[1].append(y[0][2 * ROW :] + y[1][ROW:] + y[2][ROW : 2 * ROW])
        z_rows[2].append(y[0][ROW : 2 * ROW])
        z_rows[3].append(y[2][2 * ROW :])
    for k, z in enumerate(z_rows):
        z = from_west(z[0]) + z[1] + from_east(z[2])
        zrow[k] = z if k >= 2 else z + b1[...]

    for copy in sent[:-2]:
        copy.wait_recv()
    table = cols[...].reshape(lines, LINE)
    half = FACES * STACK
    sides = SIDES * STACK
    y = unpack_outer(dot(pick[0, 0], table[:, 0:WIDE]))
    z = unpack_inner(dot(pick[0, 1, 2 * sides :], table[:, LINE - WIDE :]))
    picked = [jnp.concatenate([y[0 : 2 * sides], y[2 * sides :] + z], axis=0).astype(bf16)]
    y = unpack_outer(dot(pick[1, 0], table[:, 0:WIDE]))
    z = unpack_inner(dot(pick[1, 1], table[:, LINE - WIDE :]))
    picked.append(pltpu.roll(y + z, 64, 1).astype(bf16))

    v_side, v_near = [], []
    for b in range(3):
        lines_b = []
        for chosen in picked:
            if b == 0:
                beside = [chosen[0:half], chosen[2 * sides : 3 * sides]]
            elif b == 1:
                beside = [chosen[sides : 2 * sides]]
            else:
                beside = [chosen[half : 2 * half], chosen[3 * sides :]]
            lines_b.append(jnp.concatenate(beside, axis=0))
        y = [sum(tap(x, a, b) for tap, x in zip(taps, lines_b)) for a in range(3)]
        if b != 1:
            v_side.append([x[0:half] for x in y])
            y = [x[half:] for x in y]
        v_near.append(y)
    for k in range(2):
        zcol[k] = along_rows(*v_side[k])
    near = along_rows(*[v_near[0][a] + v_near[1][a] + v_near[2][a] for a in range(3)]) + b1[...]
    near = silu(near)
    place = lax.rem(lax.broadcasted_iota(i32, near.shape, 0), STACK)
    low = jnp.where(first, 0.0, pltpu.roll(near, 2, 0))
    high = jnp.where(last, 0.0, pltpu.roll(near, near.shape[0] - 2, 0))
    near = jnp.where(place == FIRST - 1, low, jnp.where(place == FIRST + ROWS, high, near))
    near = near.astype(bf16)

    def with_sides(z, f, q):
        west = zcol[0, pl.ds(f * STACK + q, 1), :]
        east = zcol[1, pl.ds(f * STACK + q, 1), :]
        z = z + jnp.where(column == 0, jnp.broadcast_to(west, z.shape), 0.0)
        return z + jnp.where(column == COLS - 1, jnp.broadcast_to(east, z.shape), 0.0)

    def activate(f, _):
        at = pl.ds(pl.multiple_of(f * COLS, COLS), COLS)
        rows2[0, f] = silu(with_sides(zrow[0, at], f, 1)).astype(bf16)
        rows2[1, f] = silu(with_sides(zrow[1, at], f, STACK - 2)).astype(bf16)
        rows2[2, f] = silu(with_sides(acc[f, 0:COLS] + zrow[2, at], f, FIRST)).astype(bf16)
        z = acc[f, PIX - COLS : PIX] + zrow[3, at]
        rows2[3, f] = silu(with_sides(z, f, FIRST + ROWS - 1)).astype(bf16)
        return 0

    lax.fori_loop(0, FACES, activate, 0)
    place = lax.rem(lax.broadcasted_iota(i32, (half, C), 0), STACK)
    between = (place > FIRST) & (place < FIRST + ROWS - 1)
    west, east = [
        jnp.where(between, silu(own_line[k] + zcol[k]), 0.0).astype(bf16) for k in range(2)
    ]
    tops, ends = [], []
    for f in range(FACES):
        face = g * FACES + f
        n, s = jnp.where(first, ns[0, face], f), jnp.where(last, ns[1, face], f)
        tops.append(rows2[jnp.where(first, 2 * code[0, face], 0), n])
        ends.append(rows2[jnp.where(last, 1 + 2 * code[1, face], 1), s])
    top, end = [[rows2[k, f] for f in range(FACES)] for k in (2, 3)]
    stacks = (tops + top, top + end, end + ends)
    lines = ([near[0:half], west], [west, east], [near[half : 2 * half], east])
    z_rows, v = [[], [], [], []], []
    for b in range(3):
        y = [tap2(jnp.concatenate(stacks[a] + lines[b], axis=0), a, b) for a in range(3)]
        z_rows[0].append(y[0][0:ROW] + y[1][0:ROW])
        z_rows[1].append(y[0][ROW : 2 * ROW])
        z_rows[2].append(y[2][0:ROW])
        z_rows[3].append(y[1][ROW : 2 * ROW] + y[2][ROW : 2 * ROW])
        v.append([[x[2 * ROW + k * half : 2 * ROW + (k + 1) * half] for x in y] for k in range(2)])
    for k, z in enumerate(z_rows):
        zrow[k] = from_west(z[0]) + z[1] + from_east(z[2])
    z_line[0] = along_rows(*[v[0][0][a] + v[1][0][a] for a in range(3)])
    z_line[1] = along_rows(*v[0][1])
    z_line[2] = along_rows(*v[2][1])
    z_line[3] = along_rows(*[v[2][0][a] + v[1][1][a] for a in range(3)])

    few = lax.broadcasted_iota(i32, (8, C), 0)

    def finish(f, _):
        at = pl.ds(pl.multiple_of(f * COLS, COLS), COLS)
        for i in range(ROWS):
            line = [
                jnp.broadcast_to(z_line[k, pl.ds(f * STACK + FIRST + i, 1), :], (8, C)) for k in range(4)
            ]
            west = jnp.where(few == 0, line[0], jnp.where(few == 1, line[1], 0.0))
            east = jnp.where(few == 6, line[2], jnp.where(few == 7, line[3], 0.0))
            r = i * COLS
            if 2 <= i < ROWS - 2:
                out[f, i, 0:8] = (acc2[f, r : r + 8] + feature_gain * west).astype(bf16)
                out[f, i, COLS - 8 :] = (acc2[f, r + COLS - 8 : r + COLS] + feature_gain * east).astype(bf16)
                continue
            z = zrow[i if i < 2 else i - ROWS + 4, at]
            z = jnp.concatenate([z[0:8] + west, z[8 : COLS - 8], z[COLS - 8 :] + east], axis=0)
            out[f, i] = (acc2[f, r : r + COLS] + feature_gain * z).astype(bf16)
        return 0

    lax.fori_loop(0, FACES, finish, 0)
    for copy in sent:
        copy.wait_send()


def on_device(groups, tiles, sample, noise, coarse, w1, b1, w2, b2, ns, we, code):
    C = sample.shape[-1]
    w1 = jnp.swapaxes(w1, 2, 3)
    operands = (sample, noise, coarse, ns.T, we.T, code.T, w1, b1.reshape(1, C), w2, b2.reshape(1, C))
    return pl.pallas_call(
        functools.partial(kernel, groups, tiles),
        out_shape=jax.ShapeDtypeStruct(sample.shape, bf16),
        in_specs=[pl.BlockSpec(memory_space=pltpu.HBM)] * len(operands),
        out_specs=pl.BlockSpec(memory_space=pltpu.VMEM),
        scratch_shapes=[
            (pltpu.SMEM if x.dtype == i32 else pltpu.VMEM)(x.shape, x.dtype) for x in operands
        ]
        + [
            pltpu.VMEM((FACES, PIX, WIDE), f32),
            pltpu.VMEM((FACES, PIX, C), f32),
            pltpu.VMEM((FACES, PIX, C), f32),
            pltpu.VMEM((2, FACES * STACK, C), f32),
            pltpu.VMEM((4, FACES * STACK, C), f32),
            pltpu.VMEM((FACES, PIX + 2 * COLS, WIDE), bf16),
            pltpu.VMEM((FACES, PIX + 2 * COLS, C), bf16),
            pltpu.VMEM((FACES * COLS, WIDE), bf16),
            pltpu.VMEM((3, FACES * COLS, C), f32),
            pltpu.VMEM((groups, BLOCKS, 16, LINE), bf16),
            pltpu.VMEM((2, 16, LINE), bf16),
            pltpu.VMEM((4, FACES, 3, COLS, WIDE), bf16),
            pltpu.VMEM((4, FACES, COLS, C), bf16),
            pltpu.VMEM((2, 2, 4 * SIDES * STACK, groups * BLOCKS * 16), bf16),
            pltpu.VMEM((2, FACES * STACK, C), f32),
            pltpu.VMEM((4, FACES * COLS, C), f32),
            pltpu.SemaphoreType.DMA((len(operands),)),
            pltpu.SemaphoreType.DMA((13,)),
            pltpu.SemaphoreType.DMA((13,)),
        ],
        compiler_params=pltpu.CompilerParams(
            collective_id=0, has_side_effects=True, vmem_limit_bytes=32 * 2**20
        ),
    )(*[pltpu.with_memory_space_constraint(x, pltpu.HBM) for x in operands])


def solution(mesh):
    return jax.shard_map(
        functools.partial(on_device, mesh.shape["face"], mesh.shape["tile"]),
        mesh=mesh,
        in_specs=(P("face", "tile", None, None),) * 3 + (P(),) * 7,
        out_specs=P("face", "tile", None, None),
        check_vma=False,
    )
```

```python
import functools

import jax
import jax.numpy as jnp
from jax import lax
from jax.experimental import pallas as pl
from jax.experimental.pallas import tpu as pltpu
from jax.sharding import PartitionSpec as P

MESH = pl.DeviceIdType.MESH
f32 = jnp.float32
bf16 = jnp.bfloat16
i32 = jnp.int32

noise_gain = 0.6
input_gain = 0.7071067811865476
skip_gain = 0.5
output_gain = 0.7071067811865476
step_ratio = -0.4
feature_gain = -step_ratio * output_gain

UP = 8
FACES = 3
ROWS = 8
COLS = 32
COARSE = COLS // UP
PIX = ROWS * COLS
SIDES = 2 * FACES
WIDE = 256

BLOCKS = 6
FACE, OVER, UNDER = 1, 4, 5
LINE = 384
CORNER = 4 * FACES
STACK = 16
FIRST = 4


def dot(a, b):
    return jnp.dot(a, b, preferred_element_type=f32)


def dot_t(a, b):
    return lax.dot_general(a, b, (((1,), (1,)), ((), ())), preferred_element_type=f32)


def column_of(shape):
    return lax.rem(lax.broadcasted_iota(i32, shape, 0), COLS)


def from_west(z):
    return jnp.where(column_of(z.shape) == 0, 0.0, pltpu.roll(z, 1, 0))


def from_east(z):
    return jnp.where(column_of(z.shape) == COLS - 1, 0.0, pltpu.roll(z, z.shape[0] - 1, 0))


def along_rows(v0, v1, v2):
    return pltpu.roll(v0, 1, 0) + v1 + pltpu.roll(v2, v2.shape[0] - 1, 0)


def silu(u):
    return u / (1.0 + jnp.exp(-u))


def spread(rows, count):
    width = rows[0][1].shape[1]
    place = lax.broadcasted_iota(i32, (count, width), 0)
    out = jnp.zeros((count, width), f32)
    for at, row in rows:
        out = jnp.where(place == at, jnp.broadcast_to(row, (count, width)), out)
    return out


def pack(outer, inner):
    rest = outer[:, 128:WIDE] + pltpu.roll(inner[:, 128:WIDE], 64, 1)
    return jnp.concatenate([outer[:, 0:128], rest, inner[:, 0:128]], axis=1).astype(bf16)


def unpack_outer(y):
    lane = lax.broadcasted_iota(i32, y.shape, 1)
    return jnp.where(lane < LINE // 2, y, 0.0)


def unpack_inner(y):
    return unpack_outer(jnp.concatenate([y[:, 128:], pltpu.roll(y[:, 0:128], 64, 1)], axis=1))


def kernel(
    groups,
    tiles,
    sample_hbm,
    noise_hbm,
    coarse_hbm,
    ns_hbm,
    we_hbm,
    code_hbm,
    w1_hbm,
    b1_hbm,
    w2_hbm,
    b2_hbm,
    out,
    sample,
    noise,
    coarse,
    ns,
    we,
    code,
    w1,
    b1,
    w2,
    b2,
    pf,
    acc,
    acc2,
    own_line,
    z_line,
    xp,
    hp,
    up,
    cclass,
    cols,
    corner,
    rows1,
    rows2,
    pick,
    zcol,
    zrow,
    load_sem,
    send_sem,
    recv_sem,
):
    g = lax.axis_index("face")
    t = lax.axis_index("tile")
    above = lax.rem(t + tiles - 1, tiles)
    below = lax.rem(t + 1, tiles)
    first = t == 0
    last = t == tiles - 1
    C = acc.shape[2]
    lines = groups * BLOCKS * 16

    barrier = pltpu.get_barrier_semaphore()
    for d in (2, 1, 3, 0):
        for k, there in enumerate((t, above, below)):
            if d or k:
                pl.semaphore_signal(
                    barrier, inc=1, device_id=(lax.rem(g + d, groups), there), device_id_type=MESH
                )

    loads = [
        pltpu.make_async_copy(src, dst, load_sem.at[i])
        for i, (src, dst) in enumerate(
            [
                (sample_hbm, sample),
                (noise_hbm, noise),
                (coarse_hbm, coarse),
                (ns_hbm, ns),
                (we_hbm, we),
                (code_hbm, code),
                (w1_hbm, w1),
                (b1_hbm, b1),
                (w2_hbm, w2),
                (b2_hbm, b2),
            ]
        )
    ]
    for copy in loads[:6]:
        copy.start()

    for f in range(FACES):
        zero_row = jnp.zeros((COLS, WIDE), bf16)
        xp[f, 0:COLS] = zero_row
        xp[f, COLS + PIX : 2 * COLS + PIX] = zero_row
        xp[f, COLS : COLS + PIX, 128:WIDE] = jnp.zeros((PIX, WIDE - 128), bf16)
        pf[f, :, 128:WIDE] = jnp.zeros((PIX, WIDE - 128), f32)
        hp[f, 0 : 2 * COLS] = jnp.zeros((2 * COLS, C), bf16)
        hp[f, PIX : PIX + 2 * COLS] = jnp.zeros((2 * COLS, C), bf16)

    for copy in loads[:3]:
        copy.wait()
    for f in range(FACES):
        p = sample[f].astype(f32) + noise_gain * noise[f].astype(f32)
        p = p.reshape(PIX, C)
        pf[f, :, 0:C] = p
        xp[f, COLS : COLS + PIX, 0:C] = (p * input_gain).astype(bf16)
        for r in range(2):
            rows1[2, f, r] = xp[f, (1 + r) * COLS : (2 + r) * COLS]
            rows1[3, f, r] = xp[f, PIX - COLS + r * COLS : PIX + r * COLS]
    raw, tops, ends = [([], []) for _ in range(3)]
    blank = jnp.zeros((COARSE, WIDE - C), f32)
    for f in range(FACES):
        c = coarse[f, 0].astype(f32)
        line = jnp.concatenate([c, blank], axis=1)
        c = jnp.concatenate([blank, c], axis=1)
        each = [c[j : j + 1] for j in range(COARSE)]
        wide = jnp.concatenate([jnp.broadcast_to(e, (UP, WIDE)) for e in each], axis=0).astype(bf16)
        up[f * COLS : (f + 1) * COLS] = wide
        rows1[2, f, 2] = wide
        rows1[3, f, 2] = wide
        for inner, j in ((0, 0), (1, COARSE - 1)):
            raw[inner].append((f, line[j : j + 1]))
            tops[inner].append((CORNER + f, line[j : j + 1]))
            ends[inner].append((CORNER + f, line[j : j + 1]))
        halves = ([], [])
        for inner, high, j in ((0, 0, 0), (0, 1, COLS - 1), (1, 0, 1), (1, 1, COLS - 2)):
            line_j = [pf[f, i * COLS + j : i * COLS + j + 1, :] * input_gain for i in range(ROWS)]
            halves[inner].append(spread(list(enumerate(line_j)), ROWS))
            tops[inner].extend((4 * f + 2 * high + r, line_j[r]) for r in range(2))
            ends[inner].extend((4 * f + 2 * high + r, line_j[ROWS - 2 + r]) for r in range(2))
        cols[g, FACE + f] = pack(*[jnp.concatenate(h, axis=0) for h in halves])
    cols[g, 0] = pack(*[spread(x, 16) for x in raw])
    corner[0] = pack(*[spread(x, 16) for x in tops])
    corner[1] = pack(*[spread(x, 16) for x in ends])

    sent = []

    def add(src, dst, there):
        n = len(sent)
        sent.append(
            pltpu.make_async_remote_copy(
                src_ref=src,
                dst_ref=dst,
                send_sem=send_sem.at[n],
                recv_sem=recv_sem.at[n],
                device_id=there,
                device_id_type=MESH,
            )
        )

    table = cols.at[g, pl.ds(0, OVER)]
    over = cols.at[g, OVER]
    under = cols.at[g, UNDER]
    for d in (2, 1, 3):
        far = lax.rem(g + d, groups)
        add(corner.at[0], under, (far, above))
        add(corner.at[1], over, (far, below))
        add(table, table, (far, t))
    add(corner.at[0], under, (g, above))
    add(corner.at[1], over, (g, below))
    add(rows1.at[2], rows1.at[1], (g, above))
    add(rows1.at[3], rows1.at[0], (g, below))

    pl.semaphore_wait(barrier, 3 * groups - 1)
    for copy in sent:
        copy.start()
    for copy in loads[6:]:
        copy.start()
    for copy in loads[3:6]:
        copy.wait()

    lane = lax.broadcasted_iota(i32, (STACK, lines), 1)
    place = lax.broadcasted_iota(i32, (STACK, lines), 0)

    def split(face):
        group = sum((face >= FACES * k).astype(i32) for k in range(1, groups))
        return group, face - FACES * group

    def across(face, side):
        edge = code[2 + side, face]
        return we[side, face], 3 * jnp.where(side == 1, edge, 1 - edge)

    def write_pick(at, face, column, beyond):
        group, f = split(face)
        base = group * (BLOCKS * 16)
        inner = (column == 1) | (column == 2)
        high = (column >= 2).astype(i32)

        def line(ff, row):
            if row < 0:
                return base + OVER * 16 + ff * 4 + high * 2 + 2 + row
            if row >= ROWS:
                return base + UNDER * 16 + ff * 4 + high * 2 + row - ROWS
            return base + (FACE + ff) * 16 + high * 8 + row

        def condition(ff, row):
            if row < 0:
                return base + OVER * 16 + CORNER + ff
            if row >= ROWS:
                return base + UNDER * 16 + CORNER + ff
            return base + ff

        n, s = ns[0, face], ns[1, face]
        flip_n, flip_s = code[0, face] == 1, code[1, face] == 1
        for part, where in enumerate((line, condition)):
            north = jnp.where(beyond, -1, jnp.where(flip_n, where(n, 0), where(n, -1)))
            south = jnp.where(beyond, -1, jnp.where(flip_s, where(s, ROWS - 1), where(s, ROWS)))
            target = jnp.broadcast_to(where(f, 0), place.shape)
            if part == 0:
                target = target + place - FIRST
            for q, value in (
                (0, where(f, -2)),
                (1, where(f, -1)),
                (2, jnp.where(first, -1, where(f, 0))),
                (3, jnp.where(first, north, where(f, -1))),
                (12, jnp.where(last, south, where(f, ROWS))),
                (13, jnp.where(last, -1, where(f, ROWS - 1))),
                (14, where(f, ROWS)),
                (15, where(f, ROWS + 1)),
            ):
                target = jnp.where(place == q, value, target)
            at = pl.multiple_of(at, STACK)
            second = high == 1 if part else inner
            for k, chosen in ((0, jnp.where(second, -1, target)), (1, jnp.where(second, target, -1))):
                pick[k, part, pl.ds(at, STACK), :] = jnp.where(lane == chosen, 1.0, 0.0).astype(bf16)

    def pick_side(n, _):
        side = (n >= FACES).astype(i32)
        face = g * FACES + n - FACES * side
        near, column = across(face, side)
        west_face, west_column = across(near, 0)
        east_face, east_column = across(near, 1)
        at_west = column == 0
        at_east = column == 3
        write_pick(n * STACK, near, column, True)
        write_pick(
            (2 * SIDES + n) * STACK,
            jnp.where(at_west, west_face, near),
            jnp.where(at_west, west_column, 2),
            at_west,
        )
        write_pick((SIDES + n) * STACK, near, column, False)
        write_pick(
            (3 * SIDES + n) * STACK,
            jnp.where(at_east, east_face, near),
            jnp.where(at_east, east_column, 1),
            at_east,
        )
        return 0

    lax.fori_loop(0, SIDES, pick_side, 0)

    def tap1(x, a, b):
        return dot_t(x, w1[a, b, :, 0:WIDE])

    def tap1_coarse(x, a, b):
        return dot_t(x, w1[a, b, :, w1.shape[3] - WIDE :])

    def tap2(x, a, b):
        return dot(x, w2[a, b])

    def conv_own(src, tap, f, b):
        z = tap(src[f, 0:PIX], 0, b)
        z = z + tap(src[f, COLS : COLS + PIX], 1, b)
        return z + tap(src[f, 2 * COLS : 2 * COLS + PIX], 2, b)

    for copy in loads[6:]:
        copy.wait()
    parts = []
    for b in range(3):
        c0, c1, c2 = [tap1_coarse(up[...], a, b) for a in range(3)]
        parts.append((c1 + c2, c0 + c1 + c2, c0 + c1))
    for k in range(3):
        cclass[k] = from_west(parts[0][k]) + parts[1][k] + from_east(parts[2][k]) + b1[...]

    def own1(f, _):
        z = from_west(conv_own(xp, tap1, f, 0)) + conv_own(xp, tap1, f, 1) + from_east(conv_own(xp, tap1, f, 2))
        at = pl.ds(pl.multiple_of(f * COLS, COLS), COLS)
        for i in range(ROWS):
            k = 0 if i == 0 else 2 if i == ROWS - 1 else 1
            acc[f, i * COLS : (i + 1) * COLS] = z[i * COLS : (i + 1) * COLS] + cclass[k, at]
        return 0

    lax.fori_loop(0, FACES, own1, 0)

    column = column_of((COLS, C))
    border = (column == 0) | (column == COLS - 1)

    def inside(f, _):
        for i in range(1, ROWS - 1):
            h = silu(acc[f, i * COLS : (i + 1) * COLS])
            hp[f, (i + 1) * COLS : (i + 2) * COLS] = jnp.where(border, 0.0, h).astype(bf16)
        return 0

    lax.fori_loop(0, FACES, inside, 0)

    def own2(f, _):
        z = from_west(conv_own(hp, tap2, f, 0)) + conv_own(hp, tap2, f, 1) + from_east(conv_own(hp, tap2, f, 2))
        p = pf[f, :, 0:C]
        denoised = skip_gain * p + output_gain * (z + b2[...])
        z = p + step_ratio * (p - denoised)
        acc2[f] = z
        for i in range(2, ROWS - 2):
            out[f, i] = z[i * COLS : (i + 1) * COLS].astype(bf16)
        return 0

    lax.fori_loop(0, FACES, own2, 0)
    for k, j in ((0, 0), (1, COLS - 1)):
        for f in range(FACES):
            line = [(FIRST + i, acc[f, i * COLS + j : i * COLS + j + 1, :]) for i in range(1, ROWS - 1)]
            own_line[k, f * STACK : (f + 1) * STACK] = spread(line, STACK)

    for copy in sent[-2:]:
        copy.wait_recv()

    tops, ends, after, before = [], [], [], []
    for f in range(FACES):
        face = g * FACES + f
        n, s = jnp.where(first, ns[0, face], f), jnp.where(last, ns[1, face], f)
        flip_n, flip_s = code[0, face], code[1, face]
        k = jnp.where(first, 2 * flip_n, 0)
        r = jnp.where(k == 0, 1, 0)
        tops.append((rows1[k, n, r], rows1[k, n, 2]))
        k = jnp.where(last, 1 + 2 * flip_s, 1)
        r = jnp.where(k == 1, 0, 1)
        ends.append((rows1[k, s, r], rows1[k, s, 2]))
        s = jnp.where(first, ns[1, face], f)
        k = jnp.where(first, 2 - 2 * flip_s, 2)
        r = jnp.where(k == 0, 1, 0)
        after.append((rows1[k, s, r], rows1[k, s, 2]))
        n = jnp.where(last, ns[0, face], f)
        k = jnp.where(last, 3 - 2 * flip_n, 3)
        r = jnp.where(k == 1, 0, 1)
        before.append((rows1[k, n, r], rows1[k, n, 2]))

    def landed(k, r):
        return [(rows1[k, f, r], rows1[k, f, 2]) for f in range(FACES)]

    ROW = FACES * COLS
    stacks = (
        landed(0, 0) + tops + before,
        landed(0, 1) + landed(1, 0),
        after + landed(1, 1) + ends,
    )
    taps = (tap1, tap1_coarse)
    z_rows = [[], [], [], []]
    for b in range(3):
        y = [
            sum(tap(jnp.concatenate([r[k] for r in stacks[a]], axis=0), a, b) for k, tap in enumerate(taps))
            for a in range(3)
        ]
        z_rows[0].append(y[0][0:ROW] + y[1][0:ROW] + y[2][0:ROW])
        z_rows[1].append(y[0][2 * ROW :] + y[1][ROW:] + y[2][ROW : 2 * ROW])
        z_rows[2].append(y[0][ROW : 2 * ROW])
        z_rows[3].append(y[2][2 * ROW :])
    for k, z in enumerate(z_rows):
        z = from_west(z[0]) + z[1] + from_east(z[2])
        zrow[k] = z if k >= 2 else z + b1[...]

    for copy in sent[:-2]:
        copy.wait_recv()
    table = cols[...].reshape(lines, LINE)
    half = FACES * STACK
    sides = SIDES * STACK
    y = unpack_outer(dot(pick[0].reshape(8 * sides, lines), table[:, 0:WIDE]))
    z = unpack_inner(dot(pick[1].reshape(8 * sides, lines)[2 * sides :], table[:, LINE - WIDE :]))
    picked = [jnp.concatenate([y[0 : 2 * sides], y[2 * sides : 4 * sides] + z[0 : 2 * sides]], axis=0)]
    picked.append(pltpu.roll(y[4 * sides :] + z[2 * sides :], 64, 1))
    picked = [x.astype(bf16) for x in picked]

    v_side, v_near = [], []
    for b in range(3):
        lines_b = []
        for chosen in picked:
            if b == 0:
                beside = [chosen[0:half], chosen[2 * sides : 3 * sides]]
            elif b == 1:
                beside = [chosen[sides : 2 * sides]]
            else:
                beside = [chosen[half : 2 * half], chosen[3 * sides :]]
            lines_b.append(jnp.concatenate(beside, axis=0))
        y = [sum(tap(x, a, b) for tap, x in zip(taps, lines_b)) for a in range(3)]
        if b != 1:
            v_side.append([x[0:half] for x in y])
            y = [x[half:] for x in y]
        v_near.append(y)
    for k in range(2):
        zcol[k] = along_rows(*v_side[k])
    near = along_rows(*[v_near[0][a] + v_near[1][a] + v_near[2][a] for a in range(3)]) + b1[...]
    near = silu(near)
    place = lax.rem(lax.broadcasted_iota(i32, near.shape, 0), STACK)
    low = jnp.where(first, 0.0, pltpu.roll(near, 2, 0))
    high = jnp.where(last, 0.0, pltpu.roll(near, near.shape[0] - 2, 0))
    near = jnp.where(place == FIRST - 1, low, jnp.where(place == FIRST + ROWS, high, near))
    near = near.astype(bf16)

    def with_sides(z, f, q):
        west = zcol[0, pl.ds(f * STACK + q, 1), :]
        east = zcol[1, pl.ds(f * STACK + q, 1), :]
        z = z + jnp.where(column == 0, jnp.broadcast_to(west, z.shape), 0.0)
        return z + jnp.where(column == COLS - 1, jnp.broadcast_to(east, z.shape), 0.0)

    def activate(f):
        at = pl.ds(f * COLS, COLS)
        rows2[0, f] = silu(with_sides(zrow[0, at], f, 1)).astype(bf16)
        rows2[1, f] = silu(with_sides(zrow[1, at], f, STACK - 2)).astype(bf16)
        rows2[2, f] = silu(with_sides(acc[f, 0:COLS] + zrow[2, at], f, FIRST)).astype(bf16)
        z = acc[f, PIX - COLS : PIX] + zrow[3, at]
        rows2[3, f] = silu(with_sides(z, f, FIRST + ROWS - 1)).astype(bf16)

    for f in range(FACES):
        activate(f)
    place = lax.rem(lax.broadcasted_iota(i32, (half, C), 0), STACK)
    between = (place > FIRST) & (place < FIRST + ROWS - 1)
    west, east = [
        jnp.where(between, silu(own_line[k] + zcol[k]), 0.0).astype(bf16) for k in range(2)
    ]
    tops, ends = [], []
    for f in range(FACES):
        face = g * FACES + f
        n, s = jnp.where(first, ns[0, face], f), jnp.where(last, ns[1, face], f)
        tops.append(rows2[jnp.where(first, 2 * code[0, face], 0), n])
        ends.append(rows2[jnp.where(last, 1 + 2 * code[1, face], 1), s])
    top, end = [[rows2[k, f] for f in range(FACES)] for k in (2, 3)]
    stacks = (tops + top, top + end, end + ends)
    lines = ([near[0:half], west], [west, east], [near[half : 2 * half], east])
    z_rows, v = [[], [], [], []], []
    for b in range(3):
        y = [tap2(jnp.concatenate(stacks[a] + lines[b], axis=0), a, b) for a in range(3)]
        z_rows[0].append(y[0][0:ROW] + y[1][0:ROW])
        z_rows[1].append(y[0][ROW : 2 * ROW])
        z_rows[2].append(y[2][0:ROW])
        z_rows[3].append(y[1][ROW : 2 * ROW] + y[2][ROW : 2 * ROW])
        v.append([[x[2 * ROW + k * half : 2 * ROW + (k + 1) * half] for x in y] for k in range(2)])
    for k, z in enumerate(z_rows):
        zrow[k] = from_west(z[0]) + z[1] + from_east(z[2])
    z_line[0] = along_rows(*[v[0][0][a] + v[1][0][a] for a in range(3)])
    z_line[1] = along_rows(*v[0][1])
    z_line[2] = along_rows(*v[2][1])
    z_line[3] = along_rows(*[v[2][0][a] + v[1][1][a] for a in range(3)])

    few = lax.broadcasted_iota(i32, (8, C), 0)

    def finish(f):
        at = pl.ds(f * COLS, COLS)
        for i in range(ROWS):
            line = [
                jnp.broadcast_to(z_line[k, pl.ds(f * STACK + FIRST + i, 1), :], (8, C)) for k in range(4)
            ]
            west = jnp.where(few == 0, line[0], jnp.where(few == 1, line[1], 0.0))
            east = jnp.where(few == 6, line[2], jnp.where(few == 7, line[3], 0.0))
            r = i * COLS
            if 2 <= i < ROWS - 2:
                out[f, i, 0:8] = (acc2[f, r : r + 8] + feature_gain * west).astype(bf16)
                out[f, i, COLS - 8 :] = (acc2[f, r + COLS - 8 : r + COLS] + feature_gain * east).astype(bf16)
                continue
            z = zrow[i if i < 2 else i - ROWS + 4, at]
            z = jnp.concatenate([z[0:8] + west, z[8 : COLS - 8], z[COLS - 8 :] + east], axis=0)
            out[f, i] = (acc2[f, r : r + COLS] + feature_gain * z).astype(bf16)

    for f in range(FACES):
        finish(f)
    for copy in sent:
        copy.wait_send()


def on_device(groups, tiles, sample, noise, coarse, w1, b1, w2, b2, ns, we, code):
    C = sample.shape[-1]
    w1 = jnp.swapaxes(w1, 2, 3)
    operands = (sample, noise, coarse, ns.T, we.T, code.T, w1, b1.reshape(1, C), w2, b2.reshape(1, C))
    return pl.pallas_call(
        functools.partial(kernel, groups, tiles),
        out_shape=jax.ShapeDtypeStruct(sample.shape, bf16),
        in_specs=[pl.BlockSpec(memory_space=pltpu.HBM)] * len(operands),
        out_specs=pl.BlockSpec(memory_space=pltpu.VMEM),
        scratch_shapes=[
            (pltpu.SMEM if x.dtype == i32 else pltpu.VMEM)(x.shape, x.dtype) for x in operands
        ]
        + [
            pltpu.VMEM((FACES, PIX, WIDE), f32),
            pltpu.VMEM((FACES, PIX, C), f32),
            pltpu.VMEM((FACES, PIX, C), f32),
            pltpu.VMEM((2, FACES * STACK, C), f32),
            pltpu.VMEM((4, FACES * STACK, C), f32),
            pltpu.VMEM((FACES, PIX + 2 * COLS, WIDE), bf16),
            pltpu.VMEM((FACES, PIX + 2 * COLS, C), bf16),
            pltpu.VMEM((FACES * COLS, WIDE), bf16),
            pltpu.VMEM((3, FACES * COLS, C), f32),
            pltpu.VMEM((groups, BLOCKS, 16, LINE), bf16),
            pltpu.VMEM((2, 16, LINE), bf16),
            pltpu.VMEM((4, FACES, 3, COLS, WIDE), bf16),
            pltpu.VMEM((4, FACES, COLS, C), bf16),
            pltpu.VMEM((2, 2, 4 * SIDES * STACK, groups * BLOCKS * 16), bf16),
            pltpu.VMEM((2, FACES * STACK, C), f32),
            pltpu.VMEM((4, FACES * COLS, C), f32),
            pltpu.SemaphoreType.DMA((len(operands),)),
            pltpu.SemaphoreType.DMA((13,)),
            pltpu.SemaphoreType.DMA((13,)),
        ],
        compiler_params=pltpu.CompilerParams(
            collective_id=0, has_side_effects=True, vmem_limit_bytes=32 * 2**20
        ),
    )(*[pltpu.with_memory_space_constraint(x, pltpu.HBM) for x in operands])


def solution(mesh):
    return jax.shard_map(
        functools.partial(on_device, mesh.shape["face"], mesh.shape["tile"]),
        mesh=mesh,
        in_specs=(P("face", "tile", None, None),) * 3 + (P(),) * 7,
        out_specs=P("face", "tile", None, None),
        check_vma=False,
    )
```

```python
import functools

import jax
import jax.numpy as jnp
from jax import lax
from jax.experimental import pallas as pl
from jax.experimental.pallas import tpu as pltpu
from jax.sharding import PartitionSpec as P

MESH = pl.DeviceIdType.MESH
f32 = jnp.float32
bf16 = jnp.bfloat16
i32 = jnp.int32

noise_gain = 0.6
input_gain = 0.7071067811865476
skip_gain = 0.5
output_gain = 0.7071067811865476
step_ratio = -0.4
feature_gain = -step_ratio * output_gain

UP = 8
FACES = 3
ROWS = 8
COLS = 32
COARSE = COLS // UP
PIX = ROWS * COLS
SIDES = 2 * FACES
WIDE = 256

BLOCKS = 6
FACE, OVER, UNDER = 1, 4, 5
LINE = 384
CORNER = 4 * FACES
STACK = 16
FIRST = 4


def dot(a, b):
    return jnp.dot(a, b, preferred_element_type=f32)


def dot_t(a, b):
    return lax.dot_general(a, b, (((1,), (1,)), ((), ())), preferred_element_type=f32)


def column_of(shape):
    return lax.rem(lax.broadcasted_iota(i32, shape, 0), COLS)


def from_west(z):
    return jnp.where(column_of(z.shape) == 0, 0.0, pltpu.roll(z, 1, 0))


def from_east(z):
    return jnp.where(column_of(z.shape) == COLS - 1, 0.0, pltpu.roll(z, z.shape[0] - 1, 0))


def along_rows(v0, v1, v2):
    return pltpu.roll(v0, 1, 0) + v1 + pltpu.roll(v2, v2.shape[0] - 1, 0)


def silu(u):
    return u / (1.0 + jnp.exp(-u))


def spread(rows, count):
    width = rows[0][1].shape[1]
    place = lax.broadcasted_iota(i32, (count, width), 0)
    out = jnp.zeros((count, width), f32)
    for at, row in rows:
        out = jnp.where(place == at, jnp.broadcast_to(row, (count, width)), out)
    return out


def pack(outer, inner):
    rest = outer[:, 128:WIDE] + pltpu.roll(inner[:, 128:WIDE], 64, 1)
    return jnp.concatenate([outer[:, 0:128], rest, inner[:, 0:128]], axis=1).astype(bf16)


def unpack_outer(y):
    lane = lax.broadcasted_iota(i32, y.shape, 1)
    return jnp.where(lane < LINE // 2, y, 0.0)


def unpack_inner(y):
    return unpack_outer(jnp.concatenate([y[:, 128:], pltpu.roll(y[:, 0:128], 64, 1)], axis=1))


def widened(each):
    return jnp.concatenate([jnp.broadcast_to(e, (UP, WIDE)) for e in each], axis=0).astype(bf16)


def kernel(
    groups,
    tiles,
    sample_hbm,
    noise_hbm,
    coarse_hbm,
    ns_hbm,
    we_hbm,
    code_hbm,
    w1_hbm,
    b1_hbm,
    w2_hbm,
    b2_hbm,
    out,
    sample,
    noise,
    coarse,
    ns,
    we,
    code,
    w1,
    b1,
    w2,
    b2,
    pf,
    acc,
    acc2,
    own_line,
    z_line,
    xp,
    hp,
    up,
    cclass,
    cols,
    corner,
    craw,
    rows1,
    rows2,
    pick,
    zcol,
    zrow,
    load_sem,
    send_sem,
    recv_sem,
):
    g = lax.axis_index("face")
    t = lax.axis_index("tile")
    above = lax.rem(t + tiles - 1, tiles)
    below = lax.rem(t + 1, tiles)
    first = t == 0
    last = t == tiles - 1
    C = acc.shape[2]
    lines = groups * BLOCKS * 16

    barrier = pltpu.get_barrier_semaphore()
    for d in (2, 1, 3, 0):
        for k, there in enumerate((t, above, below)):
            if d or k:
                pl.semaphore_signal(
                    barrier, inc=1, device_id=(lax.rem(g + d, groups), there), device_id_type=MESH
                )

    loads = [
        pltpu.make_async_copy(src, dst, load_sem.at[i])
        for i, (src, dst) in enumerate(
            [
                (sample_hbm, sample),
                (noise_hbm, noise),
                (coarse_hbm, coarse),
                (ns_hbm, ns),
                (we_hbm, we),
                (code_hbm, code),
                (w1_hbm, w1),
                (b1_hbm, b1),
                (w2_hbm, w2),
                (b2_hbm, b2),
            ]
        )
    ]
    for copy in loads[:6]:
        copy.start()

    for f in range(FACES):
        zero_row = jnp.zeros((COLS, WIDE), bf16)
        xp[f, 0:COLS] = zero_row
        xp[f, COLS + PIX : 2 * COLS + PIX] = zero_row
        xp[f, COLS : COLS + PIX, 128:WIDE] = jnp.zeros((PIX, WIDE - 128), bf16)
        pf[f, :, 128:WIDE] = jnp.zeros((PIX, WIDE - 128), f32)
        hp[f, 0 : 2 * COLS] = jnp.zeros((2 * COLS, C), bf16)
        hp[f, PIX : PIX + 2 * COLS] = jnp.zeros((2 * COLS, C), bf16)

    for copy in loads[:3]:
        copy.wait()
    for f in range(FACES):
        p = sample[f].astype(f32) + noise_gain * noise[f].astype(f32)
        p = p.reshape(PIX, C)
        pf[f, :, 0:C] = p
        xp[f, COLS : COLS + PIX, 0:C] = (p * input_gain).astype(bf16)
        for r in range(2):
            rows1[2, f, r] = xp[f, (1 + r) * COLS : (2 + r) * COLS]
            rows1[3, f, r] = xp[f, PIX - COLS + r * COLS : PIX + r * COLS]
    raw, tops, ends = [([], []) for _ in range(3)]
    all_raw = []
    blank = jnp.zeros((COARSE, WIDE - C), f32)
    for f in range(FACES):
        c = coarse[f, 0].astype(f32)
        line = jnp.concatenate([c, blank], axis=1)
        c = jnp.concatenate([blank, c], axis=1)
        each = [c[j : j + 1] for j in range(COARSE)]
        wide = widened(each)
        all_raw += [(f * COARSE + j, each[j]) for j in range(COARSE)]
        up[f * COLS : (f + 1) * COLS] = wide
        rows1[2, f, 2] = wide
        rows1[3, f, 2] = wide
        for inner, j in ((0, 0), (1, COARSE - 1)):
            raw[inner].append((f, line[j : j + 1]))
            tops[inner].append((CORNER + f, line[j : j + 1]))
            ends[inner].append((CORNER + f, line[j : j + 1]))
        halves = ([], [])
        for inner, high, j in ((0, 0, 0), (0, 1, COLS - 1), (1, 0, 1), (1, 1, COLS - 2)):
            line_j = [pf[f, i * COLS + j : i * COLS + j + 1, :] * input_gain for i in range(ROWS)]
            halves[inner].append(spread(list(enumerate(line_j)), ROWS))
            tops[inner].extend((4 * f + 2 * high + r, line_j[r]) for r in range(2))
            ends[inner].extend((4 * f + 2 * high + r, line_j[ROWS - 2 + r]) for r in range(2))
        cols[g, FACE + f] = pack(*[jnp.concatenate(h, axis=0) for h in halves])
    cols[g, 0] = pack(*[spread(x, 16) for x in raw])
    craw[2] = spread(all_raw, 16).astype(bf16)
    corner[0] = pack(*[spread(x, 16) for x in tops])
    corner[1] = pack(*[spread(x, 16) for x in ends])

    sent = []

    def add(src, dst, there):
        n = len(sent)
        sent.append(
            pltpu.make_async_remote_copy(
                src_ref=src,
                dst_ref=dst,
                send_sem=send_sem.at[n],
                recv_sem=recv_sem.at[n],
                device_id=there,
                device_id_type=MESH,
            )
        )

    table = cols.at[g, pl.ds(0, OVER)]
    over = cols.at[g, OVER]
    under = cols.at[g, UNDER]
    for d in (2, 1, 3):
        far = lax.rem(g + d, groups)
        add(corner.at[0], under, (far, above))
        add(corner.at[1], over, (far, below))
        add(table, table, (far, t))
    add(corner.at[0], under, (g, above))
    add(corner.at[1], over, (g, below))
    both = pl.ds(0, 2)
    add(rows1.at[2, :, both], rows1.at[1, :, both], (g, above))
    add(rows1.at[3, :, both], rows1.at[0, :, both], (g, below))
    add(craw.at[2], craw.at[1], (g, above))
    add(craw.at[2], craw.at[0], (g, below))

    pl.semaphore_wait(barrier, 3 * groups - 1)
    for copy in sent:
        copy.start()
    for copy in loads[6:]:
        copy.start()
    for copy in loads[3:6]:
        copy.wait()

    lane = lax.broadcasted_iota(i32, (STACK, lines), 1)
    place = lax.broadcasted_iota(i32, (STACK, lines), 0)

    def split(face):
        group = sum((face >= FACES * k).astype(i32) for k in range(1, groups))
        return group, face - FACES * group

    def across(face, side):
        edge = code[2 + side, face]
        return we[side, face], 3 * jnp.where(side == 1, edge, 1 - edge)

    def write_pick(at, face, column, beyond):
        group, f = split(face)
        base = group * (BLOCKS * 16)
        inner = (column == 1) | (column == 2)
        high = (column >= 2).astype(i32)

        def line(ff, row):
            if row < 0:
                return base + OVER * 16 + ff * 4 + high * 2 + 2 + row
            if row >= ROWS:
                return base + UNDER * 16 + ff * 4 + high * 2 + row - ROWS
            return base + (FACE + ff) * 16 + high * 8 + row

        def condition(ff, row):
            if row < 0:
                return base + OVER * 16 + CORNER + ff
            if row >= ROWS:
                return base + UNDER * 16 + CORNER + ff
            return base + ff

        n, s = ns[0, face], ns[1, face]
        flip_n, flip_s = code[0, face] == 1, code[1, face] == 1
        for part, where in enumerate((line, condition)):
            north = jnp.where(beyond, -1, jnp.where(flip_n, where(n, 0), where(n, -1)))
            south = jnp.where(beyond, -1, jnp.where(flip_s, where(s, ROWS - 1), where(s, ROWS)))
            target = jnp.broadcast_to(where(f, 0), place.shape)
            if part == 0:
                target = target + place - FIRST
            for q, value in (
                (0, where(f, -2)),
                (1, where(f, -1)),
                (2, jnp.where(first, -1, where(f, 0))),
                (3, jnp.where(first, north, where(f, -1))),
                (12, jnp.where(last, south, where(f, ROWS))),
                (13, jnp.where(last, -1, where(f, ROWS - 1))),
                (14, where(f, ROWS)),
                (15, where(f, ROWS + 1)),
            ):
                target = jnp.where(place == q, value, target)
            at = pl.multiple_of(at, STACK)
            second = high == 1 if part else inner
            for k, chosen in ((0, jnp.where(second, -1, target)), (1, jnp.where(second, target, -1))):
                pick[k, part, pl.ds(at, STACK), :] = jnp.where(lane == chosen, 1.0, 0.0).astype(bf16)

    def pick_side(n, _):
        side = (n >= FACES).astype(i32)
        face = g * FACES + n - FACES * side
        near, column = across(face, side)
        west_face, west_column = across(near, 0)
        east_face, east_column = across(near, 1)
        at_west = column == 0
        at_east = column == 3
        write_pick(n * STACK, near, column, True)
        write_pick(
            (2 * SIDES + n) * STACK,
            jnp.where(at_west, west_face, near),
            jnp.where(at_west, west_column, 2),
            at_west,
        )
        write_pick((SIDES + n) * STACK, near, column, False)
        write_pick(
            (3 * SIDES + n) * STACK,
            jnp.where(at_east, east_face, near),
            jnp.where(at_east, east_column, 1),
            at_east,
        )
        return 0

    lax.fori_loop(0, SIDES, pick_side, 0)

    def tap1(x, a, b):
        return dot_t(x, w1[a, b, :, 0:WIDE])

    def tap1_coarse(x, a, b):
        return dot_t(x, w1[a, b, :, w1.shape[3] - WIDE :])

    def tap2(x, a, b):
        return dot(x, w2[a, b])

    def conv_own(src, tap, f, b):
        z = tap(src[f, 0:PIX], 0, b)
        z = z + tap(src[f, COLS : COLS + PIX], 1, b)
        return z + tap(src[f, 2 * COLS : 2 * COLS + PIX], 2, b)

    for copy in loads[6:]:
        copy.wait()
    parts = []
    for b in range(3):
        c0, c1, c2 = [tap1_coarse(up[...], a, b) for a in range(3)]
        parts.append((c1 + c2, c0 + c1 + c2, c0 + c1))
    for k in range(3):
        cclass[k] = from_west(parts[0][k]) + parts[1][k] + from_east(parts[2][k]) + b1[...]

    def own1(f, _):
        z = from_west(conv_own(xp, tap1, f, 0)) + conv_own(xp, tap1, f, 1) + from_east(conv_own(xp, tap1, f, 2))
        at = pl.ds(pl.multiple_of(f * COLS, COLS), COLS)
        for i in range(ROWS):
            k = 0 if i == 0 else 2 if i == ROWS - 1 else 1
            acc[f, i * COLS : (i + 1) * COLS] = z[i * COLS : (i + 1) * COLS] + cclass[k, at]
        return 0

    lax.fori_loop(0, FACES, own1, 0)

    column = column_of((COLS, C))
    border = (column == 0) | (column == COLS - 1)

    def inside(f, _):
        for i in range(1, ROWS - 1):
            h = silu(acc[f, i * COLS : (i + 1) * COLS])
            hp[f, (i + 1) * COLS : (i + 2) * COLS] = jnp.where(border, 0.0, h).astype(bf16)
        return 0

    lax.fori_loop(0, FACES, inside, 0)

    def own2(f, _):
        z = from_west(conv_own(hp, tap2, f, 0)) + conv_own(hp, tap2, f, 1) + from_east(conv_own(hp, tap2, f, 2))
        p = pf[f, :, 0:C]
        denoised = skip_gain * p + output_gain * (z + b2[...])
        z = p + step_ratio * (p - denoised)
        acc2[f] = z
        for i in range(2, ROWS - 2):
            out[f, i] = z[i * COLS : (i + 1) * COLS].astype(bf16)
        return 0

    lax.fori_loop(0, FACES, own2, 0)
    for k, j in ((0, 0), (1, COLS - 1)):
        for f in range(FACES):
            line = [(FIRST + i, acc[f, i * COLS + j : i * COLS + j + 1, :]) for i in range(1, ROWS - 1)]
            own_line[k, f * STACK : (f + 1) * STACK] = spread(line, STACK)

    for copy in sent[-4:]:
        copy.wait_recv()
    for k in range(2):
        c = craw[k].astype(f32)
        for f in range(FACES):
            rows1[k, f, 2] = widened([c[n : n + 1] for n in range(f * COARSE, (f + 1) * COARSE)])

    tops, ends, after, before = [], [], [], []
    for f in range(FACES):
        face = g * FACES + f
        n, s = jnp.where(first, ns[0, face], f), jnp.where(last, ns[1, face], f)
        flip_n, flip_s = code[0, face], code[1, face]
        k = jnp.where(first, 2 * flip_n, 0)
        r = jnp.where(k == 0, 1, 0)
        tops.append((rows1[k, n, r], rows1[k, n, 2]))
        k = jnp.where(last, 1 + 2 * flip_s, 1)
        r = jnp.where(k == 1, 0, 1)
        ends.append((rows1[k, s, r], rows1[k, s, 2]))
        s = jnp.where(first, ns[1, face], f)
        k = jnp.where(first, 2 - 2 * flip_s, 2)
        r = jnp.where(k == 0, 1, 0)
        after.append((rows1[k, s, r], rows1[k, s, 2]))
        n = jnp.where(last, ns[0, face], f)
        k = jnp.where(last, 3 - 2 * flip_n, 3)
        r = jnp.where(k == 1, 0, 1)
        before.append((rows1[k, n, r], rows1[k, n, 2]))

    def landed(k, r):
        return [(rows1[k, f, r], rows1[k, f, 2]) for f in range(FACES)]

    ROW = FACES * COLS
    stacks = (
        landed(0, 0) + tops + before,
        landed(0, 1) + landed(1, 0),
        after + landed(1, 1) + ends,
    )
    taps = (tap1, tap1_coarse)
    z_rows = [[], [], [], []]
    for b in range(3):
        y = [
            sum(tap(jnp.concatenate([r[k] for r in stacks[a]], axis=0), a, b) for k, tap in enumerate(taps))
            for a in range(3)
        ]
        z_rows[0].append(y[0][0:ROW] + y[1][0:ROW] + y[2][0:ROW])
        z_rows[1].append(y[0][2 * ROW :] + y[1][ROW:] + y[2][ROW : 2 * ROW])
        z_rows[2].append(y[0][ROW : 2 * ROW])
        z_rows[3].append(y[2][2 * ROW :])
    for k, z in enumerate(z_rows):
        z = from_west(z[0]) + z[1] + from_east(z[2])
        zrow[k] = z if k >= 2 else z + b1[...]

    for copy in sent[:-4]:
        copy.wait_recv()
    table = cols[...].reshape(lines, LINE)
    half = FACES * STACK
    sides = SIDES * STACK
    y = unpack_outer(dot(pick[0].reshape(8 * sides, lines), table[:, 0:WIDE]))
    z = unpack_inner(dot(pick[1].reshape(8 * sides, lines)[2 * sides :], table[:, LINE - WIDE :]))
    picked = [jnp.concatenate([y[0 : 2 * sides], y[2 * sides : 4 * sides] + z[0 : 2 * sides]], axis=0)]
    picked.append(pltpu.roll(y[4 * sides :] + z[2 * sides :], 64, 1))
    picked = [x.astype(bf16) for x in picked]

    v_side, v_near = [], []
    for b in range(3):
        lines_b = []
        for chosen in picked:
            if b == 0:
                beside = [chosen[0:half], chosen[2 * sides : 3 * sides]]
            elif b == 1:
                beside = [chosen[sides : 2 * sides]]
            else:
                beside = [chosen[half : 2 * half], chosen[3 * sides :]]
            lines_b.append(jnp.concatenate(beside, axis=0))
        y = [sum(tap(x, a, b) for tap, x in zip(taps, lines_b)) for a in range(3)]
        if b != 1:
            v_side.append([x[0:half] for x in y])
            y = [x[half:] for x in y]
        v_near.append(y)
    for k in range(2):
        zcol[k] = along_rows(*v_side[k])
    near = along_rows(*[v_near[0][a] + v_near[1][a] + v_near[2][a] for a in range(3)]) + b1[...]
    near = silu(near)
    place = lax.rem(lax.broadcasted_iota(i32, near.shape, 0), STACK)
    low = jnp.where(first, 0.0, pltpu.roll(near, 2, 0))
    high = jnp.where(last, 0.0, pltpu.roll(near, near.shape[0] - 2, 0))
    near = jnp.where(place == FIRST - 1, low, jnp.where(place == FIRST + ROWS, high, near))
    near = near.astype(bf16)

    def with_sides(z, f, q):
        west = zcol[0, pl.ds(f * STACK + q, 1), :]
        east = zcol[1, pl.ds(f * STACK + q, 1), :]
        z = z + jnp.where(column == 0, jnp.broadcast_to(west, z.shape), 0.0)
        return z + jnp.where(column == COLS - 1, jnp.broadcast_to(east, z.shape), 0.0)

    def activate(f):
        at = pl.ds(f * COLS, COLS)
        rows2[0, f] = silu(with_sides(zrow[0, at], f, 1)).astype(bf16)
        rows2[1, f] = silu(with_sides(zrow[1, at], f, STACK - 2)).astype(bf16)
        rows2[2, f] = silu(with_sides(acc[f, 0:COLS] + zrow[2, at], f, FIRST)).astype(bf16)
        z = acc[f, PIX - COLS : PIX] + zrow[3, at]
        rows2[3, f] = silu(with_sides(z, f, FIRST + ROWS - 1)).astype(bf16)

    for f in range(FACES):
        activate(f)
    place = lax.rem(lax.broadcasted_iota(i32, (half, C), 0), STACK)
    between = (place > FIRST) & (place < FIRST + ROWS - 1)
    west, east = [
        jnp.where(between, silu(own_line[k] + zcol[k]), 0.0).astype(bf16) for k in range(2)
    ]
    tops, ends = [], []
    for f in range(FACES):
        face = g * FACES + f
        n, s = jnp.where(first, ns[0, face], f), jnp.where(last, ns[1, face], f)
        tops.append(rows2[jnp.where(first, 2 * code[0, face], 0), n])
        ends.append(rows2[jnp.where(last, 1 + 2 * code[1, face], 1), s])
    top, end = [[rows2[k, f] for f in range(FACES)] for k in (2, 3)]
    stacks = (tops + top, top + end, end + ends)
    lines = ([near[0:half], west], [west, east], [near[half : 2 * half], east])
    z_rows, v = [[], [], [], []], []
    for b in range(3):
        y = [tap2(jnp.concatenate(stacks[a] + lines[b], axis=0), a, b) for a in range(3)]
        z_rows[0].append(y[0][0:ROW] + y[1][0:ROW])
        z_rows[1].append(y[0][ROW : 2 * ROW])
        z_rows[2].append(y[2][0:ROW])
        z_rows[3].append(y[1][ROW : 2 * ROW] + y[2][ROW : 2 * ROW])
        v.append([[x[2 * ROW + k * half : 2 * ROW + (k + 1) * half] for x in y] for k in range(2)])
    for k, z in enumerate(z_rows):
        zrow[k] = from_west(z[0]) + z[1] + from_east(z[2])
    z_line[0] = along_rows(*[v[0][0][a] + v[1][0][a] for a in range(3)])
    z_line[1] = along_rows(*v[0][1])
    z_line[2] = along_rows(*v[2][1])
    z_line[3] = along_rows(*[v[2][0][a] + v[1][1][a] for a in range(3)])

    few = lax.broadcasted_iota(i32, (8, C), 0)

    def finish(f):
        at = pl.ds(f * COLS, COLS)
        for i in range(ROWS):
            line = [
                jnp.broadcast_to(z_line[k, pl.ds(f * STACK + FIRST + i, 1), :], (8, C)) for k in range(4)
            ]
            west = jnp.where(few == 0, line[0], jnp.where(few == 1, line[1], 0.0))
            east = jnp.where(few == 6, line[2], jnp.where(few == 7, line[3], 0.0))
            r = i * COLS
            if 2 <= i < ROWS - 2:
                out[f, i, 0:8] = (acc2[f, r : r + 8] + feature_gain * west).astype(bf16)
                out[f, i, COLS - 8 :] = (acc2[f, r + COLS - 8 : r + COLS] + feature_gain * east).astype(bf16)
                continue
            z = zrow[i if i < 2 else i - ROWS + 4, at]
            z = jnp.concatenate([z[0:8] + west, z[8 : COLS - 8], z[COLS - 8 :] + east], axis=0)
            out[f, i] = (acc2[f, r : r + COLS] + feature_gain * z).astype(bf16)

    for f in range(FACES):
        finish(f)
    for copy in sent:
        copy.wait_send()


def on_device(groups, tiles, sample, noise, coarse, w1, b1, w2, b2, ns, we, code):
    C = sample.shape[-1]
    w1 = jnp.swapaxes(w1, 2, 3)
    operands = (sample, noise, coarse, ns.T, we.T, code.T, w1, b1.reshape(1, C), w2, b2.reshape(1, C))
    return pl.pallas_call(
        functools.partial(kernel, groups, tiles),
        out_shape=jax.ShapeDtypeStruct(sample.shape, bf16),
        in_specs=[pl.BlockSpec(memory_space=pltpu.HBM)] * len(operands),
        out_specs=pl.BlockSpec(memory_space=pltpu.VMEM),
        scratch_shapes=[
            (pltpu.SMEM if x.dtype == i32 else pltpu.VMEM)(x.shape, x.dtype) for x in operands
        ]
        + [
            pltpu.VMEM((FACES, PIX, WIDE), f32),
            pltpu.VMEM((FACES, PIX, C), f32),
            pltpu.VMEM((FACES, PIX, C), f32),
            pltpu.VMEM((2, FACES * STACK, C), f32),
            pltpu.VMEM((4, FACES * STACK, C), f32),
            pltpu.VMEM((FACES, PIX + 2 * COLS, WIDE), bf16),
            pltpu.VMEM((FACES, PIX + 2 * COLS, C), bf16),
            pltpu.VMEM((FACES * COLS, WIDE), bf16),
            pltpu.VMEM((3, FACES * COLS, C), f32),
            pltpu.VMEM((groups, BLOCKS, 16, LINE), bf16),
            pltpu.VMEM((2, 16, LINE), bf16),
            pltpu.VMEM((3, 16, WIDE), bf16),
            pltpu.VMEM((4, FACES, 3, COLS, WIDE), bf16),
            pltpu.VMEM((4, FACES, COLS, C), bf16),
            pltpu.VMEM((2, 2, 4 * SIDES * STACK, groups * BLOCKS * 16), bf16),
            pltpu.VMEM((2, FACES * STACK, C), f32),
            pltpu.VMEM((4, FACES * COLS, C), f32),
            pltpu.SemaphoreType.DMA((len(operands),)),
            pltpu.SemaphoreType.DMA((15,)),
            pltpu.SemaphoreType.DMA((15,)),
        ],
        compiler_params=pltpu.CompilerParams(
            collective_id=0, has_side_effects=True, vmem_limit_bytes=32 * 2**20
        ),
    )(*[pltpu.with_memory_space_constraint(x, pltpu.HBM) for x in operands])


def solution(mesh):
    return jax.shard_map(
        functools.partial(on_device, mesh.shape["face"], mesh.shape["tile"]),
        mesh=mesh,
        in_specs=(P("face", "tile", None, None),) * 3 + (P(),) * 7,
        out_specs=P("face", "tile", None, None),
        check_vma=False,
    )
```

```python
import functools

import jax
import jax.numpy as jnp
from jax import lax
from jax.experimental import pallas as pl
from jax.experimental.pallas import tpu as pltpu
from jax.sharding import PartitionSpec as P

MESH = pl.DeviceIdType.MESH
f32 = jnp.float32
bf16 = jnp.bfloat16
i32 = jnp.int32

noise_gain = 0.6
input_gain = 0.7071067811865476
skip_gain = 0.5
output_gain = 0.7071067811865476
step_ratio = -0.4
feature_gain = -step_ratio * output_gain

UP = 8
FACES = 3
ROWS = 8
COLS = 32
COARSE = COLS // UP
PIX = ROWS * COLS
SIDES = 2 * FACES
WIDE = 256

BLOCKS = 6
FACE, OVER, UNDER = 1, 4, 5
LINE = 384
CORNER = 4 * FACES
STACK = 16
FIRST = 4


def dot(a, b):
    return jnp.dot(a, b, preferred_element_type=f32)


def dot_t(a, b):
    return lax.dot_general(a, b, (((1,), (1,)), ((), ())), preferred_element_type=f32)


def column_of(shape):
    return lax.rem(lax.broadcasted_iota(i32, shape, 0), COLS)


def from_west(z):
    return jnp.where(column_of(z.shape) == 0, 0.0, pltpu.roll(z, 1, 0))


def from_east(z):
    return jnp.where(column_of(z.shape) == COLS - 1, 0.0, pltpu.roll(z, z.shape[0] - 1, 0))


def along_rows(v0, v1, v2):
    return pltpu.roll(v0, 1, 0) + v1 + pltpu.roll(v2, v2.shape[0] - 1, 0)


def silu(u):
    return 0.5 * u * (1.0 + jnp.tanh(0.5 * u))


def spread(rows, count):
    width = rows[0][1].shape[1]
    place = lax.broadcasted_iota(i32, (count, width), 0)
    out = jnp.zeros((count, width), f32)
    for at, row in rows:
        out = jnp.where(place == at, jnp.broadcast_to(row, (count, width)), out)
    return out


def pack(outer, inner):
    rest = outer[:, 128:WIDE] + pltpu.roll(inner[:, 128:WIDE], 64, 1)
    return jnp.concatenate([outer[:, 0:128], rest, inner[:, 0:128]], axis=1).astype(bf16)


def unpack_outer(y):
    lane = lax.broadcasted_iota(i32, y.shape, 1)
    return jnp.where(lane < LINE // 2, y, 0.0)


def unpack_inner(y):
    return unpack_outer(jnp.concatenate([y[:, 128:], pltpu.roll(y[:, 0:128], 64, 1)], axis=1))


def widened(each):
    return jnp.concatenate([jnp.broadcast_to(e, (UP, WIDE)) for e in each], axis=0).astype(bf16)


def kernel(
    groups,
    tiles,
    sample_hbm,
    noise_hbm,
    coarse_hbm,
    ns_hbm,
    we_hbm,
    code_hbm,
    w1_hbm,
    b1_hbm,
    w2_hbm,
    b2_hbm,
    out,
    sample,
    noise,
    coarse,
    ns,
    we,
    code,
    w1,
    b1,
    w2,
    b2,
    pf,
    acc,
    acc2,
    own_line,
    z_line,
    xp,
    hp,
    up,
    cclass,
    cols,
    corner,
    craw,
    rows1,
    rows2,
    pick,
    zcol,
    zrow,
    load_sem,
    send_sem,
    recv_sem,
):
    g = lax.axis_index("face")
    t = lax.axis_index("tile")
    above = lax.rem(t + tiles - 1, tiles)
    below = lax.rem(t + 1, tiles)
    first = t == 0
    last = t == tiles - 1
    C = acc.shape[2]
    lines = groups * BLOCKS * 16

    barrier = pltpu.get_barrier_semaphore()
    for d in (2, 1, 3, 0):
        for k, there in enumerate((t, above, below)):
            if d or k:
                pl.semaphore_signal(
                    barrier, inc=1, device_id=(lax.rem(g + d, groups), there), device_id_type=MESH
                )

    loads = [
        pltpu.make_async_copy(src, dst, load_sem.at[i])
        for i, (src, dst) in enumerate(
            [
                (sample_hbm, sample),
                (noise_hbm, noise),
                (coarse_hbm, coarse),
                (ns_hbm, ns),
                (we_hbm, we),
                (code_hbm, code),
                (w1_hbm, w1),
                (b1_hbm, b1),
                (w2_hbm, w2),
                (b2_hbm, b2),
            ]
        )
    ]
    for copy in loads[:6]:
        copy.start()

    for f in range(FACES):
        zero_row = jnp.zeros((COLS, WIDE), bf16)
        xp[f, 0:COLS] = zero_row
        xp[f, COLS + PIX : 2 * COLS + PIX] = zero_row
        xp[f, COLS : COLS + PIX, 128:WIDE] = jnp.zeros((PIX, WIDE - 128), bf16)
        pf[f, :, 128:WIDE] = jnp.zeros((PIX, WIDE - 128), f32)
        hp[f, 0 : 2 * COLS] = jnp.zeros((2 * COLS, C), bf16)
        hp[f, PIX : PIX + 2 * COLS] = jnp.zeros((2 * COLS, C), bf16)

    for copy in loads[:3]:
        copy.wait()
    for f in range(FACES):
        p = sample[f].astype(f32) + noise_gain * noise[f].astype(f32)
        p = p.reshape(PIX, C)
        pf[f, :, 0:C] = p
        xp[f, COLS : COLS + PIX, 0:C] = (p * input_gain).astype(bf16)
        for r in range(2):
            rows1[2, f, r] = xp[f, (1 + r) * COLS : (2 + r) * COLS]
            rows1[3, f, r] = xp[f, PIX - COLS + r * COLS : PIX + r * COLS]
    raw, tops, ends = [([], []) for _ in range(3)]
    all_raw = []
    blank = jnp.zeros((COARSE, WIDE - C), f32)
    for f in range(FACES):
        c = coarse[f, 0].astype(f32)
        line = jnp.concatenate([c, blank], axis=1)
        c = jnp.concatenate([blank, c], axis=1)
        each = [c[j : j + 1] for j in range(COARSE)]
        wide = widened(each)
        all_raw += [(f * COARSE + j, each[j]) for j in range(COARSE)]
        up[f * COLS : (f + 1) * COLS] = wide
        rows1[2, f, 2] = wide
        rows1[3, f, 2] = wide
        for inner, j in ((0, 0), (1, COARSE - 1)):
            raw[inner].append((f, line[j : j + 1]))
            tops[inner].append((CORNER + f, line[j : j + 1]))
            ends[inner].append((CORNER + f, line[j : j + 1]))
        halves = ([], [])
        for inner, high, j in ((0, 0, 0), (0, 1, COLS - 1), (1, 0, 1), (1, 1, COLS - 2)):
            line_j = [pf[f, i * COLS + j : i * COLS + j + 1, :] * input_gain for i in range(ROWS)]
            halves[inner].append(spread(list(enumerate(line_j)), ROWS))
            tops[inner].extend((4 * f + 2 * high + r, line_j[r]) for r in range(2))
            ends[inner].extend((4 * f + 2 * high + r, line_j[ROWS - 2 + r]) for r in range(2))
        cols[g, FACE + f] = pack(*[jnp.concatenate(h, axis=0) for h in halves])
    cols[g, 0] = pack(*[spread(x, 16) for x in raw])
    craw[2] = spread(all_raw, 16).astype(bf16)
    corner[0] = pack(*[spread(x, 16) for x in tops])
    corner[1] = pack(*[spread(x, 16) for x in ends])

    sent = []

    def add(src, dst, there):
        n = len(sent)
        sent.append(
            pltpu.make_async_remote_copy(
                src_ref=src,
                dst_ref=dst,
                send_sem=send_sem.at[n],
                recv_sem=recv_sem.at[n],
                device_id=there,
                device_id_type=MESH,
            )
        )

    table = cols.at[g, pl.ds(0, OVER)]
    over = cols.at[g, OVER]
    under = cols.at[g, UNDER]
    for d in (2, 1, 3):
        far = lax.rem(g + d, groups)
        add(corner.at[0], under, (far, above))
        add(corner.at[1], over, (far, below))
        add(table, table, (far, t))
    add(corner.at[0], under, (g, above))
    add(corner.at[1], over, (g, below))
    both = pl.ds(0, 2)
    add(rows1.at[2, :, both], rows1.at[1, :, both], (g, above))
    add(rows1.at[3, :, both], rows1.at[0, :, both], (g, below))
    add(craw.at[2], craw.at[1], (g, above))
    add(craw.at[2], craw.at[0], (g, below))

    pl.semaphore_wait(barrier, 3 * groups - 1)
    for copy in sent:
        copy.start()
    for copy in loads[6:]:
        copy.start()
    for copy in loads[3:6]:
        copy.wait()

    lane = lax.broadcasted_iota(i32, (STACK, lines), 1)
    place = lax.broadcasted_iota(i32, (STACK, lines), 0)

    def split(face):
        group = sum((face >= FACES * k).astype(i32) for k in range(1, groups))
        return group, face - FACES * group

    def across(face, side):
        edge = code[2 + side, face]
        return we[side, face], 3 * jnp.where(side == 1, edge, 1 - edge)

    def write_pick(at, face, column, beyond):
        group, f = split(face)
        base = group * (BLOCKS * 16)
        inner = (column == 1) | (column == 2)
        high = (column >= 2).astype(i32)

        def line(ff, row):
            if row < 0:
                return base + OVER * 16 + ff * 4 + high * 2 + 2 + row
            if row >= ROWS:
                return base + UNDER * 16 + ff * 4 + high * 2 + row - ROWS
            return base + (FACE + ff) * 16 + high * 8 + row

        def condition(ff, row):
            if row < 0:
                return base + OVER * 16 + CORNER + ff
            if row >= ROWS:
                return base + UNDER * 16 + CORNER + ff
            return base + ff

        n, s = ns[0, face], ns[1, face]
        flip_n, flip_s = code[0, face] == 1, code[1, face] == 1
        for part, where in enumerate((line, condition)):
            north = jnp.where(beyond, -1, jnp.where(flip_n, where(n, 0), where(n, -1)))
            south = jnp.where(beyond, -1, jnp.where(flip_s, where(s, ROWS - 1), where(s, ROWS)))
            target = jnp.broadcast_to(where(f, 0), place.shape)
            if part == 0:
                target = target + place - FIRST
            for q, value in (
                (0, where(f, -2)),
                (1, where(f, -1)),
                (2, jnp.where(first, -1, where(f, 0))),
                (3, jnp.where(first, north, where(f, -1))),
                (12, jnp.where(last, south, where(f, ROWS))),
                (13, jnp.where(last, -1, where(f, ROWS - 1))),
                (14, where(f, ROWS)),
                (15, where(f, ROWS + 1)),
            ):
                target = jnp.where(place == q, value, target)
            at = pl.multiple_of(at, STACK)
            second = high == 1 if part else inner
            for k, chosen in ((0, jnp.where(second, -1, target)), (1, jnp.where(second, target, -1))):
                pick[k, part, pl.ds(at, STACK), :] = jnp.where(lane == chosen, 1.0, 0.0).astype(bf16)

    def pick_side(n, _):
        side = (n >= FACES).astype(i32)
        face = g * FACES + n - FACES * side
        near, column = across(face, side)
        west_face, west_column = across(near, 0)
        east_face, east_column = across(near, 1)
        at_west = column == 0
        at_east = column == 3
        write_pick(n * STACK, near, column, True)
        write_pick(
            (2 * SIDES + n) * STACK,
            jnp.where(at_west, west_face, near),
            jnp.where(at_west, west_column, 2),
            at_west,
        )
        write_pick((SIDES + n) * STACK, near, column, False)
        write_pick(
            (3 * SIDES + n) * STACK,
            jnp.where(at_east, east_face, near),
            jnp.where(at_east, east_column, 1),
            at_east,
        )
        return 0

    lax.fori_loop(0, SIDES, pick_side, 0)

    def tap1(x, a, b):
        return dot_t(x, w1[a, b, :, 0:WIDE])

    def tap1_coarse(x, a, b):
        return dot_t(x, w1[a, b, :, w1.shape[3] - WIDE :])

    def tap2(x, a, b):
        return dot(x, w2[a, b])

    def conv_own(src, tap, f, b):
        z = tap(src[f, 0:PIX], 0, b)
        z = z + tap(src[f, COLS : COLS + PIX], 1, b)
        return z + tap(src[f, 2 * COLS : 2 * COLS + PIX], 2, b)

    for copy in loads[6:]:
        copy.wait()
    parts = []
    for b in range(3):
        c0, c1, c2 = [tap1_coarse(up[...], a, b) for a in range(3)]
        parts.append((c1 + c2, c0 + c1 + c2, c0 + c1))
    for k in range(3):
        cclass[k] = from_west(parts[0][k]) + parts[1][k] + from_east(parts[2][k]) + b1[...]

    def own1(f, _):
        z = from_west(conv_own(xp, tap1, f, 0)) + conv_own(xp, tap1, f, 1) + from_east(conv_own(xp, tap1, f, 2))
        at = pl.ds(pl.multiple_of(f * COLS, COLS), COLS)
        for i in range(ROWS):
            k = 0 if i == 0 else 2 if i == ROWS - 1 else 1
            acc[f, i * COLS : (i + 1) * COLS] = z[i * COLS : (i + 1) * COLS] + cclass[k, at]
        return 0

    lax.fori_loop(0, FACES, own1, 0)

    column = column_of((COLS, C))
    border = (column == 0) | (column == COLS - 1)

    def inside(f, _):
        for i in range(1, ROWS - 1):
            h = silu(acc[f, i * COLS : (i + 1) * COLS])
            hp[f, (i + 1) * COLS : (i + 2) * COLS] = jnp.where(border, 0.0, h).astype(bf16)
        return 0

    lax.fori_loop(0, FACES, inside, 0)

    def own2(f, _):
        z = from_west(conv_own(hp, tap2, f, 0)) + conv_own(hp, tap2, f, 1) + from_east(conv_own(hp, tap2, f, 2))
        p = pf[f, :, 0:C]
        denoised = skip_gain * p + output_gain * (z + b2[...])
        z = p + step_ratio * (p - denoised)
        acc2[f] = z
        for i in range(2, ROWS - 2):
            out[f, i] = z[i * COLS : (i + 1) * COLS].astype(bf16)
        return 0

    lax.fori_loop(0, FACES, own2, 0)
    for k, j in ((0, 0), (1, COLS - 1)):
        for f in range(FACES):
            line = [(FIRST + i, acc[f, i * COLS + j : i * COLS + j + 1, :]) for i in range(1, ROWS - 1)]
            own_line[k, f * STACK : (f + 1) * STACK] = spread(line, STACK)

    for copy in sent[-4:]:
        copy.wait_recv()
    for k in range(2):
        c = craw[k].astype(f32)
        for f in range(FACES):
            rows1[k, f, 2] = widened([c[n : n + 1] for n in range(f * COARSE, (f + 1) * COARSE)])

    tops, ends, after, before = [], [], [], []
    for f in range(FACES):
        face = g * FACES + f
        n, s = jnp.where(first, ns[0, face], f), jnp.where(last, ns[1, face], f)
        flip_n, flip_s = code[0, face], code[1, face]
        k = jnp.where(first, 2 * flip_n, 0)
        r = jnp.where(k == 0, 1, 0)
        tops.append((rows1[k, n, r], rows1[k, n, 2]))
        k = jnp.where(last, 1 + 2 * flip_s, 1)
        r = jnp.where(k == 1, 0, 1)
        ends.append((rows1[k, s, r], rows1[k, s, 2]))
        s = jnp.where(first, ns[1, face], f)
        k = jnp.where(first, 2 - 2 * flip_s, 2)
        r = jnp.where(k == 0, 1, 0)
        after.append((rows1[k, s, r], rows1[k, s, 2]))
        n = jnp.where(last, ns[0, face], f)
        k = jnp.where(last, 3 - 2 * flip_n, 3)
        r = jnp.where(k == 1, 0, 1)
        before.append((rows1[k, n, r], rows1[k, n, 2]))

    def landed(k, r):
        return [(rows1[k, f, r], rows1[k, f, 2]) for f in range(FACES)]

    ROW = FACES * COLS
    stacks = (
        landed(0, 0) + tops + before,
        landed(0, 1) + landed(1, 0),
        after + landed(1, 1) + ends,
    )
    taps = (tap1, tap1_coarse)
    z_rows = [[], [], [], []]
    for b in range(3):
        y = [
            sum(tap(jnp.concatenate([r[k] for r in stacks[a]], axis=0), a, b) for k, tap in enumerate(taps))
            for a in range(3)
        ]
        z_rows[0].append(y[0][0:ROW] + y[1][0:ROW] + y[2][0:ROW])
        z_rows[1].append(y[0][2 * ROW :] + y[1][ROW:] + y[2][ROW : 2 * ROW])
        z_rows[2].append(y[0][ROW : 2 * ROW])
        z_rows[3].append(y[2][2 * ROW :])
    for k, z in enumerate(z_rows):
        z = from_west(z[0]) + z[1] + from_east(z[2])
        zrow[k] = z if k >= 2 else z + b1[...]

    for copy in sent[:-4]:
        copy.wait_recv()
    table = cols[...].reshape(lines, LINE)
    half = FACES * STACK
    sides = SIDES * STACK
    y = unpack_outer(dot(pick[0].reshape(8 * sides, lines), table[:, 0:WIDE]))
    z = unpack_inner(dot(pick[1].reshape(8 * sides, lines)[2 * sides :], table[:, LINE - WIDE :]))
    picked = [jnp.concatenate([y[0 : 2 * sides], y[2 * sides : 4 * sides] + z[0 : 2 * sides]], axis=0)]
    picked.append(pltpu.roll(y[4 * sides :] + z[2 * sides :], 64, 1))
    picked = [x.astype(bf16) for x in picked]

    v_side, v_near = [], []
    for b in range(3):
        lines_b = []
        for chosen in picked:
            if b == 0:
                beside = [chosen[0:half], chosen[2 * sides : 3 * sides]]
            elif b == 1:
                beside = [chosen[sides : 2 * sides]]
            else:
                beside = [chosen[half : 2 * half], chosen[3 * sides :]]
            lines_b.append(jnp.concatenate(beside, axis=0))
        y = [sum(tap(x, a, b) for tap, x in zip(taps, lines_b)) for a in range(3)]
        if b != 1:
            v_side.append([x[0:half] for x in y])
            y = [x[half:] for x in y]
        v_near.append(y)
    for k in range(2):
        zcol[k] = along_rows(*v_side[k])
    near = along_rows(*[v_near[0][a] + v_near[1][a] + v_near[2][a] for a in range(3)]) + b1[...]
    near = silu(near)
    place = lax.rem(lax.broadcasted_iota(i32, near.shape, 0), STACK)
    low = jnp.where(first, 0.0, pltpu.roll(near, 2, 0))
    high = jnp.where(last, 0.0, pltpu.roll(near, near.shape[0] - 2, 0))
    near = jnp.where(place == FIRST - 1, low, jnp.where(place == FIRST + ROWS, high, near))
    near = near.astype(bf16)

    def with_sides(z, f, q):
        west = zcol[0, pl.ds(f * STACK + q, 1), :]
        east = zcol[1, pl.ds(f * STACK + q, 1), :]
        z = z + jnp.where(column == 0, jnp.broadcast_to(west, z.shape), 0.0)
        return z + jnp.where(column == COLS - 1, jnp.broadcast_to(east, z.shape), 0.0)

    def activate(f):
        at = pl.ds(f * COLS, COLS)
        rows2[0, f] = silu(with_sides(zrow[0, at], f, 1)).astype(bf16)
        rows2[1, f] = silu(with_sides(zrow[1, at], f, STACK - 2)).astype(bf16)
        rows2[2, f] = silu(with_sides(acc[f, 0:COLS] + zrow[2, at], f, FIRST)).astype(bf16)
        z = acc[f, PIX - COLS : PIX] + zrow[3, at]
        rows2[3, f] = silu(with_sides(z, f, FIRST + ROWS - 1)).astype(bf16)

    for f in range(FACES):
        activate(f)
    place = lax.rem(lax.broadcasted_iota(i32, (half, C), 0), STACK)
    between = (place > FIRST) & (place < FIRST + ROWS - 1)
    west, east = [
        jnp.where(between, silu(own_line[k] + zcol[k]), 0.0).astype(bf16) for k in range(2)
    ]
    tops, ends = [], []
    for f in range(FACES):
        face = g * FACES + f
        n, s = jnp.where(first, ns[0, face], f), jnp.where(last, ns[1, face], f)
        tops.append(rows2[jnp.where(first, 2 * code[0, face], 0), n])
        ends.append(rows2[jnp.where(last, 1 + 2 * code[1, face], 1), s])
    top, end = [[rows2[k, f] for f in range(FACES)] for k in (2, 3)]
    stacks = (tops + top, top + end, end + ends)
    lines = ([near[0:half], west], [west, east], [near[half : 2 * half], east])
    z_rows, v = [[], [], [], []], []
    for b in range(3):
        y = [tap2(jnp.concatenate(stacks[a] + lines[b], axis=0), a, b) for a in range(3)]
        z_rows[0].append(y[0][0:ROW] + y[1][0:ROW])
        z_rows[1].append(y[0][ROW : 2 * ROW])
        z_rows[2].append(y[2][0:ROW])
        z_rows[3].append(y[1][ROW : 2 * ROW] + y[2][ROW : 2 * ROW])
        v.append([[x[2 * ROW + k * half : 2 * ROW + (k + 1) * half] for x in y] for k in range(2)])
    for k, z in enumerate(z_rows):
        zrow[k] = from_west(z[0]) + z[1] + from_east(z[2])
    z_line[0] = along_rows(*[v[0][0][a] + v[1][0][a] for a in range(3)])
    z_line[1] = along_rows(*v[0][1])
    z_line[2] = along_rows(*v[2][1])
    z_line[3] = along_rows(*[v[2][0][a] + v[1][1][a] for a in range(3)])

    few = lax.broadcasted_iota(i32, (8, C), 0)

    def finish(f):
        at = pl.ds(f * COLS, COLS)
        for i in range(ROWS):
            line = [
                jnp.broadcast_to(z_line[k, pl.ds(f * STACK + FIRST + i, 1), :], (8, C)) for k in range(4)
            ]
            west = jnp.where(few == 0, line[0], jnp.where(few == 1, line[1], 0.0))
            east = jnp.where(few == 6, line[2], jnp.where(few == 7, line[3], 0.0))
            r = i * COLS
            if 2 <= i < ROWS - 2:
                out[f, i, 0:8] = (acc2[f, r : r + 8] + feature_gain * west).astype(bf16)
                out[f, i, COLS - 8 :] = (acc2[f, r + COLS - 8 : r + COLS] + feature_gain * east).astype(bf16)
                continue
            z = zrow[i if i < 2 else i - ROWS + 4, at]
            z = jnp.concatenate([z[0:8] + west, z[8 : COLS - 8], z[COLS - 8 :] + east], axis=0)
            out[f, i] = (acc2[f, r : r + COLS] + feature_gain * z).astype(bf16)

    for f in range(FACES):
        finish(f)
    for copy in sent:
        copy.wait_send()


def on_device(groups, tiles, sample, noise, coarse, w1, b1, w2, b2, ns, we, code):
    C = sample.shape[-1]
    w1 = jnp.swapaxes(w1, 2, 3)
    operands = (sample, noise, coarse, ns.T, we.T, code.T, w1, b1.reshape(1, C), w2, b2.reshape(1, C))
    return pl.pallas_call(
        functools.partial(kernel, groups, tiles),
        out_shape=jax.ShapeDtypeStruct(sample.shape, bf16),
        in_specs=[pl.BlockSpec(memory_space=pltpu.HBM)] * len(operands),
        out_specs=pl.BlockSpec(memory_space=pltpu.VMEM),
        scratch_shapes=[
            (pltpu.SMEM if x.dtype == i32 else pltpu.VMEM)(x.shape, x.dtype) for x in operands
        ]
        + [
            pltpu.VMEM((FACES, PIX, WIDE), f32),
            pltpu.VMEM((FACES, PIX, C), f32),
            pltpu.VMEM((FACES, PIX, C), f32),
            pltpu.VMEM((2, FACES * STACK, C), f32),
            pltpu.VMEM((4, FACES * STACK, C), f32),
            pltpu.VMEM((FACES, PIX + 2 * COLS, WIDE), bf16),
            pltpu.VMEM((FACES, PIX + 2 * COLS, C), bf16),
            pltpu.VMEM((FACES * COLS, WIDE), bf16),
            pltpu.VMEM((3, FACES * COLS, C), f32),
            pltpu.VMEM((groups, BLOCKS, 16, LINE), bf16),
            pltpu.VMEM((2, 16, LINE), bf16),
            pltpu.VMEM((3, 16, WIDE), bf16),
            pltpu.VMEM((4, FACES, 3, COLS, WIDE), bf16),
            pltpu.VMEM((4, FACES, COLS, C), bf16),
            pltpu.VMEM((2, 2, 4 * SIDES * STACK, groups * BLOCKS * 16), bf16),
            pltpu.VMEM((2, FACES * STACK, C), f32),
            pltpu.VMEM((4, FACES * COLS, C), f32),
            pltpu.SemaphoreType.DMA((len(operands),)),
            pltpu.SemaphoreType.DMA((15,)),
            pltpu.SemaphoreType.DMA((15,)),
        ],
        compiler_params=pltpu.CompilerParams(
            collective_id=0, has_side_effects=True, vmem_limit_bytes=32 * 2**20
        ),
    )(*[pltpu.with_memory_space_constraint(x, pltpu.HBM) for x in operands])


def solution(mesh):
    return jax.shard_map(
        functools.partial(on_device, mesh.shape["face"], mesh.shape["tile"]),
        mesh=mesh,
        in_specs=(P("face", "tile", None, None),) * 3 + (P(),) * 7,
        out_specs=P("face", "tile", None, None),
        check_vma=False,
    )
```
